256 devices in a mesh: dp: 4 (over y), row: 4 (over z_hi, core), col: 16 (over x, z_lo).
Axes of the slice: x: 4, y: 4, z: 8 (z_hi: 2, z_lo: 4; z = z_hi * 4 + z_lo), core: 2. Of those that a mesh axis runs over, the one named last changes fastest.
Arguments:
- features: bfloat16 [8, 256, 6144], P('dp', 'row', 'col'), may hold values from -6 to 6
- ln_gain: float32 [6144], P('col'), may hold values from 0.5 to 10, as said below
- w_qkv: bfloat16 [6144, 3, 3072], P('col', None, 'row'), may hold values from -0.078125 to 0.078125
- qk_gain: float32 [2, 128], replicated, may hold values from 0.25 to 1.75
- w_up: bfloat16 [6144, 12288], P('col', 'row'), may hold values from -1 to 1
- w_out: bfloat16 [3072, 6144], P('row', 'col'), may hold values from -0.109375 to 0.109375
- w_down: bfloat16 [12288, 6144], P('row', 'col'), may hold values from -0.0546875 to 0.0546875
- cotangent: bfloat16 [8, 256, 6144], P('dp', 'row', 'col'), may hold values from -6 to 6
Outputs:
- output: bfloat16 [8, 256, 6144], P('dp', 'row', 'col')
- input_grad: bfloat16 [8, 256, 6144], P('dp', 'row', 'col')
- ln_grad: float32 [6144], P('col')
- gain_grads: float32 [2, 128], replicated
- qkv_grad: float32 [6144, 3, 3072], P('col', None, ('row', 'dp'))
- up_grad: float32 [6144, 12288], P('col', ('row', 'dp'))
- out_grad: float32 [3072, 6144], P(('row', 'dp'), 'col')
- down_grad: float32 [12288, 6144], P(('row', 'dp'), 'col')
The draws below stay inside these ranges and needn't reach their ends.
Inputs may be any that keep to these rules, and one draw needn't show every extreme that they name: `ln_gain`: positive gains.
All inputs are finite; a program needn't handle non-finite values.
Results may differ from the reference program's by a relative error of at most 0.034.
Values may be sent and summed in bfloat16 or wider, within the bound.
A program may use at most 128 MiB of HBM per device.

```python
import jax
import jax.numpy as jnp
from jax import lax

D = 6144
HEAD_DIM = 128
HEADS = 24
FF = 12288
PATCHES = 256
HD = 3072
IMAGES = 8


def draw_ln_gain(key, part):
    key = jax.random.fold_in(key, 11)
    position = jnp.arange(D, dtype=jnp.float32) / (D - 1)
    rise = jnp.exp(position * jnp.log(4.0))
    rough = jax.random.uniform(key, (D,), jnp.float32, 0.7, 1.3)
    return (rise * rough).astype(jnp.float32)


def draw_w_up(key, part):
    key = jax.random.fold_in(key, 23)
    first_key, second_key = jax.random.split(key)
    scale = D ** (-0.5)
    own = jnp.clip(jax.random.normal(first_key, (D, FF), jnp.float32), -6.0, 6.0) * scale
    column = jnp.clip(jax.random.normal(second_key, (FF,), jnp.float32), -6.0, 6.0) * scale
    return (own + column[None, :]).astype(jnp.bfloat16)


def block_scale(key, dims, cuts, low, largest):
    factor_of = 1.0
    for dim, parts in cuts:
        heights = jax.random.uniform(jax.random.fold_in(jax.random.fold_in(key, 6), dim), (parts,), jnp.float32, low / len(cuts), largest / len(cuts))
        factor_of = factor_of * jnp.repeat(jnp.exp(heights), dims[dim] // parts).reshape((-1,) + (1,) * (len(dims) - 1 - dim))
    return factor_of


def noise(rng, shape, scale, reach, pieces=(), kind=jnp.bfloat16):
    loudness = block_scale(rng, shape, pieces, -0.22, 0.18) if pieces else 1.0
    values = jax.random.normal(rng, shape, jnp.float32) * scale * loudness
    return jnp.minimum(jnp.maximum(values, -reach), reach).astype(kind)


def setup_inputs(seed: int = 0) -> dict:
    arg_keys = jax.random.split(jax.random.key(seed), 9)
    return {
        "features": noise(arg_keys[0], (IMAGES, PATCHES, D), 1.0, 6.0, ((0, 4), (1, 4), (2, 16))),
        "ln_gain": draw_ln_gain(jax.random.fold_in(arg_keys[8], 71), 0),
        "w_qkv": noise(arg_keys[2], (D, 3, HD), D ** -0.5, 0.078125, ((0, 16), (2, 4))),
        "qk_gain": jnp.clip(1.0 + 0.15 * jax.random.normal(arg_keys[3], (2, HEAD_DIM), jnp.float32), 0.25, 1.75),
        "w_up": draw_w_up(jax.random.fold_in(arg_keys[8], 71), 0),
        "w_out": noise(arg_keys[5], (HD, D), HD ** -0.5, 0.109375, ((0, 4), (1, 16))),
        "w_down": noise(arg_keys[6], (FF, D), FF ** -0.5, 0.0546875, ((0, 4), (1, 16))),
        "cotangent": noise(arg_keys[7], (IMAGES, PATCHES, D), 1.0, 6.0, ((0, 4), (1, 4), (2, 16))),
    }


EPS = 1e-06
SQRT_HALF = 0.7071067811865476
INV_ROOT = 0.3989422804014327

def gelu_value(values):
    return 0.5 * values * (1.0 + jax.scipy.special.erf(values * SQRT_HALF))

def gelu_slope(values):
    return 0.5 * (1.0 + jax.scipy.special.erf(values * SQRT_HALF)) + values * jnp.exp(-0.5 * values * values) * INV_ROOT

def normalize(values):
    average = lax.optimization_barrier(jnp.mean(values, -1, keepdims=True))
    spread = lax.optimization_barrier(jnp.mean(values * values, -1, keepdims=True)) - average * average
    factor = lax.rsqrt(spread + EPS)
    return ((values - average) * factor, factor)

def norm_back(grad_normed, normed, factor, gain):
    scaled = grad_normed * gain
    centre = lax.optimization_barrier(jnp.mean(scaled, -1, keepdims=True))
    along = lax.optimization_barrier(jnp.mean(scaled * normed, -1, keepdims=True))
    return factor * (scaled - centre - normed * along)

def rounded(values):
    return lax.optimization_barrier(values.astype(jnp.bfloat16)).astype(jnp.float32)

def reference(features, ln_gain, w_qkv, qk_gain, w_up, w_out, w_down, cotangent):
    token_count = IMAGES * PATCHES
    inputs_wide = features.astype(jnp.float32)
    normed, factor = normalize(inputs_wide)
    scaled_in = (normed * ln_gain).astype(jnp.bfloat16)
    flat_in = scaled_in.reshape(token_count, D)
    qkv_flat = w_qkv.reshape(D, 3 * HD)
    projected = jnp.dot(flat_in, qkv_flat, preferred_element_type=jnp.float32).reshape(IMAGES, PATCHES, 3, HEADS, HEAD_DIM)
    hidden_pre = jnp.dot(flat_in, w_up, preferred_element_type=jnp.float32)
    query_hat, query_factor = normalize(projected[:, :, 0])
    key_hat, key_factor = normalize(projected[:, :, 1])
    query_wide = rounded(query_hat * qk_gain[0])
    key_wide = rounded(key_hat * qk_gain[1])
    value_wide = rounded(projected[:, :, 2])
    scale = HEAD_DIM ** (-0.5)
    scores = jnp.einsum('bqhd,bkhd->bhqk', query_wide, key_wide) * scale
    expo = jnp.exp(scores)
    weights = expo / lax.optimization_barrier(jnp.sum(expo, -1, keepdims=True))
    weights_wide = rounded(weights)
    attended = jnp.einsum('bhqk,bkhd->bqhd', weights_wide, value_wide).astype(jnp.bfloat16).reshape(token_count, HD)
    hidden = gelu_value(hidden_pre).astype(jnp.bfloat16)
    mixed = jnp.dot(attended, w_out, preferred_element_type=jnp.float32) + jnp.dot(hidden, w_down, preferred_element_type=jnp.float32)
    output = (inputs_wide + mixed.reshape(IMAGES, PATCHES, D)).astype(jnp.bfloat16)
    grad_flat = cotangent.reshape(token_count, D)
    attn_grad = jnp.dot(grad_flat, w_out.T, preferred_element_type=jnp.float32).astype(jnp.bfloat16)
    hidden_grad = jnp.dot(grad_flat, w_down.T, preferred_element_type=jnp.float32)
    pre_grad = (hidden_grad * gelu_slope(hidden_pre)).astype(jnp.bfloat16)
    attn_heads = attn_grad.reshape(IMAGES, PATCHES, HEADS, HEAD_DIM).astype(jnp.float32)
    weight_grad = jnp.einsum('bqhd,bkhd->bhqk', attn_heads, value_wide)
    score_grad = rounded(weights * (weight_grad - lax.optimization_barrier(jnp.sum(weights * weight_grad, -1, keepdims=True))))
    query_grad = jnp.einsum('bhqk,bkhd->bqhd', score_grad, key_wide) * scale
    key_grad = jnp.einsum('bhqk,bqhd->bkhd', score_grad, query_wide) * scale
    value_grad = jnp.einsum('bhqk,bqhd->bkhd', weights_wide, attn_heads)
    gain_grads = jnp.stack([lax.optimization_barrier(jnp.sum(query_grad * query_hat, (0, 1, 2))), lax.optimization_barrier(jnp.sum(key_grad * key_hat, (0, 1, 2)))])
    query_back = norm_back(query_grad, query_hat, query_factor, qk_gain[0])
    key_back = norm_back(key_grad, key_hat, key_factor, qk_gain[1])
    proj_grad = jnp.stack([query_back, key_back, value_grad], 2).astype(jnp.bfloat16).reshape(token_count, 3 * HD)
    norm_grad = jnp.dot(proj_grad, qkv_flat.T, preferred_element_type=jnp.float32) + jnp.dot(pre_grad, w_up.T, preferred_element_type=jnp.float32)
    norm_grad = norm_grad.reshape(IMAGES, PATCHES, D)
    input_grad = (cotangent.astype(jnp.float32) + norm_back(norm_grad, normed, factor, ln_gain)).astype(jnp.bfloat16)
    ln_grad = lax.optimization_barrier(jnp.sum(norm_grad * normed, (0, 1)))
    qkv_grad = jnp.dot(flat_in.T, proj_grad, preferred_element_type=jnp.float32).reshape(D, 3, HD)
    up_grad = jnp.dot(flat_in.T, pre_grad, preferred_element_type=jnp.float32)
    out_grad = jnp.dot(attended.T, grad_flat, preferred_element_type=jnp.float32)
    down_grad = jnp.dot(hidden.T, grad_flat, preferred_element_type=jnp.float32)
    return (output, input_grad, ln_grad, gain_grads, qkv_grad, up_grad, out_grad, down_grad)
```

```python
import functools

import jax
import jax.numpy as jnp
from jax import lax
from jax.experimental import pallas as pl
from jax.experimental.pallas import tpu as pltpu
from jax.sharding import PartitionSpec as P

EPS = 1e-06
SQRT_HALF = 0.7071067811865476
INV_ROOT = 0.3989422804014327
HEAD = 128
SIDE = 4
PIECES = 9
MESH = pl.DeviceIdType.MESH
F32 = jnp.float32
BF16 = jnp.bfloat16


def gelu_both(values):
    cdf = 0.5 * (1.0 + lax.erf(values * SQRT_HALF))
    slope = cdf + values * jnp.exp(-0.5 * values * values) * INV_ROOT
    return values * cdf, slope


def normalize(values):
    average = jnp.mean(values, -1, keepdims=True)
    spread = jnp.mean(values * values, -1, keepdims=True) - average * average
    factor = lax.rsqrt(spread + EPS)
    return ((values - average) * factor, factor)


def norm_back(grad_normed, normed, factor, gain):
    scaled = grad_normed * gain
    centre = jnp.mean(scaled, -1, keepdims=True)
    along = jnp.mean(scaled * normed, -1, keepdims=True)
    return factor * (scaled - centre - normed * along)


def dot(a, b):
    return lax.dot_general(a, b, (((1,), (0,)), ((), ())), preferred_element_type=F32)


def dot_nt(a, b):
    return lax.dot_general(a, b, (((1,), (1,)), ((), ())), preferred_element_type=F32)


def exact_nt(a, b):
    return lax.dot_general(
        a,
        b,
        (((1,), (1,)), ((), ())),
        precision=lax.Precision.HIGHEST,
        preferred_element_type=F32,
    )


def greet(peers):
    barrier = pltpu.get_barrier_semaphore()
    for peer in peers:
        pl.semaphore_signal(barrier, inc=1, device_id=peer, device_id_type=MESH)
    pl.semaphore_wait(barrier, len(peers))


def remote(src, dst, send, recv, peer):
    return pltpu.make_async_remote_copy(
        src_ref=src,
        dst_ref=dst,
        send_sem=send,
        recv_sem=recv,
        device_id=peer,
        device_id_type=MESH,
    )


def pre_kernel(
    rows, cols, x_ref, gain_ref, cot_ref,
    xin_ref, call_ref, avg_ref, factor_ref,
    mine, stats, stat_send, stat_recv, row_send, row_recv,
):
    dp, row, col = lax.axis_index("dp"), lax.axis_index("row"), lax.axis_index("col")
    images, patches, width = x_ref.shape
    tokens = images * patches

    def col_peer(k):
        return (dp, row, lax.rem(col + k, cols))

    def row_peer(k):
        return (dp, lax.rem(row + k, rows), col)

    greet([col_peer(k) for k in range(1, cols)] + [row_peer(k) for k in range(1, rows)])
    here = pl.ds(pl.multiple_of(row * patches, patches), patches)
    sends = []
    for k in range(1, rows):
        copy = remote(
            cot_ref, call_ref.at[:, here, :], row_send.at[0, k - 1], row_recv.at[0, k - 1], row_peer(k)
        )
        copy.start()
        sends.append(copy)
    x = x_ref[...].astype(F32).reshape(tokens, width)
    ones = jnp.ones((8, width), F32)
    first = exact_nt(ones, x)
    second = exact_nt(ones, x * x)
    which = lax.broadcasted_iota(jnp.int32, (8, tokens), 0)
    local = jnp.where(which == 0, first, second)
    mine[...] = local
    stat_copies = []
    for k in range(1, cols):
        copy = remote(mine, stats.at[k - 1], stat_send.at[k - 1], stat_recv.at[k - 1], col_peer(k))
        copy.start()
        stat_copies.append(copy)
    call_ref[:, here, :] = cot_ref[...]
    total = local
    for k in range(1, cols):
        stat_copies[k - 1].wait_recv()
        total = total + stats[k - 1]
    total = total * (1.0 / (width * cols))
    average = total[0:1]
    factor = lax.rsqrt(total[1:2] - average * average + EPS)
    both = jnp.where(which == 0, average, factor)
    eye = (
        lax.broadcasted_iota(jnp.int32, (tokens, tokens), 0)
        == lax.broadcasted_iota(jnp.int32, (tokens, tokens), 1)
    ).astype(F32)
    turned = exact_nt(eye, both)
    avg_col, factor_col = turned[:, 0:1], turned[:, 1:2]
    normed = (x - avg_col) * factor_col
    xin_ref[:, here, :] = (normed * gain_ref[...]).astype(BF16).reshape(images, patches, width)
    for k in range(1, rows):
        copy = remote(
            xin_ref.at[:, here, :],
            xin_ref.at[:, here, :],
            row_send.at[1, k - 1],
            row_recv.at[1, k - 1],
            row_peer(k),
        )
        copy.start()
        sends.append(copy)
    avg_ref[...] = jnp.broadcast_to(avg_col, avg_ref.shape)
    factor_ref[...] = jnp.broadcast_to(factor_col, factor_ref.shape)
    for copy in sends:
        copy.wait_recv()
    for copy in sends + stat_copies:
        copy.wait_send()


def vmem(count):
    return [pl.BlockSpec(memory_space=pltpu.VMEM)] * count


def gather_inputs(features, ln_gain, cotangent):
    rows, cols = lax.axis_size("row"), lax.axis_size("col")
    images, patches, width = features.shape
    tokens = images * patches
    whole = jax.ShapeDtypeStruct((images, patches * rows, width), BF16)
    column = jax.ShapeDtypeStruct((tokens, HEAD), F32)
    return pl.pallas_call(
        functools.partial(pre_kernel, rows, cols),
        out_shape=(whole, whole, column, column),
        in_specs=vmem(3),
        out_specs=tuple(vmem(4)),
        scratch_shapes=[
            pltpu.VMEM((8, tokens), F32),
            pltpu.VMEM((cols - 1, 8, tokens), F32),
            pltpu.SemaphoreType.DMA((cols - 1,)),
            pltpu.SemaphoreType.DMA((cols - 1,)),
            pltpu.SemaphoreType.DMA((2, max(rows - 1, 1))),
            pltpu.SemaphoreType.DMA((2, max(rows - 1, 1))),
        ],
        compiler_params=pltpu.CompilerParams(collective_id=0, has_side_effects=True),
        name="gather_inputs",
    )(features, ln_gain.reshape(1, width), cotangent)


def owner_z(piece):
    return piece if piece < 3 else piece - 3 if piece < 6 else 3


def owner_slot(piece):
    return 0 if piece < 3 else 1 if piece < 6 else piece - 6


def core_kernel(
    x_ref, c_ref, wq_ref, wup_ref, wout_ref, wdown_ref, gain_ref,
    g_ref, gains_ref,
    opp, right_send, left_send, right_acc, left_acc, own,
    half_left, half_right, full_left, full_right, z_send, z_recv,
    s_opp, r_half, s_side, r_full, s_z, r_z, s_own, r_own, s_fwd, r_fwd, s_zag, r_zag,
):
    dp, row, col = lax.axis_index("dp"), lax.axis_index("row"), lax.axis_index("col")
    xi, zi = col // SIDE, lax.rem(col, SIDE)
    xr, xl, xo = lax.rem(xi + 1, SIDE), lax.rem(xi + 3, SIDE), lax.rem(xi + 2, SIDE)
    right, left = (dp, row, xr * SIDE + zi), (dp, row, xl * SIDE + zi)

    def z_peer(k):
        return (dp, row, xi * SIDE + lax.rem(zi + k, SIDE))

    greet([right, left] + [z_peer(k) for k in range(1, SIDE)])

    def partial_block(block, emit):
        image, run = block // 2, lax.rem(block, 2)
        triple = pl.ds(pl.multiple_of(run * 3 * HEAD, 3 * HEAD), 3 * HEAD)
        for part in range(3):
            start = part * 6 * HEAD + run * 3 * HEAD
            values = dot(x_ref[image], wq_ref[:, pl.ds(pl.multiple_of(start, HEAD), 3 * HEAD)])
            for z in range(3):
                emit(z, part, values[:, z * HEAD : (z + 1) * HEAD])
        values = dot_nt(c_ref[image], wout_ref[triple, :])
        for z in range(3):
            emit(z, 3, values[:, z * HEAD : (z + 1) * HEAD])
        hidden = pl.ds(pl.multiple_of(block * 6 * HEAD, 6 * HEAD), 6 * HEAD)
        for im in range(2):
            values = dot(x_ref[im], wup_ref[:, hidden])
            for j in range(6):
                emit(3 + j, im, values[:, j * HEAD : (j + 1) * HEAD])
            values = dot_nt(c_ref[im], wdown_ref[hidden, :])
            for j in range(6):
                emit(3 + j, 2 + im, values[:, j * HEAD : (j + 1) * HEAD])

    low, high = pl.ds(0, 2), pl.ds(2, 2)

    def opp_right(p):
        return remote(opp.at[p, low], half_left.at[p], s_opp.at[0, p], r_half.at[0, p], right)

    def opp_left(p):
        return remote(opp.at[p, high], half_right.at[p], s_opp.at[1, p], r_half.at[1, p], left)

    def side_right(p, half):
        part = pl.ds(2 * half, 2)
        return remote(
            right_send.at[p, part],
            full_left.at[p, part],
            s_side.at[0, half, p],
            r_full.at[0, half, p],
            right,
        )

    def side_left(p, half):
        part = pl.ds(2 * half, 2)
        return remote(
            left_send.at[p, part],
            full_right.at[p, part],
            s_side.at[1, half, p],
            r_full.at[1, half, p],
            left,
        )

    def emit_opp(p, part, values):
        opp[p, part] = values.astype(BF16)

    partial_block(xo, emit_opp)
    for p in range(PIECES):
        opp_right(p).start()
        opp_left(p).start()

    def emit_right(p, part, values):
        if part >= 2:
            right_send[p, part] = values.astype(BF16)
        else:
            right_acc[p, part] = values

    partial_block(xr, emit_right)
    for p in range(PIECES):
        side_right(p, 1).start()

    def emit_left(p, part, values):
        if part < 2:
            left_send[p, part] = values.astype(BF16)
        else:
            left_acc[p, part - 2] = values

    partial_block(xl, emit_left)
    for p in range(PIECES):
        side_left(p, 0).start()

    def emit_own(p, part, values):
        own[p, part] = values

    partial_block(xi, emit_own)

    def pass_on(p, carry):
        opp_right(p).wait_recv()
        right_send[p, low] = (right_acc[p] + half_left[p].astype(F32)).astype(BF16)
        side_right(p, 0).start()
        opp_left(p).wait_recv()
        left_send[p, high] = (left_acc[p] + half_right[p].astype(F32)).astype(BF16)
        side_left(p, 1).start()
        return carry

    lax.fori_loop(0, PIECES, pass_on, 0)

    def z_copy(p, k):
        return remote(
            z_send.at[p],
            z_recv.at[k - 1, owner_slot(p)],
            s_z.at[p],
            r_z.at[k - 1, owner_slot(p)],
            z_peer(k),
        )

    for p in range(PIECES):
        for half in range(2):
            side_right(p, half).wait_recv()
            side_left(p, half).wait_recv()
        own[p] = own[p] + full_left[p].astype(F32) + full_right[p].astype(F32)
        for k in range(1, SIDE):

            @pl.when(lax.rem(zi + k, SIDE) == owner_z(p))
            def _():
                z_send[p] = own[p].astype(BF16)
                z_copy(p, k).start()

    def arrived(p, slot):
        total = own[p]
        for k in range(1, SIDE):
            remote(
                z_send.at[0], z_recv.at[k - 1, slot], s_z.at[0], r_z.at[k - 1, slot], z_peer(k)
            ).wait_recv()
            total = total + z_recv[k - 1, slot].astype(F32)
        return total

    def own_ag(p, way):
        peer = right if way == 0 else left
        return remote(g_ref.at[xi, p], g_ref.at[xi, p], s_own.at[way, p], r_own.at[way, p], peer)

    def z_ag(p, k):
        return remote(g_ref.at[xi, p], g_ref.at[xi, p], s_zag.at[k - 1, p], r_zag.at[p], z_peer(k))

    def launch(p):
        for way in range(2):
            own_ag(p, way).start()
        for k in range(1, SIDE):
            z_ag(p, k).start()

    def hidden_units(p, slot):
        total = arrived(p, slot)
        for im in range(2):
            value, slope = gelu_both(total[im])
            g_ref[xi, p, im] = value.astype(BF16)
            g_ref[xi, p, 2 + im] = (total[2 + im] * slope).astype(BF16)
        launch(p)

    scale = HEAD ** (-0.5)

    def attention(p):
        total = arrived(p, 0)
        query_hat, query_factor = normalize(total[0])
        key_hat, key_factor = normalize(total[1])
        query_gain, key_gain = gain_ref[0:1, :], gain_ref[1:2, :]
        query = (query_hat * query_gain).astype(BF16)
        key = (key_hat * key_gain).astype(BF16)
        value = total[2].astype(BF16)
        grad = total[3].astype(BF16)
        expo = jnp.exp(dot_nt(query, key) * scale)
        weights = expo / jnp.sum(expo, -1, keepdims=True)
        weights_half = weights.astype(BF16)
        g_ref[xi, p, 0] = dot(weights_half, value).astype(BF16)
        weight_grad = dot_nt(grad, value)
        score_grad = weights * (weight_grad - jnp.sum(weights * weight_grad, -1, keepdims=True))
        score_grad = score_grad.astype(BF16)
        query_grad = dot(score_grad, key) * scale
        key_grad = dot(score_grad.T, query) * scale
        value_grad = dot(weights_half.T, grad)
        gains_ref[0:1, :] = jnp.sum(query_grad * query_hat, 0, keepdims=True)
        gains_ref[1:2, :] = jnp.sum(key_grad * key_hat, 0, keepdims=True)
        g_ref[xi, p, 1] = norm_back(query_grad, query_hat, query_factor, query_gain).astype(BF16)
        g_ref[xi, p, 2] = norm_back(key_grad, key_hat, key_factor, key_gain).astype(BF16)
        g_ref[xi, p, 3] = value_grad.astype(BF16)
        launch(p)

    gains_ref[...] = jnp.zeros_like(gains_ref)

    @pl.when(zi < 3)
    def _():
        hidden_units(zi + 3, 1)
        attention(zi)

    @pl.when(zi == 3)
    def _():
        for j in range(3):
            hidden_units(6 + j, j)

    def fwd_copy(p, way):
        block = xl if way == 0 else xr
        part = low if way == 0 else high
        there = right if way == 0 else left
        return remote(
            g_ref.at[block, p, part],
            g_ref.at[block, p, part],
            s_fwd.at[way, p],
            r_fwd.at[way, p],
            there,
        )

    def each_piece(step, body):
        z = lax.rem(zi + step, SIDE)

        @pl.when(z < 3)
        def _():
            body(z + 3)
            body(z)

        @pl.when(z == 3)
        def _():
            for j in range(3):
                body(6 + j)

    def spread(p):
        z_ag(p, 1).wait_recv()
        for way in range(2):
            own_ag(p, way).start()

    def relay(p):
        for way in range(2):
            own_ag(p, way).wait_recv()
            fwd_copy(p, way).start()

    each_piece(1, spread)
    each_piece(0, relay)
    each_piece(2, spread)
    each_piece(1, relay)
    each_piece(3, spread)
    each_piece(2, relay)
    each_piece(3, relay)

    def finish(p, carry):
        opp_right(p).wait_send()
        opp_left(p).wait_send()
        for half in range(2):
            side_right(p, half).wait_send()
            side_left(p, half).wait_send()
        for way in range(2):
            own_ag(p, way).wait_send()
            fwd_copy(p, way).wait()
        return carry

    lax.fori_loop(0, PIECES, finish, 0)
    for p in range(PIECES):

        @pl.when(zi != owner_z(p))
        def _():
            z_copy(p, 1).wait_send()

        @pl.when(zi == owner_z(p))
        def _():
            for k in range(1, SIDE):
                z_ag(p, k).wait_send()


def exchange(x_all, c_all, w_qkv, w_up, w_out, w_down, qk_gain):
    images, patches, width = x_all.shape
    piece = (4, patches, HEAD)
    half = (2, patches, HEAD)
    dma = pltpu.SemaphoreType.DMA
    return pl.pallas_call(
        core_kernel,
        out_shape=(
            jax.ShapeDtypeStruct((SIDE, PIECES) + piece, BF16),
            jax.ShapeDtypeStruct((8, HEAD), F32),
        ),
        in_specs=vmem(7),
        out_specs=tuple(vmem(2)),
        scratch_shapes=[
            pltpu.VMEM((PIECES,) + piece, BF16),
            pltpu.VMEM((PIECES,) + piece, BF16),
            pltpu.VMEM((PIECES,) + piece, BF16),
            pltpu.VMEM((PIECES,) + half, F32),
            pltpu.VMEM((PIECES,) + half, F32),
            pltpu.VMEM((PIECES,) + piece, F32),
            pltpu.VMEM((PIECES,) + half, BF16),
            pltpu.VMEM((PIECES,) + half, BF16),
            pltpu.VMEM((PIECES,) + piece, BF16),
            pltpu.VMEM((PIECES,) + piece, BF16),
            pltpu.VMEM((PIECES,) + piece, BF16),
            pltpu.VMEM((SIDE - 1, 3) + piece, BF16),
            dma((2, PIECES)),
            dma((2, PIECES)),
            dma((2, 2, PIECES)),
            dma((2, 2, PIECES)),
            dma((PIECES,)),
            dma((SIDE - 1, 3)),
            dma((2, PIECES)),
            dma((2, PIECES)),
            dma((2, PIECES)),
            dma((2, PIECES)),
            dma((SIDE - 1, PIECES)),
            dma((PIECES,)),
        ],
        compiler_params=pltpu.CompilerParams(
            collective_id=1, has_side_effects=True, vmem_limit_bytes=60 * 1024 * 1024
        ),
        name="exchange",
    )(x_all, c_all, w_qkv, w_up, w_out, w_down, qk_gain)


def on_device(features, ln_gain, w_qkv, qk_gain, w_up, w_out, w_down, cotangent):
    images, patches, width = features.shape
    head_cols = w_qkv.shape[2]
    total_width = width * lax.axis_size("col")
    x_all, c_all, average, factor = gather_inputs(features, ln_gain, cotangent)
    qkv_flat = w_qkv.reshape(width, 3 * head_cols)
    pieces, gains = exchange(x_all, c_all, qkv_flat, w_up, w_out, w_down, qk_gain)
    every = pieces.shape[3]
    inputs_wide = features.astype(F32)
    average = average[:, :1].reshape(images, patches, 1)
    factor = factor[:, :1].reshape(images, patches, 1)
    normed = (inputs_wide - average) * factor

    def heads_of(part):
        values = pieces[:, 0:3, part].reshape(2, 2, 3, every, HEAD)
        return jnp.transpose(values, (0, 3, 1, 2, 4)).reshape(images, every, head_cols)

    def units_of(first):
        values = pieces[:, 3:9, first : first + 2]
        return jnp.transpose(values, (2, 3, 0, 1, 4)).reshape(images, every, 6 * SIDE * HEAD)

    attended_all = heads_of(0)
    proj_all = jnp.concatenate([heads_of(1), heads_of(2), heads_of(3)], -1)
    hidden_all, pre_all = units_of(0), units_of(2)

    def row_sum(first, second):
        return lax.psum_scatter(
            (first + second).astype(BF16), "row", scatter_dimension=1, tiled=True
        ).astype(F32)

    def ein(spec, a, b):
        return jnp.einsum(spec, a, b, preferred_element_type=F32)

    mixed = row_sum(
        ein("bpx,xd->bpd", attended_all, w_out), ein("bpf,fd->bpd", hidden_all, w_down)
    )
    output = (inputs_wide + mixed).astype(BF16)
    norm_grad = row_sum(
        ein("bpx,dx->bpd", proj_all, qkv_flat), ein("bpf,df->bpd", pre_all, w_up)
    )
    scaled_grad = norm_grad * ln_gain
    centre_sum, along_sum = lax.psum(
        (jnp.sum(scaled_grad, -1), jnp.sum(scaled_grad * normed, -1)), "col"
    )
    centre = (centre_sum / total_width)[..., None]
    along = (along_sum / total_width)[..., None]
    input_grad = (
        cotangent.astype(F32) + factor * (scaled_grad - centre - normed * along)
    ).astype(BF16)
    ln_grad = lax.psum(jnp.sum(norm_grad * normed, (0, 1)), ("dp", "row"))
    gain_grads = lax.psum(gains[:2], ("dp", "row", "col"))

    def dp_sum(values, dim):
        return lax.psum_scatter(
            values.astype(BF16), "dp", scatter_dimension=dim, tiled=True
        ).astype(F32)

    qkv_grad = dp_sum(ein("bpd,bpx->dx", x_all, proj_all).reshape(width, 3, head_cols), 2)
    up_grad = dp_sum(ein("bpd,bpf->df", x_all, pre_all), 1)
    out_grad = dp_sum(ein("bpx,bpd->xd", attended_all, c_all), 0)
    down_grad = dp_sum(ein("bpf,bpd->fd", hidden_all, c_all), 0)
    return (output, input_grad, ln_grad, gain_grads, qkv_grad, up_grad, out_grad, down_grad)


def solution(mesh):
    in_specs = (
        P("dp", "row", "col"),
        P("col"),
        P("col", None, "row"),
        P(),
        P("col", "row"),
        P("row", "col"),
        P("row", "col"),
        P("dp", "row", "col"),
    )
    out_specs = (
        P("dp", "row", "col"),
        P("dp", "row", "col"),
        P("col"),
        P(),
        P("col", None, ("row", "dp")),
        P("col", ("row", "dp")),
        P(("row", "dp"), "col"),
        P(("row", "dp"), "col"),
    )
    return jax.shard_map(
        on_device, mesh=mesh, in_specs=in_specs, out_specs=out_specs, check_vma=False
    )
```

```python
import functools

import jax
import jax.numpy as jnp
from jax import lax
from jax.experimental import pallas as pl
from jax.experimental.pallas import tpu as pltpu
from jax.sharding import PartitionSpec as P

EPS = 1e-06
SQRT_HALF = 0.7071067811865476
INV_ROOT = 0.3989422804014327
HEAD = 128
SIDE = 4
PIECES = 9
MESH = pl.DeviceIdType.MESH
VMEM_BYTES = 62 * 1024 * 1024
F32 = jnp.float32
BF16 = jnp.bfloat16


def gelu_both(values):
    cdf = 0.5 * (1.0 + lax.erf(values * SQRT_HALF))
    slope = cdf + values * jnp.exp(-0.5 * values * values) * INV_ROOT
    return values * cdf, slope


def normalize(values):
    average = jnp.mean(values, -1, keepdims=True)
    spread = jnp.mean(values * values, -1, keepdims=True) - average * average
    factor = lax.rsqrt(spread + EPS)
    return ((values - average) * factor, factor)


def norm_back(grad_normed, normed, factor, gain):
    scaled = grad_normed * gain
    centre = jnp.mean(scaled, -1, keepdims=True)
    along = jnp.mean(scaled * normed, -1, keepdims=True)
    return factor * (scaled - centre - normed * along)


def dot(a, b):
    return lax.dot_general(a, b, (((1,), (0,)), ((), ())), preferred_element_type=F32)


def dot_nt(a, b):
    return lax.dot_general(a, b, (((1,), (1,)), ((), ())), preferred_element_type=F32)


def exact_nt(a, b):
    return lax.dot_general(
        a,
        b,
        (((1,), (1,)), ((), ())),
        precision=lax.Precision.HIGHEST,
        preferred_element_type=F32,
    )


def greet(peers):
    barrier = pltpu.get_barrier_semaphore()
    for peer in peers:
        pl.semaphore_signal(barrier, inc=1, device_id=peer, device_id_type=MESH)
    pl.semaphore_wait(barrier, len(peers))


def remote(src, dst, send, recv, peer):
    return pltpu.make_async_remote_copy(
        src_ref=src,
        dst_ref=dst,
        send_sem=send,
        recv_sem=recv,
        device_id=peer,
        device_id_type=MESH,
    )


def pre_kernel(
    rows, cols, x_ref, gain_ref, cot_ref,
    xin_ref, call_ref, avg_ref, factor_ref,
    mine, stats, stat_send, stat_recv, row_send, row_recv,
):
    dp, row, col = lax.axis_index("dp"), lax.axis_index("row"), lax.axis_index("col")
    images, patches, width = x_ref.shape
    tokens = images * patches

    def col_peer(k):
        return (dp, row, lax.rem(col + k, cols))

    def row_peer(k):
        return (dp, lax.rem(row + k, rows), col)

    greet([col_peer(k) for k in range(1, cols)] + [row_peer(k) for k in range(1, rows)])
    here = pl.ds(pl.multiple_of(row * patches, patches), patches)
    sends = []
    for k in range(1, rows):
        copy = remote(
            cot_ref, call_ref.at[:, here, :], row_send.at[0, k - 1], row_recv.at[0, k - 1], row_peer(k)
        )
        copy.start()
        sends.append(copy)
    x = x_ref[...].astype(F32).reshape(tokens, width)
    ones = jnp.ones((8, width), F32)
    first = exact_nt(ones, x)
    second = exact_nt(ones, x * x)
    which = lax.broadcasted_iota(jnp.int32, (8, tokens), 0)
    local = jnp.where(which == 0, first, second)
    mine[...] = local
    stat_copies = []
    for k in range(1, cols):
        copy = remote(mine, stats.at[k - 1], stat_send.at[k - 1], stat_recv.at[k - 1], col_peer(k))
        copy.start()
        stat_copies.append(copy)
    call_ref[:, here, :] = cot_ref[...]
    total = local
    for k in range(1, cols):
        stat_copies[k - 1].wait_recv()
        total = total + stats[k - 1]
    total = total * (1.0 / (width * cols))
    average = total[0:1]
    factor = lax.rsqrt(total[1:2] - average * average + EPS)
    both = jnp.where(which == 0, average, factor)
    eye = (
        lax.broadcasted_iota(jnp.int32, (tokens, tokens), 0)
        == lax.broadcasted_iota(jnp.int32, (tokens, tokens), 1)
    ).astype(F32)
    turned = exact_nt(eye, both)
    avg_col, factor_col = turned[:, 0:1], turned[:, 1:2]
    normed = (x - avg_col) * factor_col
    xin_ref[:, here, :] = (normed * gain_ref[...]).astype(BF16).reshape(images, patches, width)
    for k in range(1, rows):
        copy = remote(
            xin_ref.at[:, here, :],
            xin_ref.at[:, here, :],
            row_send.at[1, k - 1],
            row_recv.at[1, k - 1],
            row_peer(k),
        )
        copy.start()
        sends.append(copy)
    avg_ref[...] = jnp.broadcast_to(avg_col, avg_ref.shape)
    factor_ref[...] = jnp.broadcast_to(factor_col, factor_ref.shape)
    for copy in sends:
        copy.wait_recv()
    for copy in sends + stat_copies:
        copy.wait_send()


def vmem(count):
    return [pl.BlockSpec(memory_space=pltpu.VMEM)] * count


def gather_inputs(features, ln_gain, cotangent):
    rows, cols = lax.axis_size("row"), lax.axis_size("col")
    images, patches, width = features.shape
    tokens = images * patches
    whole = jax.ShapeDtypeStruct((images, patches * rows, width), BF16)
    column = jax.ShapeDtypeStruct((tokens, HEAD), F32)
    return pl.pallas_call(
        functools.partial(pre_kernel, rows, cols),
        out_shape=(whole, whole, column, column),
        in_specs=vmem(3),
        out_specs=tuple(vmem(4)),
        scratch_shapes=[
            pltpu.VMEM((8, tokens), F32),
            pltpu.VMEM((cols - 1, 8, tokens), F32),
            pltpu.SemaphoreType.DMA((cols - 1,)),
            pltpu.SemaphoreType.DMA((cols - 1,)),
            pltpu.SemaphoreType.DMA((2, max(rows - 1, 1))),
            pltpu.SemaphoreType.DMA((2, max(rows - 1, 1))),
        ],
        compiler_params=pltpu.CompilerParams(collective_id=0, has_side_effects=True),
        name="gather_inputs",
    )(features, ln_gain.reshape(1, width), cotangent)


def owner_z(piece):
    return piece if piece < 3 else piece - 3 if piece < 6 else 3


def owner_slot(piece):
    return 0 if piece < 3 else 1 if piece < 6 else piece - 6


UNITS = 20
STEPS = PIECES + 3


def core_kernel(
    dps, rows, cols,
    x_ref, c_ref, wq_ref, wup_ref, wout_ref, wdown_ref, gain_ref,
    feat_ref, cot_ref, ln_ref, avg_ref, factor_ref,
    output_ref, input_grad_ref, ln_grad_ref, gains_ref, qkv_ref, up_ref, out_ref, down_ref,
    g_ref, opp, right_send, left_send, right_acc, left_acc, own,
    half_left, half_right, full_left, full_right, z_send, z_recv,
    dhalf_left, dhalf_right, dfull_left, dfull_right,
    x_turned, c_turned, out_acc, norm_acc, row_out, row_in,
    gain_mine, gain_in, stat_mine, stat_in, last_mine, last_in,
    s_opp, r_half, s_side, r_full, s_z, r_z, s_own, r_own, s_fwd, r_fwd, s_zag, r_zag,
    s_dopp, r_dhalf, s_dside, r_dfull, s_row, r_row, s_gain, r_gain, s_stat, r_stat, s_last, r_last,
):
    dp, row, col = lax.axis_index("dp"), lax.axis_index("row"), lax.axis_index("col")
    xi, zi = col // SIDE, lax.rem(col, SIDE)
    xr, xl, xo = lax.rem(xi + 1, SIDE), lax.rem(xi + 3, SIDE), lax.rem(xi + 2, SIDE)
    right, left = (dp, row, xr * SIDE + zi), (dp, row, xl * SIDE + zi)
    images, patches, width = x_ref.shape
    own_patches = patches // rows
    tokens = images * own_patches
    teams = dps * rows
    full_rows, half_rows = 4 * patches, 2 * patches

    def z_peer(k):
        return (dp, row, xi * SIDE + lax.rem(zi + k, SIDE))

    def col_peer(k):
        return (dp, row, lax.rem(col + k, cols))

    def row_peer(k):
        return (dp, lax.rem(row + k, rows), col)

    def team_peer(k):
        other = lax.rem(dp * rows + row + k, teams)
        return (other // rows, lax.rem(other, rows), col)

    greet([col_peer(k) for k in range(1, cols)] + [team_peer(k) for k in range(1, teams)])

    def run_start(block, pair):
        dest = lax.rem(block + pair, 4)
        return (dest * 6 + pair * 2) * HEAD, dest

    def partial_block(block, emit):
        image, run = block // 2, lax.rem(block, 2)
        triple = pl.ds(pl.multiple_of(run * 3 * HEAD, 3 * HEAD), 3 * HEAD)
        for part in range(3):
            start = part * 6 * HEAD + run * 3 * HEAD
            values = dot(x_ref[image], wq_ref[:, pl.ds(pl.multiple_of(start, HEAD), 3 * HEAD)])
            for z in range(3):
                emit(z, part, values[:, z * HEAD : (z + 1) * HEAD])
        values = dot_nt(c_ref[image], wout_ref[triple, :])
        for z in range(3):
            emit(z, 3, values[:, z * HEAD : (z + 1) * HEAD])
        for pair in range(3):
            start, _ = run_start(block, pair)
            hidden = pl.ds(pl.multiple_of(start, 2 * HEAD), 2 * HEAD)
            for im in range(2):
                values = dot(x_ref[im], wup_ref[:, hidden])
                for j in range(2):
                    emit(3 + 2 * pair + j, im, values[:, j * HEAD : (j + 1) * HEAD])
                values = dot_nt(c_ref[im], wdown_ref[hidden, :])
                for j in range(2):
                    emit(3 + 2 * pair + j, 2 + im, values[:, j * HEAD : (j + 1) * HEAD])

    def at(ref, p, part, parts=1):
        return ref.at[span(p, part, parts)]

    def span(p, part, parts=1):
        return pl.ds(pl.multiple_of(p * full_rows + part * patches, patches), parts * patches)

    def half_span(p):
        return pl.ds(pl.multiple_of(p * half_rows, half_rows), half_rows)

    def opp_right(p):
        return remote(
            at(opp, p, 0, 2), half_left.at[half_span(p)], s_opp.at[0, p], r_half.at[0, p], right
        )

    def opp_left(p):
        return remote(
            at(opp, p, 2, 2), half_right.at[half_span(p)], s_opp.at[1, p], r_half.at[1, p], left
        )

    def side_right(p, half):
        return remote(
            at(right_send, p, 2 * half, 2),
            at(full_left, p, 2 * half, 2),
            s_side.at[0, half, p],
            r_full.at[0, half, p],
            right,
        )

    def side_left(p, half):
        return remote(
            at(left_send, p, 2 * half, 2),
            at(full_right, p, 2 * half, 2),
            s_side.at[1, half, p],
            r_full.at[1, half, p],
            left,
        )

    def turn_order(i):
        return lax.rem(i + 2, 3) * 3 + i // 3

    def emit_opp(p, part, values):
        opp[span(p, part)] = values.astype(BF16)

    partial_block(xo, emit_opp)

    def send_opp(i, carry):
        p = turn_order(i)
        opp_right(p).start()
        opp_left(p).start()
        return carry

    lax.fori_loop(0, PIECES, send_opp, 0)

    def emit_right(p, part, values):
        if part >= 2:
            right_send[span(p, part)] = values.astype(BF16)
        else:
            right_acc[pl.ds(p * half_rows + part * patches, patches)] = values

    partial_block(xr, emit_right)

    def emit_left(p, part, values):
        if part < 2:
            left_send[span(p, part)] = values.astype(BF16)
        else:
            left_acc[pl.ds(p * half_rows + (part - 2) * patches, patches)] = values

    partial_block(xl, emit_left)

    def pass_on(i, carry):
        p = turn_order(i)
        side_right(p, 1).start()
        side_left(p, 0).start()
        opp_right(p).wait_recv()
        right_send[span(p, 0, 2)] = (
            right_acc[half_span(p)] + half_left[half_span(p)].astype(F32)
        ).astype(BF16)
        side_right(p, 0).start()
        opp_left(p).wait_recv()
        left_send[span(p, 2, 2)] = (
            left_acc[half_span(p)] + half_right[half_span(p)].astype(F32)
        ).astype(BF16)
        side_left(p, 1).start()
        return carry

    lax.fori_loop(0, PIECES, pass_on, 0)

    def emit_own(p, part, values):
        own[span(p, part)] = values

    partial_block(xi, emit_own)
    for im in range(images):
        here = slice(im * patches, (im + 1) * patches)
        x_turned[:, here] = x_ref[im].T
        c_turned[:, here] = c_ref[im].T

    def z_copy(p, k):
        return remote(
            at(z_send, p, 0, 4),
            z_recv.at[k - 1, owner_slot(p)],
            s_z.at[p],
            r_z.at[k - 1, owner_slot(p)],
            z_peer(k),
        )

    for i in range(PIECES):
        p = ((i + 2) % 3) * 3 + i // 3
        for half in range(2):
            side_right(p, half).wait_recv()
            side_left(p, half).wait_recv()
        here = span(p, 0, 4)
        own[here] = own[here] + full_left[here].astype(F32) + full_right[here].astype(F32)
        for k in range(1, SIDE):

            @pl.when(lax.rem(zi + k, SIDE) == owner_z(p))
            def _():
                z_send[here] = own[here].astype(BF16)
                z_copy(p, k).start()

    def arrived(p, slot):
        for k in range(1, SIDE):
            remote(
                at(z_send, 0, 0, 4),
                z_recv.at[k - 1, slot],
                s_z.at[0],
                r_z.at[k - 1, slot],
                z_peer(k),
            ).wait_recv()

    def summed(p, slot, part):
        total = own[span(p, part)]
        here = slice(part * patches, (part + 1) * patches)
        for k in range(1, SIDE):
            total = total + z_recv[k - 1, slot, here].astype(F32)
        return total

    def own_ag(p, way):
        peer = right if way == 0 else left
        return remote(g_ref.at[xi, p], g_ref.at[xi, p], s_own.at[way, p], r_own.at[way, p], peer)

    def z_ag(p, k):
        return remote(g_ref.at[xi, p], g_ref.at[xi, p], s_zag.at[k - 1, p], r_zag.at[p], z_peer(k))

    def launch(p):
        for way in range(2):
            own_ag(p, way).start()
        for k in range(1, SIDE):
            z_ag(p, k).start()

    def hidden_units(p, slot):
        arrived(p, slot)
        for im in range(2):
            value, slope = gelu_both(summed(p, slot, im))
            g_ref[xi, p, im] = value.astype(BF16)
            g_ref[xi, p, 2 + im] = (summed(p, slot, 2 + im) * slope).astype(BF16)
        launch(p)

    scale = HEAD ** (-0.5)

    def attention(p):
        arrived(p, 0)
        query_hat, query_factor = normalize(summed(p, 0, 0))
        key_hat, key_factor = normalize(summed(p, 0, 1))
        query_gain, key_gain = gain_ref[0:1, :], gain_ref[1:2, :]
        query = (query_hat * query_gain).astype(BF16)
        key = (key_hat * key_gain).astype(BF16)
        value = summed(p, 0, 2).astype(BF16)
        grad = summed(p, 0, 3).astype(BF16)
        expo = jnp.exp(dot_nt(query, key) * scale)
        weights = expo / jnp.sum(expo, -1, keepdims=True)
        weights_half = weights.astype(BF16)
        g_ref[xi, p, 0] = dot(weights_half, value).astype(BF16)
        weight_grad = dot_nt(grad, value)
        score_grad = weights * (weight_grad - jnp.sum(weights * weight_grad, -1, keepdims=True))
        score_grad = score_grad.astype(BF16)
        query_grad = dot(score_grad, key) * scale
        key_grad = dot(score_grad.T, query) * scale
        value_grad = dot(weights_half.T, grad)
        gain_mine[0:1, :] = jnp.sum(query_grad * query_hat, 0, keepdims=True)
        gain_mine[1:2, :] = jnp.sum(key_grad * key_hat, 0, keepdims=True)
        g_ref[xi, p, 1] = norm_back(query_grad, query_hat, query_factor, query_gain).astype(BF16)
        g_ref[xi, p, 2] = norm_back(key_grad, key_hat, key_factor, key_gain).astype(BF16)
        g_ref[xi, p, 3] = value_grad.astype(BF16)
        launch(p)

    gain_mine[...] = jnp.zeros_like(gain_mine)

    @pl.when(zi < 3)
    def _():
        hidden_units(zi + 3, 1)
        attention(zi)

    @pl.when(zi == 3)
    def _():
        for j in range(3):
            hidden_units(6 + j, j)

    def gain_copy(k):
        return remote(
            gain_mine, gain_in.at[k - 1], s_gain.at[k - 1], r_gain.at[k - 1], col_peer(k)
        )

    for k in range(1, cols):
        gain_copy(k).start()

    def settle(p, carry):
        opp_right(p).wait_send()
        opp_left(p).wait_send()
        for half in range(2):
            side_right(p, half).wait_send()
            side_left(p, half).wait_send()
        return carry

    lax.fori_loop(0, PIECES, settle, 0)
    out_acc[...] = jnp.zeros_like(out_acc)
    norm_acc[...] = jnp.zeros_like(norm_acc)

    low, high = pl.ds(0, 2), pl.ds(2, 2)

    def fwd_copy(p, way):
        block = xl if way == 0 else xr
        part = low if way == 0 else high
        there = right if way == 0 else left
        return remote(
            g_ref.at[block, p, part],
            g_ref.at[block, p, part],
            s_fwd.at[way, p],
            r_fwd.at[way, p],
            there,
        )

    own_count = jnp.where(zi == 3, 3, 2)

    def piece_at(i):
        piece, start = i * 0, 0
        for step in range(SIDE):
            z = lax.rem(zi + step, SIDE)
            count = jnp.where(z == 3, 3, 2)
            slot = i - start
            named = jnp.where(z == 3, 6 + slot, z + 3 * slot)
            piece = jnp.where((slot >= 0) & (slot < count), named, piece)
            start = start + count
        return piece

    dp_right = (lax.rem(dp + 1, dps), row, col)
    dp_left = (lax.rem(dp + dps - 1, dps), row, col)
    half_width = width // 2

    def unit_span(u, half=None):
        if half is None:
            return pl.ds(pl.multiple_of(u * width, width), width)
        return pl.ds(pl.multiple_of(u * width + half * half_width, half_width), half_width)

    def small_span(u):
        return pl.ds(pl.multiple_of(u * half_width, half_width), half_width)

    def dopp_right(u):
        return remote(
            opp.at[unit_span(u, 0)], dhalf_left.at[small_span(u)],
            s_dopp.at[0, u], r_dhalf.at[0, u], dp_right,
        )

    def dopp_left(u):
        return remote(
            opp.at[unit_span(u, 1)], dhalf_right.at[small_span(u)],
            s_dopp.at[1, u], r_dhalf.at[1, u], dp_left,
        )

    def dside_right(u, half):
        return remote(
            right_send.at[unit_span(u, half)], dfull_left.at[unit_span(u, half)],
            s_dside.at[0, half, u], r_dfull.at[0, half, u], dp_right,
        )

    def dside_left(u, half):
        return remote(
            left_send.at[unit_span(u, half)], dfull_right.at[unit_span(u, half)],
            s_dside.at[1, half, u], r_dfull.at[1, half, u], dp_left,
        )

    def emit_unit(dest, u, values):
        away = lax.rem(dest - dp + 4, 4)

        @pl.when(away == 0)
        def _():
            own[unit_span(u)] = values

        if dps == 1:
            return

        @pl.when(away == 2)
        def _():
            opp[unit_span(u)] = values.astype(BF16)
            dopp_right(u).start()
            dopp_left(u).start()

        @pl.when(away == 1)
        def _():
            right_acc[small_span(u)] = values[:half_width]
            right_send[unit_span(u, 1)] = values[half_width:].astype(BF16)
            dside_right(u, 1).start()

        @pl.when(away == 3)
        def _():
            left_acc[small_span(u)] = values[half_width:]
            left_send[unit_span(u, 0)] = values[:half_width].astype(BF16)
            dside_left(u, 0).start()

    def pass_unit(dest, u):
        if dps == 1:
            return
        away = lax.rem(dest - dp + 4, 4)

        @pl.when(away == 1)
        def _():
            dopp_right(u).wait_recv()
            right_send[unit_span(u, 0)] = (
                right_acc[small_span(u)] + dhalf_left[small_span(u)].astype(F32)
            ).astype(BF16)
            dside_right(u, 0).start()

        @pl.when(away == 3)
        def _():
            dopp_left(u).wait_recv()
            left_send[unit_span(u, 1)] = (
                left_acc[small_span(u)] + dhalf_right[small_span(u)].astype(F32)
            ).astype(BF16)
            dside_left(u, 1).start()

    def hidden_place(block, p):
        pair, second = (p - 3) // 2, lax.rem(p - 3, 2)
        start, dest = run_start(block, pair)
        return pl.multiple_of(start + second * HEAD, HEAD), dest, pair * 2 + second

    def hidden_back(block, p):
        start, dest, u = hidden_place(block, p)
        run = pl.ds(start, HEAD)
        hidden = g_ref[block, p, low].reshape(half_rows, HEAD)
        pre = g_ref[block, p, high].reshape(half_rows, HEAD)
        emit_unit(dest, u, dot(x_turned[...], pre))
        emit_unit(dest, 6 + u, dot(c_turned[...], hidden))
        out_acc[...] += dot(hidden, wdown_ref[run, :])
        norm_acc[...] += dot_nt(pre, wup_ref[:, run])

    def attention_dests(run, z):
        return 2 * run + jnp.where(z == 2, 1, 0), 2 * run + 1, jnp.where(z == 1, 1, 0)

    def attention_back(block, z):
        image, run = block // 2, lax.rem(block, 2)
        head = run * 3 + z
        here = pl.ds(pl.multiple_of(image * patches, patches), patches)
        out_acc[here] += dot(
            g_ref[block, z, 0], wout_ref[pl.ds(pl.multiple_of(head * HEAD, HEAD), HEAD), :]
        )
        total = norm_acc[here]
        for part in range(3):
            columns = pl.ds(pl.multiple_of((part * 6 + head) * HEAD, HEAD), HEAD)
            total = total + dot_nt(g_ref[block, z, 1 + part], wq_ref[:, columns])
        norm_acc[here] = total

    def attention_weights(run, z):
        dest, second, which = attention_dests(run, z)
        for t in range(4):
            turned = c_turned if t == 3 else x_turned
            part = 0 if t == 3 else t + 1
            values = dot(turned[:, 0:patches], g_ref[run, z, part]) + dot(
                turned[:, patches : 2 * patches], g_ref[run + 2, z, part]
            )
            u = 12 + 2 * t + which
            emit_unit(dest, u, values)

            @pl.when(z == 1)
            def _():
                emit_unit(second, u, values)

    def pass_hidden(block, p):
        _, dest, u = hidden_place(block, p)
        pass_unit(dest, u)
        pass_unit(dest, 6 + u)

    def pass_attention(run, z):
        dest, second, which = attention_dests(run, z)
        for t in range(4):
            u = 12 + 2 * t + which
            pass_unit(dest, u)

            @pl.when(z == 1)
            def _():
                pass_unit(second, u)

    def step(i, carry):
        ahead = i + 2

        @pl.when((ahead >= own_count) & (ahead < PIECES))
        def _():
            p = piece_at(ahead)
            z_ag(p, 1).wait_recv()
            for way in range(2):
                own_ag(p, way).start()

        @pl.when(i < PIECES)
        def _():
            p = piece_at(i)
            for way in range(2):
                own_ag(p, way).wait_recv()
                fwd_copy(p, way).start()

        @pl.when((i >= 2) & (i < PIECES + 2))
        def _():
            p = piece_at(i - 2)
            for way in range(2):
                fwd_copy(p, way).wait_recv()

        def each_block(k, carry):
            block = lax.rem(xi + k, 4)
            turn = i - jnp.where(k == 2, 2, 0)
            p = piece_at(turn)
            live = (turn >= 0) & (turn < PIECES)

            @pl.when(live & (p >= 3))
            def _():
                hidden_back(block, p)

            @pl.when(live & (p < 3))
            def _():
                attention_back(block, p)

            @pl.when(live & (p < 3) & (k >= 2))
            def _():
                attention_weights(lax.rem(block, 2), p)

            return carry

        lax.fori_loop(0, SIDE, each_block, 0)

        def each_pass(k, carry):
            block = lax.rem(xi + k, 4)
            turn = i - jnp.where(k == 2, 3, 1)
            p = piece_at(turn)
            live = (turn >= 0) & (turn < PIECES)

            @pl.when(live & (p >= 3))
            def _():
                pass_hidden(block, p)

            @pl.when(live & (p < 3) & (k >= 2))
            def _():
                pass_attention(lax.rem(block, 2), p)

            return carry

        lax.fori_loop(0, SIDE, each_pass, 0)
        return carry

    lax.fori_loop(0, STEPS, step, 0)

    for which, acc in enumerate((out_acc, norm_acc)):
        for im in range(images):
            here = slice(im * patches, (im + 1) * patches)
            row_out[which, im] = acc[here].astype(BF16)

    def row_copy(k):
        there = lax.rem(row + k, rows)
        return remote(
            row_out.at[:, :, pl.ds(pl.multiple_of(there * own_patches, own_patches), own_patches), :],
            row_in.at[k - 1],
            s_row.at[k - 1],
            r_row.at[k - 1],
            row_peer(k),
        )

    for k in range(1, rows):
        row_copy(k).start()
    for k in range(1, rows):
        row_copy(k).wait_recv()

    def row_total(which, acc):
        parts = []
        for im in range(images):
            start = im * patches + row * own_patches
            total = acc[pl.ds(pl.multiple_of(start, own_patches), own_patches)]
            for k in range(1, rows):
                total = total + row_in[k - 1, which, im].astype(F32)
            parts.append(total)
        return jnp.concatenate(parts, 0)

    inputs_wide = feat_ref[...].astype(F32).reshape(tokens, width)
    average, factor = avg_ref[:, 0:1], factor_ref[:, 0:1]
    normed = (inputs_wide - average) * factor
    norm_grad = row_total(1, norm_acc)
    scaled = norm_grad * ln_ref[...]
    ones = jnp.ones((8, width), F32)
    which = lax.broadcasted_iota(jnp.int32, (8, tokens), 0)
    stats = jnp.where(which == 0, exact_nt(ones, scaled), exact_nt(ones, scaled * normed))
    stat_mine[...] = stats

    def stat_copy(k):
        return remote(
            stat_mine, stat_in.at[k - 1], s_stat.at[k - 1], r_stat.at[k - 1], col_peer(k)
        )

    for k in range(1, cols):
        stat_copy(k).start()
    gains = gain_mine[...]
    for k in range(1, cols):
        gain_copy(k).wait_recv()
        gains = gains + gain_in[k - 1]
    last_mine[:, 0:HEAD] = gains
    last_mine[:, HEAD:] = jnp.broadcast_to(
        jnp.sum(norm_grad * normed, 0, keepdims=True), (8, width)
    )

    def last_copy(k):
        return remote(
            last_mine, last_in.at[k - 1], s_last.at[k - 1], r_last.at[k - 1], team_peer(k)
        )

    for k in range(1, teams):
        last_copy(k).start()
    output_ref[...] = (
        (inputs_wide + row_total(0, out_acc)).astype(BF16).reshape(images, own_patches, width)
    )
    for k in range(1, cols):
        stat_copy(k).wait_recv()
        stats = stats + stat_in[k - 1]
    stats = stats * (1.0 / (width * cols))
    eye = (
        lax.broadcasted_iota(jnp.int32, (tokens, tokens), 0)
        == lax.broadcasted_iota(jnp.int32, (tokens, tokens), 1)
    ).astype(F32)
    turned = exact_nt(eye, stats)
    centre, along = turned[:, 0:1], turned[:, 1:2]
    input_grad = cot_ref[...].astype(F32).reshape(tokens, width) + factor * (
        scaled - centre - normed * along
    )
    input_grad_ref[...] = input_grad.astype(BF16).reshape(images, own_patches, width)

    def unit_total(u):
        here = unit_span(u)
        total = own[here]
        if dps > 1:
            for half in range(2):
                dside_right(u, half).wait_recv()
                dside_left(u, half).wait_recv()
            total = total + dfull_left[here].astype(F32) + dfull_right[here].astype(F32)
        return total

    for u in range(6):
        columns = slice(u * HEAD, (u + 1) * HEAD)
        up_ref[:, columns] = unit_total(u)
        down_ref[columns, :] = unit_total(6 + u).T
        qkv_ref[u] = unit_total(12 + u)
    whole, split = unit_total(18).T, unit_total(19).T
    mid = HEAD // 2

    @pl.when(lax.rem(dp, 2) == 0)
    def _():
        out_ref[0:HEAD, :] = whole
        out_ref[HEAD : HEAD + mid, :] = split[0:mid]

    @pl.when(lax.rem(dp, 2) == 1)
    def _():
        out_ref[0:mid, :] = split[mid:]
        out_ref[mid : HEAD + mid, :] = whole

    last = last_mine[...]
    for k in range(1, teams):
        last_copy(k).wait_recv()
        last = last + last_in[k - 1]
    gains_ref[...] = last[:, 0:HEAD]
    ln_grad_ref[...] = last[0:1, HEAD:]

    def finish(p, carry):
        for way in range(2):
            own_ag(p, way).wait_send()
            fwd_copy(p, way).wait_send()
        return carry

    lax.fori_loop(0, PIECES, finish, 0)

    def finish_unit(u, carry):
        dopp_right(u).wait_send()
        dopp_left(u).wait_send()
        for half in range(2):
            dside_right(u, half).wait_send()
            dside_left(u, half).wait_send()
        return carry

    if dps > 1:
        lax.fori_loop(0, UNITS, finish_unit, 0)
    for p in range(PIECES):

        @pl.when(zi != owner_z(p))
        def _():
            z_copy(p, 1).wait_send()

        @pl.when(zi == owner_z(p))
        def _():
            for k in range(1, SIDE):
                z_ag(p, k).wait_send()

    for k in range(1, cols):
        gain_copy(k).wait_send()
        stat_copy(k).wait_send()
    for k in range(1, rows):
        row_copy(k).wait_send()
    for k in range(1, teams):
        last_copy(k).wait_send()


def exchange(
    x_all, c_all, w_qkv, w_up, w_out, w_down, qk_gain, features, cotangent, ln_gain, average, factor
):
    dps, rows, cols = lax.axis_size("dp"), lax.axis_size("row"), lax.axis_size("col")
    images, patches, width = x_all.shape
    own_patches = features.shape[1]
    tokens = images * own_patches
    teams = dps * rows
    dma = pltpu.SemaphoreType.DMA
    whole = max(PIECES * 4 * patches, UNITS * width)
    half = max(PIECES * 2 * patches, UNITS * width // 2)
    units = UNITS * width
    struct = jax.ShapeDtypeStruct
    others, mates, peers = max(teams - 1, 1), max(rows - 1, 1), cols - 1
    return pl.pallas_call(
        functools.partial(core_kernel, dps, rows, cols),
        out_shape=(
            struct(features.shape, BF16),
            struct(features.shape, BF16),
            struct((1, width), F32),
            struct((8, HEAD), F32),
            struct((6, width, HEAD), F32),
            struct((width, 6 * HEAD), F32),
            struct((3 * HEAD // 2, width), F32),
            struct((6 * HEAD, width), F32),
        ),
        in_specs=vmem(12),
        out_specs=tuple(vmem(8)),
        scratch_shapes=[
            pltpu.VMEM((SIDE, PIECES, 4, patches, HEAD), BF16),
            pltpu.VMEM((whole, HEAD), BF16),
            pltpu.VMEM((whole, HEAD), BF16),
            pltpu.VMEM((whole, HEAD), BF16),
            pltpu.VMEM((half, HEAD), F32),
            pltpu.VMEM((half, HEAD), F32),
            pltpu.VMEM((whole, HEAD), F32),
            pltpu.VMEM((PIECES * 2 * patches, HEAD), BF16),
            pltpu.VMEM((PIECES * 2 * patches, HEAD), BF16),
            pltpu.VMEM((PIECES * 4 * patches, HEAD), BF16),
            pltpu.VMEM((PIECES * 4 * patches, HEAD), BF16),
            pltpu.VMEM((PIECES * 4 * patches, HEAD), BF16),
            pltpu.VMEM((SIDE - 1, 3, 4 * patches, HEAD), BF16),
            pltpu.VMEM((units // 2, HEAD), BF16),
            pltpu.VMEM((units // 2, HEAD), BF16),
            pltpu.VMEM((units, HEAD), BF16),
            pltpu.VMEM((units, HEAD), BF16),
            pltpu.VMEM((width, images * patches), BF16),
            pltpu.VMEM((width, images * patches), BF16),
            pltpu.VMEM((images * patches, width), F32),
            pltpu.VMEM((images * patches, width), F32),
            pltpu.VMEM((2, images, patches, width), BF16),
            pltpu.VMEM((mates, 2, images, own_patches, width), BF16),
            pltpu.VMEM((8, HEAD), F32),
            pltpu.VMEM((peers, 8, HEAD), F32),
            pltpu.VMEM((8, tokens), F32),
            pltpu.VMEM((peers, 8, tokens), F32),
            pltpu.VMEM((8, HEAD + width), F32),
            pltpu.VMEM((others, 8, HEAD + width), F32),
            dma((2, PIECES)),
            dma((2, PIECES)),
            dma((2, 2, PIECES)),
            dma((2, 2, PIECES)),
            dma((PIECES,)),
            dma((SIDE - 1, 3)),
            dma((2, PIECES)),
            dma((2, PIECES)),
            dma((2, PIECES)),
            dma((2, PIECES)),
            dma((SIDE - 1, PIECES)),
            dma((PIECES,)),
            dma((2, UNITS)),
            dma((2, UNITS)),
            dma((2, 2, UNITS)),
            dma((2, 2, UNITS)),
            dma((mates,)),
            dma((mates,)),
            dma((peers,)),
            dma((peers,)),
            dma((peers,)),
            dma((peers,)),
            dma((others,)),
            dma((others,)),
        ],
        compiler_params=pltpu.CompilerParams(
            collective_id=1, has_side_effects=True, vmem_limit_bytes=VMEM_BYTES
        ),
        name="exchange",
    )(
        x_all, c_all, w_qkv, w_up, w_out, w_down, qk_gain,
        features, cotangent, ln_gain, average, factor,
    )


def on_device(features, ln_gain, w_qkv, qk_gain, w_up, w_out, w_down, cotangent):
    images, patches, width = features.shape
    head_cols = w_qkv.shape[2]
    x_all, c_all, average, factor = gather_inputs(features, ln_gain, cotangent)
    qkv_flat = w_qkv.reshape(width, 3 * head_cols)
    output, input_grad, ln_grad, gains, qkv_units, up_grad, out_grad, down_grad = exchange(
        x_all, c_all, qkv_flat, w_up, w_out, w_down, qk_gain,
        features, cotangent, ln_gain.reshape(1, width), average, factor,
    )
    units = qkv_units.reshape(3, 2, width, HEAD)
    whole, split = units[:, 0], units[:, 1]
    mid = HEAD // 2
    qkv_grad = jnp.where(
        lax.rem(lax.axis_index("dp"), 2) == 0,
        jnp.concatenate([whole, split[..., :mid]], -1),
        jnp.concatenate([split[..., mid:], whole], -1),
    )
    qkv_grad = jnp.transpose(qkv_grad, (1, 0, 2))
    return (
        output, input_grad, ln_grad.reshape(width), gains[:2], qkv_grad, up_grad, out_grad, down_grad
    )


def solution(mesh):
    in_specs = (
        P("dp", "row", "col"),
        P("col"),
        P("col", None, "row"),
        P(),
        P("col", "row"),
        P("row", "col"),
        P("row", "col"),
        P("dp", "row", "col"),
    )
    out_specs = (
        P("dp", "row", "col"),
        P("dp", "row", "col"),
        P("col"),
        P(),
        P("col", None, ("row", "dp")),
        P("col", ("row", "dp")),
        P(("row", "dp"), "col"),
        P(("row", "dp"), "col"),
    )
    return jax.shard_map(
        on_device, mesh=mesh, in_specs=in_specs, out_specs=out_specs, check_vma=False
    )
```

```python
import functools

import jax
import jax.numpy as jnp
from jax import lax
from jax.experimental import pallas as pl
from jax.experimental.pallas import tpu as pltpu
from jax.sharding import PartitionSpec as P

EPS = 1e-06
SQRT_HALF = 0.7071067811865476
INV_ROOT = 0.3989422804014327
HEAD = 128
SIDE = 4
PIECES = 9
MESH = pl.DeviceIdType.MESH
VMEM_BYTES = 62 * 1024 * 1024
F32 = jnp.float32
BF16 = jnp.bfloat16


def gelu_both(values):
    cdf = 0.5 * (1.0 + lax.erf(values * SQRT_HALF))
    slope = cdf + values * jnp.exp(-0.5 * values * values) * INV_ROOT
    return values * cdf, slope


def normalize(values):
    average = jnp.mean(values, -1, keepdims=True)
    spread = jnp.mean(values * values, -1, keepdims=True) - average * average
    factor = lax.rsqrt(spread + EPS)
    return ((values - average) * factor, factor)


def norm_back(grad_normed, normed, factor, gain):
    scaled = grad_normed * gain
    centre = jnp.mean(scaled, -1, keepdims=True)
    along = jnp.mean(scaled * normed, -1, keepdims=True)
    return factor * (scaled - centre - normed * along)


def dot(a, b):
    return lax.dot_general(a, b, (((1,), (0,)), ((), ())), preferred_element_type=F32)


def dot_nt(a, b):
    return lax.dot_general(a, b, (((1,), (1,)), ((), ())), preferred_element_type=F32)


def exact_nt(a, b):
    return lax.dot_general(
        a,
        b,
        (((1,), (1,)), ((), ())),
        precision=lax.Precision.HIGHEST,
        preferred_element_type=F32,
    )


def greet(peers):
    barrier = pltpu.get_barrier_semaphore()
    for peer in peers:
        pl.semaphore_signal(barrier, inc=1, device_id=peer, device_id_type=MESH)
    pl.semaphore_wait(barrier, len(peers))


def remote(src, dst, send, recv, peer):
    return pltpu.make_async_remote_copy(
        src_ref=src,
        dst_ref=dst,
        send_sem=send,
        recv_sem=recv,
        device_id=peer,
        device_id_type=MESH,
    )


def vmem(count):
    return [pl.BlockSpec(memory_space=pltpu.VMEM)] * count


def owner_z(piece):
    return piece if piece < 3 else piece - 3 if piece < 6 else 3


def owner_slot(piece):
    return 0 if piece < 3 else 1 if piece < 6 else piece - 6


UNITS = 20
BEHIND = 2
LATE = 1
STEPS = PIECES + 2 + LATE
SUM_ORDER = (6, 0, 7, 3, 8, 1, 2, 4, 5)
GATHER_ORDER = (
    (0, 3, 1, 4, 2, 5, 6, 7, 8),
    (1, 4, 0, 2, 3, 5, 6, 7, 8),
    (2, 5, 1, 6, 4, 7, 0, 8, 3),
    (6, 7, 8, 2, 5, 1, 4, 0, 3),
)


def core_kernel(
    dps, rows, cols,
    wq_hbm, wup_hbm, wout_hbm, wdown_hbm, gain_ref, feat_ref, cot_ref, ln_ref,
    output_ref, input_grad_ref, ln_grad_ref, gains_ref, qkv_ref, up_ref, out_ref, down_ref,
    x_ref, c_ref, wq_ref, wup_ref, wout_ref, wdown_ref, avg_ref, factor_ref,
    g_ref, opp, right_send, left_send, right_acc, left_acc, own,
    half_left, half_right, full_left, full_right, z_send, z_recv,
    dhalf_left, dhalf_right, dfull_left, dfull_right,
    x_turned, c_turned, out_acc, norm_acc, core_out, core_in, row_out, row_in,
    norm_mine, norm_in,
    gain_mine, gain_in, stat_mine, stat_in, last_mine, last_in,
    s_opp, r_half, s_side, r_full, s_z, r_z, s_own, r_own, s_fwd, r_fwd, s_zag, r_zag,
    s_load, s_norm, r_norm, s_rowg, r_rowg, s_core, r_core,
    s_dopp, r_dhalf, s_dside, r_dfull, s_row, r_row, s_gain, r_gain, s_stat, r_stat, s_last, r_last,
):
    dp, row, col = lax.axis_index("dp"), lax.axis_index("row"), lax.axis_index("col")
    xi, zi = col // SIDE, lax.rem(col, SIDE)
    xr, xl, xo = lax.rem(xi + 1, SIDE), lax.rem(xi + 3, SIDE), lax.rem(xi + 2, SIDE)
    right, left = (dp, row, xr * SIDE + zi), (dp, row, xl * SIDE + zi)
    images, patches, width = x_ref.shape
    own_patches = patches // rows
    tokens = images * own_patches
    teams = dps * rows
    full_rows, half_rows = 4 * patches, 2 * patches

    def col_peer(k):
        return (dp, row, lax.rem(col + k, cols))

    mate = (dp, row + 1 - 2 * lax.rem(row, 2), col)
    cross = (dp, lax.rem(row + 2, rows), col)

    def team_peer(k):
        other = lax.rem(dp * rows + row + k, teams)
        return (other // rows, lax.rem(other, rows), col)

    loads = [
        pltpu.make_async_copy(src, dst, s_load.at[i])
        for i, (src, dst) in enumerate(
            ((wdown_hbm, wdown_ref), (wout_hbm, wout_ref), (wup_hbm, wup_ref), (wq_hbm, wq_ref))
        )
    ]
    for load in loads:
        load.start()
    greet([col_peer(k) for k in range(1, cols)] + [team_peer(k) for k in range(1, teams)])

    def patch_rows(r):
        return pl.ds(pl.multiple_of(r * own_patches, own_patches), own_patches)

    def row_gather(which, ref, step):
        here = ref.at[:, patch_rows(row if step < 2 else lax.rem(row + 2, rows)), :]
        return remote(
            here, here, s_rowg.at[which, step], r_rowg.at[which, step], cross if step == 1 else mate
        )

    def row_send(which, ref):
        if rows > 1:
            row_gather(which, ref, 1).start()
            row_gather(which, ref, 0).start()

    def row_arrive(which, ref):
        if rows > 1:
            row_gather(which, ref, 1).wait_recv()
            row_gather(which, ref, 2).start()
            row_gather(which, ref, 0).wait_recv()
            row_gather(which, ref, 2).wait_recv()

    c_ref[:, patch_rows(row), :] = cot_ref[...]
    row_send(0, c_ref)
    inputs_wide = feat_ref[...].astype(F32).reshape(tokens, width)
    ones = jnp.ones((8, width), F32)
    which = lax.broadcasted_iota(jnp.int32, (8, tokens), 0)
    norm_sums = jnp.where(
        which == 0, exact_nt(ones, inputs_wide), exact_nt(ones, inputs_wide * inputs_wide)
    )
    norm_mine[...] = norm_sums

    def norm_copy(k):
        return remote(
            norm_mine, norm_in.at[k - 1], s_norm.at[k - 1], r_norm.at[k - 1], col_peer(k)
        )

    for k in range(1, cols):
        norm_copy(k).start()
    eye = (
        lax.broadcasted_iota(jnp.int32, (tokens, tokens), 0)
        == lax.broadcasted_iota(jnp.int32, (tokens, tokens), 1)
    ).astype(F32)

    def run_start(block, pair):
        dest = lax.rem(block + pair, 4)
        return (dest * 6 + pair * 2) * HEAD, dest

    def cot_block(block, emit, send=None):
        image, run = block // 2, lax.rem(block, 2)
        triple = pl.ds(pl.multiple_of(run * 3 * HEAD, 3 * HEAD), 3 * HEAD)
        for pair in range(3):
            start, _ = run_start(block, pair)
            hidden = pl.ds(pl.multiple_of(start, 2 * HEAD), 2 * HEAD)
            for im in range(2):
                values = dot_nt(c_ref[im], wdown_ref[hidden, :])
                for j in range(2):
                    emit(3 + 2 * pair + j, 2 + im, values[:, j * HEAD : (j + 1) * HEAD])
            if send is not None:
                for j in range(2):
                    send(3 + 2 * pair + j)
        values = dot_nt(c_ref[image], wout_ref[triple, :])
        for z in range(3):
            emit(z, 3, values[:, z * HEAD : (z + 1) * HEAD])

    def x_block(block, emit):
        image, run = block // 2, lax.rem(block, 2)
        for part in range(3):
            start = part * 6 * HEAD + run * 3 * HEAD
            values = dot(x_ref[image], wq_ref[:, pl.ds(pl.multiple_of(start, HEAD), 3 * HEAD)])
            for z in range(3):
                emit(z, part, values[:, z * HEAD : (z + 1) * HEAD])
        for pair in range(3):
            start, _ = run_start(block, pair)
            hidden = pl.ds(pl.multiple_of(start, 2 * HEAD), 2 * HEAD)
            for im in range(2):
                values = dot(x_ref[im], wup_ref[:, hidden])
                for j in range(2):
                    emit(3 + 2 * pair + j, im, values[:, j * HEAD : (j + 1) * HEAD])

    def at(ref, p, part, parts=1):
        return ref.at[span(p, part, parts)]

    def span(p, part, parts=1):
        return pl.ds(pl.multiple_of(p * full_rows + part * patches, patches), parts * patches)

    def half_span(p):
        return pl.ds(pl.multiple_of(p * half_rows, half_rows), half_rows)

    def opp_right(p):
        return remote(
            at(opp, p, 0, 2), half_left.at[half_span(p)], s_opp.at[0, p], r_half.at[0, p], right
        )

    def opp_left(p):
        return remote(
            at(opp, p, 2, 2), half_right.at[half_span(p)], s_opp.at[1, p], r_half.at[1, p], left
        )

    def side_right(p, half):
        return remote(
            at(right_send, p, 2 * half, 2),
            at(full_left, p, 2 * half, 2),
            s_side.at[0, half, p],
            r_full.at[0, half, p],
            right,
        )

    def side_left(p, half):
        return remote(
            at(left_send, p, 2 * half, 2),
            at(full_right, p, 2 * half, 2),
            s_side.at[1, half, p],
            r_full.at[1, half, p],
            left,
        )

    def emit_opp(p, part, values):
        opp[span(p, part)] = values.astype(BF16)

    def emit_right(p, part, values):
        if part >= 2:
            right_send[span(p, part)] = values.astype(BF16)
        else:
            right_acc[pl.ds(p * half_rows + part * patches, patches)] = values

    def emit_left(p, part, values):
        if part < 2:
            left_send[span(p, part)] = values.astype(BF16)
        else:
            left_acc[pl.ds(p * half_rows + (part - 2) * patches, patches)] = values

    def emit_own(p, part, values):
        own[span(p, part)] = values

    normed_sums = norm_sums
    for k in range(1, cols):
        norm_copy(k).wait_recv()
        normed_sums = normed_sums + norm_in[k - 1]
    normed_sums = normed_sums * (1.0 / (width * cols))
    average = normed_sums[0:1]
    factor = lax.rsqrt(normed_sums[1:2] - average * average + EPS)
    turned = exact_nt(eye, jnp.where(which == 0, average, factor))
    avg_ref[...] = jnp.broadcast_to(turned[:, 0:1], avg_ref.shape)
    factor_ref[...] = jnp.broadcast_to(turned[:, 1:2], factor_ref.shape)
    normed = (inputs_wide - turned[:, 0:1]) * turned[:, 1:2]
    x_ref[:, patch_rows(row), :] = (
        (normed * ln_ref[...]).astype(BF16).reshape(images, own_patches, width)
    )
    row_send(1, x_ref)

    row_arrive(0, c_ref)
    loads[0].wait()
    loads[1].wait()
    cot_block(xo, emit_opp, lambda p: opp_left(p).start())
    cot_block(xr, emit_right, lambda p: side_right(p, 1).start())
    loads[2].wait()
    loads[3].wait()
    row_arrive(1, x_ref)
    x_block(xo, emit_opp)
    for p in range(3):
        opp_left(p).start()
    for i in range(2):
        opp_right(SUM_ORDER[i]).start()
    x_block(xl, emit_left)
    for i in range(2):
        side_left(SUM_ORDER[i], 0).start()
    cot_block(xl, emit_left)
    x_block(xr, emit_right)
    cot_block(xi, emit_own)
    x_block(xi, emit_own)

    def pass_on(i):
        p = SUM_ORDER[i]
        if i + 2 < PIECES:
            opp_right(SUM_ORDER[i + 2]).start()
            side_left(SUM_ORDER[i + 2], 0).start()
        if p < 3:
            side_right(p, 1).start()
        opp_left(p).wait_recv()
        left_send[span(p, 2, 2)] = (
            left_acc[half_span(p)] + half_right[half_span(p)].astype(F32)
        ).astype(BF16)
        side_left(p, 1).start()
        opp_right(p).wait_recv()
        right_send[span(p, 0, 2)] = (
            right_acc[half_span(p)] + half_left[half_span(p)].astype(F32)
        ).astype(BF16)
        side_right(p, 0).start()

    z_up, z_down = (dp, row, xi * SIDE + lax.rem(zi + 1, SIDE)), (
        dp, row, xi * SIDE + lax.rem(zi + 3, SIDE)
    )

    def chain_copy(p, up):
        slot = p if up else jnp.where(zi - 1 == owner_z(p), PIECES + owner_slot(p), p)
        return remote(
            at(z_send, p, 0, 4),
            at(z_recv, slot, 0, 4),
            s_z.at[p],
            r_z.at[slot],
            z_up if up else z_down,
        )

    def chain_pass(p, up):
        here = span(p, 0, 4)
        chain_copy(p, True).wait_recv()
        z_send[here] = (own[here] + z_recv[here].astype(F32)).astype(BF16)
        chain_copy(p, up).start()

    def chain_end(p, up):
        here = span(p, 0, 4)
        z_send[here] = own[here].astype(BF16)
        chain_copy(p, up).start()

    for turn in range(PIECES + BEHIND + 2):
        if turn < PIECES:
            pass_on(turn)
        i = turn - BEHIND
        if 0 <= i < PIECES:
            p = SUM_ORDER[i]
            for half in range(2):
                side_right(p, half).wait_recv()
                side_left(p, half).wait_recv()
            here = span(p, 0, 4)
            own[here] = own[here] + full_left[here].astype(F32) + full_right[here].astype(F32)
            if owner_z(p) > 0:
                pl.when(zi == 0)(functools.partial(chain_end, p, True))
            if owner_z(p) < 3:
                pl.when(zi == 3)(functools.partial(chain_end, p, False))
        for lag in range(1, 3):
            if 0 <= i - lag < PIECES:
                p = SUM_ORDER[i - lag]
                if owner_z(p) > lag:
                    pl.when(zi == lag)(functools.partial(chain_pass, p, True))
                if owner_z(p) < 3 - lag:
                    pl.when(zi == 3 - lag)(functools.partial(chain_pass, p, False))

    for im in range(images):
        here = slice(im * patches, (im + 1) * patches)
        x_turned[:, here] = x_ref[im].T
        c_turned[:, here] = c_ref[im].T

    def arrived(p, slot):
        for come, place in ((zi > 0, p), (zi < 3, PIECES + slot)):

            @pl.when(come)
            def _():
                there, here = span(place, 0, 4), span(p, 0, 4)
                remote(
                    at(z_send, 0, 0, 4), z_recv.at[there], s_z.at[0], r_z.at[place], z_up
                ).wait_recv()
                own[here] = own[here] + z_recv[there].astype(F32)

    def summed(p, part):
        return own[span(p, part)]

    def own_ag(p, way):
        peer = right if way == 0 else left
        return remote(g_ref.at[xi, p], g_ref.at[xi, p], s_own.at[way, p], r_own.at[way, p], peer)

    def z_ag(p, up):
        way = 0 if up else 1
        peer = z_up if up else z_down
        return remote(g_ref.at[xi, p], g_ref.at[xi, p], s_zag.at[way, p], r_zag.at[p], peer)

    def launch(p):
        for way in range(2):
            own_ag(p, way).start()
        pl.when(zi < 3)(lambda: z_ag(p, True).start())
        pl.when(zi > 0)(lambda: z_ag(p, False).start())

    def hidden_units(p, slot):
        arrived(p, slot)
        for im in range(2):
            value, slope = gelu_both(summed(p, im))
            g_ref[xi, p, im] = value.astype(BF16)
            g_ref[xi, p, 2 + im] = (summed(p, 2 + im) * slope).astype(BF16)
        launch(p)

    scale = HEAD ** (-0.5)

    def attention(p):
        arrived(p, 0)
        query_hat, query_factor = normalize(summed(p, 0))
        key_hat, key_factor = normalize(summed(p, 1))
        query_gain, key_gain = gain_ref[0:1, :], gain_ref[1:2, :]
        query = (query_hat * query_gain).astype(BF16)
        key = (key_hat * key_gain).astype(BF16)
        value = summed(p, 2).astype(BF16)
        grad = summed(p, 3).astype(BF16)
        expo = jnp.exp(dot_nt(query, key) * scale)
        weights = expo / jnp.sum(expo, -1, keepdims=True)
        weights_half = weights.astype(BF16)
        g_ref[xi, p, 0] = dot(weights_half, value).astype(BF16)
        weight_grad = dot_nt(grad, value)
        score_grad = weights * (weight_grad - jnp.sum(weights * weight_grad, -1, keepdims=True))
        score_grad = score_grad.astype(BF16)
        query_grad = dot(score_grad, key) * scale
        key_grad = dot(score_grad.T, query) * scale
        value_grad = dot(weights_half.T, grad)
        gain_mine[0:1, :] = jnp.sum(query_grad * query_hat, 0, keepdims=True)
        gain_mine[1:2, :] = jnp.sum(key_grad * key_hat, 0, keepdims=True)
        g_ref[xi, p, 1] = norm_back(query_grad, query_hat, query_factor, query_gain).astype(BF16)
        g_ref[xi, p, 2] = norm_back(key_grad, key_hat, key_factor, key_gain).astype(BF16)
        g_ref[xi, p, 3] = value_grad.astype(BF16)
        launch(p)

    gain_mine[...] = jnp.zeros_like(gain_mine)

    @pl.when(zi < 3)
    def _():
        attention(zi)
        hidden_units(zi + 3, 1)

    @pl.when(zi == 3)
    def _():
        for j in range(3):
            hidden_units(6 + j, j)

    def gain_copy(k):
        return remote(
            gain_mine, gain_in.at[k - 1], s_gain.at[k - 1], r_gain.at[k - 1], col_peer(k)
        )

    for k in range(1, cols):
        gain_copy(k).start()

    def settle(p, carry):
        opp_right(p).wait_send()
        opp_left(p).wait_send()
        for half in range(2):
            side_right(p, half).wait_send()
            side_left(p, half).wait_send()
        return carry

    lax.fori_loop(0, PIECES, settle, 0)
    out_acc[...] = jnp.zeros_like(out_acc)
    norm_acc[...] = jnp.zeros_like(norm_acc)

    low, high = pl.ds(0, 2), pl.ds(2, 2)

    def fwd_copy(p, way):
        block = xl if way == 0 else xr
        part = low if way == 0 else high
        there = right if way == 0 else left
        return remote(
            g_ref.at[block, p, part],
            g_ref.at[block, p, part],
            s_fwd.at[way, p],
            r_fwd.at[way, p],
            there,
        )

    own_count = jnp.where(zi == 3, 3, 2)

    def piece_at(i):
        piece = i * 0
        for place in range(PIECES):
            named = GATHER_ORDER[0][place]
            for z in range(1, SIDE):
                named = jnp.where(zi == z, GATHER_ORDER[z][place], named)
            piece = jnp.where(i == place, named, piece)
        return piece

    def owner_of(p):
        return jnp.where(p < 3, p, jnp.where(p < 6, p - 3, 3))

    dp_right = (lax.rem(dp + 1, dps), row, col)
    dp_left = (lax.rem(dp + dps - 1, dps), row, col)
    half_width = width // 2

    def unit_span(u, half=None):
        if half is None:
            return pl.ds(pl.multiple_of(u * width, width), width)
        return pl.ds(pl.multiple_of(u * width + half * half_width, half_width), half_width)

    def small_span(u):
        return pl.ds(pl.multiple_of(u * half_width, half_width), half_width)

    def dopp_right(u):
        return remote(
            opp.at[unit_span(u, 0)], dhalf_left.at[small_span(u)],
            s_dopp.at[0, u], r_dhalf.at[0, u], dp_right,
        )

    def dopp_left(u):
        return remote(
            opp.at[unit_span(u, 1)], dhalf_right.at[small_span(u)],
            s_dopp.at[1, u], r_dhalf.at[1, u], dp_left,
        )

    def dside_right(u, half):
        return remote(
            right_send.at[unit_span(u, half)], dfull_left.at[unit_span(u, half)],
            s_dside.at[0, half, u], r_dfull.at[0, half, u], dp_right,
        )

    def dside_left(u, half):
        return remote(
            left_send.at[unit_span(u, half)], dfull_right.at[unit_span(u, half)],
            s_dside.at[1, half, u], r_dfull.at[1, half, u], dp_left,
        )

    def emit_unit(dest, u, values):
        away = lax.rem(dest - dp + 4, 4)

        @pl.when(away == 0)
        def _():
            own[unit_span(u)] = values

        if dps == 1:
            return

        @pl.when(away == 2)
        def _():
            opp[unit_span(u)] = values.astype(BF16)
            dopp_right(u).start()
            dopp_left(u).start()

        @pl.when(away == 1)
        def _():
            right_acc[small_span(u)] = values[:half_width]
            right_send[unit_span(u, 1)] = values[half_width:].astype(BF16)
            dside_right(u, 1).start()

        @pl.when(away == 3)
        def _():
            left_acc[small_span(u)] = values[half_width:]
            left_send[unit_span(u, 0)] = values[:half_width].astype(BF16)
            dside_left(u, 0).start()

    def pass_unit(dest, u):
        if dps == 1:
            return
        away = lax.rem(dest - dp + 4, 4)

        @pl.when(away == 1)
        def _():
            dopp_right(u).wait_recv()
            right_send[unit_span(u, 0)] = (
                right_acc[small_span(u)] + dhalf_left[small_span(u)].astype(F32)
            ).astype(BF16)
            dside_right(u, 0).start()

        @pl.when(away == 3)
        def _():
            dopp_left(u).wait_recv()
            left_send[unit_span(u, 1)] = (
                left_acc[small_span(u)] + dhalf_right[small_span(u)].astype(F32)
            ).astype(BF16)
            dside_left(u, 1).start()

    def hidden_place(block, p):
        pair, second = (p - 3) // 2, lax.rem(p - 3, 2)
        start, dest = run_start(block, pair)
        return pl.multiple_of(start + second * HEAD, HEAD), dest, pair * 2 + second

    def hidden_back(block, p):
        start, dest, u = hidden_place(block, p)
        run = pl.ds(start, HEAD)
        hidden = g_ref[block, p, low].reshape(half_rows, HEAD)
        pre = g_ref[block, p, high].reshape(half_rows, HEAD)
        emit_unit(dest, u, dot(x_turned[...], pre))
        emit_unit(dest, 6 + u, dot(c_turned[...], hidden))
        out_acc[...] += dot(hidden, wdown_ref[run, :])
        norm_acc[...] += dot_nt(pre, wup_ref[:, run])

    def attention_dests(run, z):
        return 2 * run + jnp.where(z == 2, 1, 0), 2 * run + 1, jnp.where(z == 1, 1, 0)

    def attention_back(block, z):
        image, run = block // 2, lax.rem(block, 2)
        head = run * 3 + z
        here = pl.ds(pl.multiple_of(image * patches, patches), patches)
        out_acc[here] += dot(
            g_ref[block, z, 0], wout_ref[pl.ds(pl.multiple_of(head * HEAD, HEAD), HEAD), :]
        )
        total = norm_acc[here]
        for part in range(3):
            columns = pl.ds(pl.multiple_of((part * 6 + head) * HEAD, HEAD), HEAD)
            total = total + dot_nt(g_ref[block, z, 1 + part], wq_ref[:, columns])
        norm_acc[here] = total

    def attention_weights(run, z):
        dest, second, which = attention_dests(run, z)
        for t in range(4):
            turned = c_turned if t == 3 else x_turned
            part = 0 if t == 3 else t + 1
            values = dot(turned[:, 0:patches], g_ref[run, z, part]) + dot(
                turned[:, patches : 2 * patches], g_ref[run + 2, z, part]
            )
            u = 12 + 2 * t + which
            emit_unit(dest, u, values)

            @pl.when(z == 1)
            def _():
                emit_unit(second, u, values)

    def pass_hidden(block, p):
        _, dest, u = hidden_place(block, p)
        pass_unit(dest, u)
        pass_unit(dest, 6 + u)

    def pass_attention(run, z):
        dest, second, which = attention_dests(run, z)
        for t in range(4):
            u = 12 + 2 * t + which
            pass_unit(dest, u)

            @pl.when(z == 1)
            def _():
                pass_unit(second, u)

    def step(i, carry):
        ahead = i + 2

        @pl.when((ahead >= own_count) & (ahead < PIECES))
        def _():
            p = piece_at(ahead)
            z_ag(p, True).wait_recv()
            for way in range(2):
                own_ag(p, way).start()
            owner = owner_of(p)
            pl.when((owner < zi) & (zi < 3))(lambda: z_ag(p, True).start())
            pl.when((owner > zi) & (zi > 0))(lambda: z_ag(p, False).start())

        @pl.when(i < PIECES)
        def _():
            p = piece_at(i)
            for way in range(2):
                own_ag(p, way).wait_recv()
                fwd_copy(p, way).start()

        @pl.when((i >= 2) & (i < PIECES + 2))
        def _():
            p = piece_at(i - 2)
            for way in range(2):
                fwd_copy(p, way).wait_recv()

        def each_block(k, carry):
            block = lax.rem(xi + k, 4)
            turn = i - jnp.where(k == 2, 2, 0)
            p = piece_at(turn)
            live = (turn >= 0) & (turn < PIECES)

            @pl.when(live & (p >= 3))
            def _():
                hidden_back(block, p)

            @pl.when(live & (p < 3))
            def _():
                attention_back(block, p)

            @pl.when(live & (p < 3) & (k >= 2))
            def _():
                attention_weights(lax.rem(block, 2), p)

            return carry

        lax.fori_loop(0, SIDE, each_block, 0)

        def each_pass(k, carry):
            block = lax.rem(xi + k, 4)
            turn = i - LATE - jnp.where(k == 2, 2, 0)
            p = piece_at(turn)
            live = (turn >= 0) & (turn < PIECES)

            @pl.when(live & (p >= 3))
            def _():
                pass_hidden(block, p)

            @pl.when(live & (p < 3) & (k >= 2))
            def _():
                pass_attention(lax.rem(block, 2), p)

            return carry

        lax.fori_loop(0, SIDE, each_pass, 0)
        return carry

    lax.fori_loop(0, STEPS, step, 0)

    accs = (out_acc, norm_acc)
    parity = lax.rem(row, 2)

    def row_part(acc, r, im):
        start = im * patches + r * own_patches
        return acc[pl.ds(pl.multiple_of(start, own_patches), own_patches)]

    core_copy = remote(core_out, core_in, s_core.at[0], r_core.at[0], mate)
    row_copy = remote(row_out, row_in, s_row.at[0], r_row.at[0], cross)
    other_high = lax.rem(row // 2 + 1, 2)
    if rows > 1:
        for w, acc in enumerate(accs):
            for im in range(images):
                for j, high_z in enumerate((other_high, row // 2)):
                    core_out[j, w, im] = row_part(acc, high_z * 2 + 1 - parity, im).astype(BF16)
        core_copy.start()
        core_copy.wait_recv()
        for w, acc in enumerate(accs):
            for im in range(images):
                row_out[w, im] = (
                    row_part(acc, lax.rem(row + 2, rows), im) + core_in[0, w, im].astype(F32)
                ).astype(BF16)
        row_copy.start()
        row_copy.wait_recv()

    def row_total(w, acc):
        parts = []
        for im in range(images):
            total = row_part(acc, row, im)
            if rows > 1:
                total = total + core_in[1, w, im].astype(F32) + row_in[w, im].astype(F32)
            parts.append(total)
        return jnp.concatenate(parts, 0)

    inputs_wide = feat_ref[...].astype(F32).reshape(tokens, width)
    average, factor = avg_ref[:, 0:1], factor_ref[:, 0:1]
    normed = (inputs_wide - average) * factor
    norm_grad = row_total(1, norm_acc)
    scaled = norm_grad * ln_ref[...]
    stats = jnp.where(which == 0, exact_nt(ones, scaled), exact_nt(ones, scaled * normed))
    stat_mine[...] = stats

    def stat_copy(k):
        return remote(
            stat_mine, stat_in.at[k - 1], s_stat.at[k - 1], r_stat.at[k - 1], col_peer(k)
        )

    for k in range(1, cols):
        stat_copy(k).start()
    gains = gain_mine[...]
    for k in range(1, cols):
        gain_copy(k).wait_recv()
        gains = gains + gain_in[k - 1]
    last_mine[:, 0:HEAD] = gains
    last_mine[:, HEAD:] = jnp.broadcast_to(
        jnp.sum(norm_grad * normed, 0, keepdims=True), (8, width)
    )

    def last_copy(k):
        return remote(
            last_mine, last_in.at[k - 1], s_last.at[k - 1], r_last.at[k - 1], team_peer(k)
        )

    for k in range(1, teams):
        last_copy(k).start()
    output_ref[...] = (
        (inputs_wide + row_total(0, out_acc)).astype(BF16).reshape(images, own_patches, width)
    )
    for k in range(1, cols):
        stat_copy(k).wait_recv()
        stats = stats + stat_in[k - 1]
    stats = stats * (1.0 / (width * cols))
    turned = exact_nt(eye, stats)
    centre, along = turned[:, 0:1], turned[:, 1:2]
    input_grad = cot_ref[...].astype(F32).reshape(tokens, width) + factor * (
        scaled - centre - normed * along
    )
    input_grad_ref[...] = input_grad.astype(BF16).reshape(images, own_patches, width)

    def unit_total(u):
        here = unit_span(u)
        total = own[here]
        if dps > 1:
            for half in range(2):
                dside_right(u, half).wait_recv()
                dside_left(u, half).wait_recv()
            total = total + dfull_left[here].astype(F32) + dfull_right[here].astype(F32)
        return total

    for u in range(6):
        columns = slice(u * HEAD, (u + 1) * HEAD)
        up_ref[:, columns] = unit_total(u)
        down_ref[columns, :] = unit_total(6 + u).T
        qkv_ref[u] = unit_total(12 + u)
    whole, split = unit_total(18).T, unit_total(19).T
    mid = HEAD // 2

    @pl.when(lax.rem(dp, 2) == 0)
    def _():
        out_ref[0:HEAD, :] = whole
        out_ref[HEAD : HEAD + mid, :] = split[0:mid]

    @pl.when(lax.rem(dp, 2) == 1)
    def _():
        out_ref[0:mid, :] = split[mid:]
        out_ref[mid : HEAD + mid, :] = whole

    last = last_mine[...]
    for k in range(1, teams):
        last_copy(k).wait_recv()
        last = last + last_in[k - 1]
    gains_ref[...] = last[:, 0:HEAD]
    ln_grad_ref[...] = last[0:1, HEAD:]

    def finish(p, carry):
        for way in range(2):
            own_ag(p, way).wait_send()
            fwd_copy(p, way).wait_send()
        return carry

    lax.fori_loop(0, PIECES, finish, 0)

    def finish_unit(u, carry):
        dopp_right(u).wait_send()
        dopp_left(u).wait_send()
        for half in range(2):
            dside_right(u, half).wait_send()
            dside_left(u, half).wait_send()
        return carry

    if dps > 1:
        lax.fori_loop(0, UNITS, finish_unit, 0)
    for p in range(PIECES):
        pl.when(zi != owner_z(p))(lambda: chain_copy(p, True).wait_send())
        if owner_z(p) < 3:
            pl.when((zi >= owner_z(p)) & (zi < 3))(lambda: z_ag(p, True).wait_send())
        if owner_z(p) > 0:
            pl.when((zi <= owner_z(p)) & (zi > 0))(lambda: z_ag(p, False).wait_send())

    for k in range(1, cols):
        gain_copy(k).wait_send()
        stat_copy(k).wait_send()
    for k in range(1, cols):
        norm_copy(k).wait_send()
    if rows > 1:
        core_copy.wait_send()
        row_copy.wait_send()
        for w, ref in enumerate((c_ref, x_ref)):
            for turn in range(3):
                row_gather(w, ref, turn).wait_send()
    for k in range(1, teams):
        last_copy(k).wait_send()


def exchange(w_qkv, w_up, w_out, w_down, qk_gain, features, cotangent, ln_gain):
    dps, rows, cols = lax.axis_size("dp"), lax.axis_size("row"), lax.axis_size("col")
    images, own_patches, width = features.shape
    patches = own_patches * rows
    tokens = images * own_patches
    teams = dps * rows
    dma = pltpu.SemaphoreType.DMA
    whole = max(PIECES * 4 * patches, UNITS * width)
    half = max(PIECES * 2 * patches, UNITS * width // 2)
    units = UNITS * width
    struct = jax.ShapeDtypeStruct
    others, peers = max(teams - 1, 1), cols - 1
    return pl.pallas_call(
        functools.partial(core_kernel, dps, rows, cols),
        out_shape=(
            struct(features.shape, BF16),
            struct(features.shape, BF16),
            struct((1, width), F32),
            struct((8, HEAD), F32),
            struct((6, width, HEAD), F32),
            struct((width, 6 * HEAD), F32),
            struct((3 * HEAD // 2, width), F32),
            struct((6 * HEAD, width), F32),
        ),
        in_specs=[pl.BlockSpec(memory_space=pl.ANY)] * 4 + vmem(4),
        out_specs=tuple(vmem(8)),
        scratch_shapes=[
            pltpu.VMEM((images, patches, width), BF16),
            pltpu.VMEM((images, patches, width), BF16),
            pltpu.VMEM(w_qkv.shape, BF16),
            pltpu.VMEM(w_up.shape, BF16),
            pltpu.VMEM(w_out.shape, BF16),
            pltpu.VMEM(w_down.shape, BF16),
            pltpu.VMEM((tokens, HEAD), F32),
            pltpu.VMEM((tokens, HEAD), F32),
            pltpu.VMEM((SIDE, PIECES, 4, patches, HEAD), BF16),
            pltpu.VMEM((whole, HEAD), BF16),
            pltpu.VMEM((whole, HEAD), BF16),
            pltpu.VMEM((whole, HEAD), BF16),
            pltpu.VMEM((half, HEAD), F32),
            pltpu.VMEM((half, HEAD), F32),
            pltpu.VMEM((whole, HEAD), F32),
            pltpu.VMEM((PIECES * 2 * patches, HEAD), BF16),
            pltpu.VMEM((PIECES * 2 * patches, HEAD), BF16),
            pltpu.VMEM((PIECES * 4 * patches, HEAD), BF16),
            pltpu.VMEM((PIECES * 4 * patches, HEAD), BF16),
            pltpu.VMEM((PIECES * 4 * patches, HEAD), BF16),
            pltpu.VMEM(((PIECES + 3) * 4 * patches, HEAD), BF16),
            pltpu.VMEM((units // 2, HEAD), BF16),
            pltpu.VMEM((units // 2, HEAD), BF16),
            pltpu.VMEM((units, HEAD), BF16),
            pltpu.VMEM((units, HEAD), BF16),
            pltpu.VMEM((width, images * patches), BF16),
            pltpu.VMEM((width, images * patches), BF16),
            pltpu.VMEM((images * patches, width), F32),
            pltpu.VMEM((images * patches, width), F32),
            pltpu.VMEM((2, 2, images, own_patches, width), BF16),
            pltpu.VMEM((2, 2, images, own_patches, width), BF16),
            pltpu.VMEM((2, images, own_patches, width), BF16),
            pltpu.VMEM((2, images, own_patches, width), BF16),
            pltpu.VMEM((8, tokens), F32),
            pltpu.VMEM((peers, 8, tokens), F32),
            pltpu.VMEM((8, HEAD), F32),
            pltpu.VMEM((peers, 8, HEAD), F32),
            pltpu.VMEM((8, tokens), F32),
            pltpu.VMEM((peers, 8, tokens), F32),
            pltpu.VMEM((8, HEAD + width), F32),
            pltpu.VMEM((others, 8, HEAD + width), F32),
            dma((2, PIECES)),
            dma((2, PIECES)),
            dma((2, 2, PIECES)),
            dma((2, 2, PIECES)),
            dma((PIECES,)),
            dma((PIECES + 3,)),
            dma((2, PIECES)),
            dma((2, PIECES)),
            dma((2, PIECES)),
            dma((2, PIECES)),
            dma((2, PIECES)),
            dma((PIECES,)),
            dma((4,)),
            dma((peers,)),
            dma((peers,)),
            dma((2, 3)),
            dma((2, 3)),
            dma((1,)),
            dma((1,)),
            dma((2, UNITS)),
            dma((2, UNITS)),
            dma((2, 2, UNITS)),
            dma((2, 2, UNITS)),
            dma((1,)),
            dma((1,)),
            dma((peers,)),
            dma((peers,)),
            dma((peers,)),
            dma((peers,)),
            dma((others,)),
            dma((others,)),
        ],
        compiler_params=pltpu.CompilerParams(
            collective_id=0, has_side_effects=True, vmem_limit_bytes=VMEM_BYTES
        ),
        name="exchange",
    )(w_qkv, w_up, w_out, w_down, qk_gain, features, cotangent, ln_gain)


def on_device(features, ln_gain, w_qkv, qk_gain, w_up, w_out, w_down, cotangent):
    images, patches, width = features.shape
    head_cols = w_qkv.shape[2]
    qkv_flat = w_qkv.reshape(width, 3 * head_cols)
    output, input_grad, ln_grad, gains, qkv_units, up_grad, out_grad, down_grad = exchange(
        qkv_flat, w_up, w_out, w_down, qk_gain, features, cotangent, ln_gain.reshape(1, width)
    )
    units = qkv_units.reshape(3, 2, width, HEAD)
    whole, split = units[:, 0], units[:, 1]
    mid = HEAD // 2
    qkv_grad = jnp.where(
        lax.rem(lax.axis_index("dp"), 2) == 0,
        jnp.concatenate([whole, split[..., :mid]], -1),
        jnp.concatenate([split[..., mid:], whole], -1),
    )
    qkv_grad = jnp.transpose(qkv_grad, (1, 0, 2))
    return (
        output, input_grad, ln_grad.reshape(width), gains[:2], qkv_grad, up_grad, out_grad, down_grad
    )


def solution(mesh):
    in_specs = (
        P("dp", "row", "col"),
        P("col"),
        P("col", None, "row"),
        P(),
        P("col", "row"),
        P("row", "col"),
        P("row", "col"),
        P("dp", "row", "col"),
    )
    out_specs = (
        P("dp", "row", "col"),
        P("dp", "row", "col"),
        P("col"),
        P(),
        P("col", None, ("row", "dp")),
        P("col", ("row", "dp")),
        P(("row", "dp"), "col"),
        P(("row", "dp"), "col"),
    )
    return jax.shard_map(
        on_device, mesh=mesh, in_specs=in_specs, out_specs=out_specs, check_vma=False
    )
```

```python
import functools

import jax
import jax.numpy as jnp
from jax import lax
from jax.experimental import pallas as pl
from jax.experimental.pallas import tpu as pltpu
from jax.sharding import PartitionSpec as P

EPS = 1e-06
SQRT_HALF = 0.7071067811865476
INV_ROOT = 0.3989422804014327
HEAD = 128
SIDE = 4
PIECES = 9
MESH = pl.DeviceIdType.MESH
VMEM_BYTES = 62 * 1024 * 1024
F32 = jnp.float32
BF16 = jnp.bfloat16


def gelu_both(values):
    cdf = 0.5 * (1.0 + lax.erf(values * SQRT_HALF))
    slope = cdf + values * jnp.exp(-0.5 * values * values) * INV_ROOT
    return values * cdf, slope


def normalize(values):
    average = jnp.mean(values, -1, keepdims=True)
    spread = jnp.mean(values * values, -1, keepdims=True) - average * average
    factor = lax.rsqrt(spread + EPS)
    return ((values - average) * factor, factor)


def norm_back(grad_normed, normed, factor, gain):
    scaled = grad_normed * gain
    centre = jnp.mean(scaled, -1, keepdims=True)
    along = jnp.mean(scaled * normed, -1, keepdims=True)
    return factor * (scaled - centre - normed * along)


def dot(a, b):
    return lax.dot_general(a, b, (((1,), (0,)), ((), ())), preferred_element_type=F32)


def dot_nt(a, b):
    return lax.dot_general(a, b, (((1,), (1,)), ((), ())), preferred_element_type=F32)


def exact_nt(a, b):
    return lax.dot_general(
        a,
        b,
        (((1,), (1,)), ((), ())),
        precision=lax.Precision.HIGHEST,
        preferred_element_type=F32,
    )


def lane_sums(values):
    ones = jnp.ones((8, values.shape[1]), BF16)
    high = values.astype(BF16)
    low = (values - high.astype(F32)).astype(BF16)
    return dot_nt(ones, high) + dot_nt(ones, low)


def greet(peers, meanwhile):
    barrier = pltpu.get_barrier_semaphore()
    for peer in peers:
        pl.semaphore_signal(barrier, inc=1, device_id=peer, device_id_type=MESH)
    result = meanwhile()
    pl.semaphore_wait(barrier, len(peers))
    return result


def remote(src, dst, send, recv, peer):
    return pltpu.make_async_remote_copy(
        src_ref=src,
        dst_ref=dst,
        send_sem=send,
        recv_sem=recv,
        device_id=peer,
        device_id_type=MESH,
    )


def vmem(count):
    return [pl.BlockSpec(memory_space=pltpu.VMEM)] * count


def owner_z(piece):
    return piece if piece < 3 else piece - 3 if piece < 6 else 3


def owner_slot(piece):
    return 0 if piece < 3 else 1 if piece < 6 else piece - 6


UNITS = 20
BEHIND = 2
STEPS = PIECES + 2
SUM_ORDER = (6, 0, 7, 3, 1, 2, 8, 4, 5)
GATHER_ORDER = (
    (0, 3, 1, 4, 2, 5, 6, 7, 8),
    (1, 4, 0, 2, 3, 5, 6, 7, 8),
    (2, 5, 1, 6, 0, 7, 4, 8, 3),
    (6, 7, 8, 2, 5, 1, 0, 4, 3),
)


def core_kernel(
    dps, rows, cols,
    wq_hbm, wup_hbm, wout_hbm, wdown_hbm, gain_ref, feat_ref, cot_ref, ln_ref,
    output_ref, input_grad_ref, ln_grad_ref, gains_ref, qkv_ref, up_ref, out_ref, down_ref,
    x_ref, c_ref, wq_ref, wup_ref, wout_ref, wdown_ref, avg_ref, factor_ref,
    g_ref, opp, right_send, left_send, right_acc, left_acc, own,
    half_left, half_right, full_left, full_right, z_send, z_recv,
    dhalf_left, dhalf_right, dfull_left, dfull_right,
    x_turned, c_turned, out_acc, norm_acc, core_out, core_in, row_out, row_in,
    norm_mine, norm_in,
    gain_mine, gain_in, stat_mine, stat_in, last_mine, last_in, both_mine, both_in,
    s_opp, r_half, s_side, r_full, s_z, r_z, s_own, r_own, s_fwd, r_fwd, s_zag, r_zag,
    s_load, s_norm, r_norm, s_rowg, r_rowg, s_core, r_core,
    s_dopp, r_dhalf, s_dside, r_dfull, s_row, r_row, s_gain, r_gain, s_stat, r_stat, s_last, r_last, s_both, r_both,
):
    dp, row, col = lax.axis_index("dp"), lax.axis_index("row"), lax.axis_index("col")
    xi, zi = col // SIDE, lax.rem(col, SIDE)
    xr, xl, xo = lax.rem(xi + 1, SIDE), lax.rem(xi + 3, SIDE), lax.rem(xi + 2, SIDE)
    right, left = (dp, row, xr * SIDE + zi), (dp, row, xl * SIDE + zi)
    images, patches, width = x_ref.shape
    own_patches = patches // rows
    tokens = images * own_patches
    teams = dps * rows
    full_rows, half_rows = 4 * patches, 2 * patches

    def col_peer(k):
        return (dp, row, lax.rem(col + k, cols))

    mate = (dp, row + 1 - 2 * lax.rem(row, 2), col)
    cross = (dp, lax.rem(row + 2, rows), col)

    def team_peer(k):
        other = lax.rem(dp * rows + row + k, teams)
        return (other // rows, lax.rem(other, rows), col)

    loads = [
        pltpu.make_async_copy(src, dst, s_load.at[i])
        for i, (src, dst) in enumerate(
            ((wdown_hbm, wdown_ref), (wout_hbm, wout_ref), (wup_hbm, wup_ref), (wq_hbm, wq_ref))
        )
    ]
    for load in loads:
        load.start()
    def patch_rows(r):
        return pl.ds(pl.multiple_of(r * own_patches, own_patches), own_patches)

    def row_gather(which, ref, step):
        here = ref.at[:, patch_rows(row if step < 2 else lax.rem(row + 2, rows)), :]
        return remote(
            here, here, s_rowg.at[which, step], r_rowg.at[which, step], cross if step == 1 else mate
        )

    def row_send(which, ref):
        if rows > 1:
            row_gather(which, ref, 1).start()
            row_gather(which, ref, 0).start()

    def row_arrive(which, ref):
        if rows > 1:
            row_gather(which, ref, 1).wait_recv()
            row_gather(which, ref, 2).start()
            row_gather(which, ref, 0).wait_recv()
            row_gather(which, ref, 2).wait_recv()

    inputs_wide = feat_ref[...].astype(F32).reshape(tokens, width)
    which = lax.broadcasted_iota(jnp.int32, (8, tokens), 0)

    def own_sums():
        c_ref[:, patch_rows(row), :] = cot_ref[...]
        sums = jnp.where(
            which == 0, lane_sums(inputs_wide), lane_sums(inputs_wide * inputs_wide)
        )
        norm_mine[...] = sums
        return sums

    norm_sums = greet(
        [col_peer(k) for k in range(1, cols)] + [team_peer(k) for k in range(1, teams)], own_sums
    )
    row_send(0, c_ref)

    def norm_copy(k):
        return remote(
            norm_mine, norm_in.at[k - 1], s_norm.at[k - 1], r_norm.at[k - 1], col_peer(k)
        )

    for k in range(1, cols):
        norm_copy(k).start()
    eye = (
        lax.broadcasted_iota(jnp.int32, (tokens, tokens), 0)
        == lax.broadcasted_iota(jnp.int32, (tokens, tokens), 1)
    ).astype(F32)

    def run_start(block, pair):
        dest = lax.rem(block + pair, 4)
        return (dest * 6 + pair * 2) * HEAD, dest

    def cot_block(block, emit, send=None):
        image, run = block // 2, lax.rem(block, 2)
        triple = pl.ds(pl.multiple_of(run * 3 * HEAD, 3 * HEAD), 3 * HEAD)
        for pair in range(3):
            start, _ = run_start(block, pair)
            hidden = pl.ds(pl.multiple_of(start, 2 * HEAD), 2 * HEAD)
            for im in range(2):
                values = dot_nt(c_ref[im], wdown_ref[hidden, :])
                for j in range(2):
                    emit(3 + 2 * pair + j, 2 + im, values[:, j * HEAD : (j + 1) * HEAD])
            if send is not None:
                for j in range(2):
                    send(3 + 2 * pair + j)
        values = dot_nt(c_ref[image], wout_ref[triple, :])
        for z in range(3):
            emit(z, 3, values[:, z * HEAD : (z + 1) * HEAD])

    def x_block(block, emit):
        image, run = block // 2, lax.rem(block, 2)
        triple = pl.ds(pl.multiple_of(run * 3 * HEAD, 3 * HEAD), 3 * HEAD)
        for part in range(3):
            values = dot(x_ref[image], wq_ref[part, :, triple])
            for z in range(3):
                emit(z, part, values[:, z * HEAD : (z + 1) * HEAD])
        for pair in range(3):
            start, _ = run_start(block, pair)
            hidden = pl.ds(pl.multiple_of(start, 2 * HEAD), 2 * HEAD)
            for im in range(2):
                values = dot(x_ref[im], wup_ref[:, hidden])
                for j in range(2):
                    emit(3 + 2 * pair + j, im, values[:, j * HEAD : (j + 1) * HEAD])

    def at(ref, p, part, parts=1):
        return ref.at[span(p, part, parts)]

    def span(p, part, parts=1):
        return pl.ds(pl.multiple_of(p * full_rows + part * patches, patches), parts * patches)

    def half_span(p):
        return pl.ds(pl.multiple_of(p * half_rows, half_rows), half_rows)

    def opp_right(p):
        return remote(
            at(opp, p, 0, 2), half_left.at[half_span(p)], s_opp.at[0, p], r_half.at[0, p], right
        )

    def opp_left(p):
        return remote(
            at(opp, p, 2, 2), half_right.at[half_span(p)], s_opp.at[1, p], r_half.at[1, p], left
        )

    def side_right(p, half):
        return remote(
            at(right_send, p, 2 * half, 2),
            at(full_left, p, 2 * half, 2),
            s_side.at[0, half, p],
            r_full.at[0, half, p],
            right,
        )

    def side_left(p, half):
        return remote(
            at(left_send, p, 2 * half, 2),
            at(full_right, p, 2 * half, 2),
            s_side.at[1, half, p],
            r_full.at[1, half, p],
            left,
        )

    def emit_opp(p, part, values):
        opp[span(p, part)] = values.astype(BF16)

    def emit_right(p, part, values):
        if part >= 2:
            right_send[span(p, part)] = values.astype(BF16)
        else:
            right_acc[pl.ds(p * half_rows + part * patches, patches)] = values

    def emit_left(p, part, values):
        if part < 2:
            left_send[span(p, part)] = values.astype(BF16)
        else:
            left_acc[pl.ds(p * half_rows + (part - 2) * patches, patches)] = values

    def emit_own(p, part, values):
        own[span(p, part)] = values

    row_arrive(0, c_ref)
    loads[0].wait()
    loads[1].wait()
    cot_block(xo, emit_opp, lambda p: opp_left(p).start())
    cot_block(xr, emit_right, lambda p: side_right(p, 1).start())
    normed_sums = norm_sums
    for k in range(1, cols):
        norm_copy(k).wait_recv()
        normed_sums = normed_sums + norm_in[k - 1]
    normed_sums = normed_sums * (1.0 / (width * cols))
    average = normed_sums[0:1]
    factor = lax.rsqrt(normed_sums[1:2] - average * average + EPS)
    turned = exact_nt(eye, jnp.where(which == 0, average, factor))
    avg_ref[...] = jnp.broadcast_to(turned[:, 0:1], avg_ref.shape)
    factor_ref[...] = jnp.broadcast_to(turned[:, 1:2], factor_ref.shape)
    normed = (inputs_wide - turned[:, 0:1]) * turned[:, 1:2]
    x_ref[:, patch_rows(row), :] = (
        (normed * ln_ref[...]).astype(BF16).reshape(images, own_patches, width)
    )
    row_send(1, x_ref)

    cot_block(xl, emit_left)
    cot_block(xi, emit_own)
    loads[2].wait()
    loads[3].wait()
    row_arrive(1, x_ref)
    x_block(xo, emit_opp)
    for p in range(3):
        opp_left(p).start()
    for i in range(2):
        opp_right(SUM_ORDER[i]).start()
    x_block(xl, emit_left)
    for i in range(2):
        side_left(SUM_ORDER[i], 0).start()
    x_block(xr, emit_right)
    x_block(xi, emit_own)

    for im in range(images):
        here = slice(im * patches, (im + 1) * patches)
        x_turned[:, here] = x_ref[im].T
        c_turned[:, here] = c_ref[im].T

    def pass_on(i):
        p = SUM_ORDER[i]
        if i + 2 < PIECES:
            opp_right(SUM_ORDER[i + 2]).start()
            side_left(SUM_ORDER[i + 2], 0).start()
        if p < 3:
            side_right(p, 1).start()
        opp_left(p).wait_recv()
        left_send[span(p, 2, 2)] = (
            left_acc[half_span(p)] + half_right[half_span(p)].astype(F32)
        ).astype(BF16)
        side_left(p, 1).start()
        opp_right(p).wait_recv()
        right_send[span(p, 0, 2)] = (
            right_acc[half_span(p)] + half_left[half_span(p)].astype(F32)
        ).astype(BF16)
        side_right(p, 0).start()

    z_up, z_down = (dp, row, xi * SIDE + lax.rem(zi + 1, SIDE)), (
        dp, row, xi * SIDE + lax.rem(zi + 3, SIDE)
    )

    def chain_copy(p, up):
        slot = p if up else jnp.where(zi - 1 == owner_z(p), PIECES + owner_slot(p), p)
        return remote(
            at(z_send, p, 0, 4),
            at(z_recv, slot, 0, 4),
            s_z.at[p],
            r_z.at[slot],
            z_up if up else z_down,
        )

    def chain_pass(p, up):
        here = span(p, 0, 4)
        chain_copy(p, True).wait_recv()
        z_send[here] = (own[here] + z_recv[here].astype(F32)).astype(BF16)
        chain_copy(p, up).start()

    def chain_end(p, up):
        here = span(p, 0, 4)
        z_send[here] = own[here].astype(BF16)
        chain_copy(p, up).start()

    def arrived(p, slot):
        for come, place in ((zi > 0, p), (zi < 3, PIECES + slot)):

            @pl.when(come)
            def _():
                there, here = span(place, 0, 4), span(p, 0, 4)
                remote(
                    at(z_send, 0, 0, 4), z_recv.at[there], s_z.at[0], r_z.at[place], z_up
                ).wait_recv()
                own[here] = own[here] + z_recv[there].astype(F32)

    def summed(p, part):
        return own[span(p, part)]

    def own_ag(p, way):
        peer = right if way == 0 else left
        return remote(g_ref.at[xi, p], g_ref.at[xi, p], s_own.at[way, p], r_own.at[way, p], peer)

    def z_ag(p, up):
        way = 0 if up else 1
        peer = z_up if up else z_down
        return remote(g_ref.at[xi, p], g_ref.at[xi, p], s_zag.at[way, p], r_zag.at[p], peer)

    def launch(p):
        for way in range(2):
            own_ag(p, way).start()
        pl.when(zi < 3)(lambda: z_ag(p, True).start())
        pl.when(zi > 0)(lambda: z_ag(p, False).start())

    def hidden_units(p, slot):
        arrived(p, slot)
        for im in range(2):
            value, slope = gelu_both(summed(p, im))
            g_ref[xi, p, im] = value.astype(BF16)
            g_ref[xi, p, 2 + im] = (summed(p, 2 + im) * slope).astype(BF16)
        launch(p)

    scale = HEAD ** (-0.5)

    def attention(p):
        arrived(p, 0)
        query_hat, query_factor = normalize(summed(p, 0))
        key_hat, key_factor = normalize(summed(p, 1))
        query_gain, key_gain = gain_ref[0:1, :], gain_ref[1:2, :]
        query = (query_hat * query_gain).astype(BF16)
        key = (key_hat * key_gain).astype(BF16)
        value = summed(p, 2).astype(BF16)
        grad = summed(p, 3).astype(BF16)
        expo = jnp.exp(dot_nt(query, key) * scale)
        weights = expo / jnp.sum(expo, -1, keepdims=True)
        weights_half = weights.astype(BF16)
        g_ref[xi, p, 0] = dot(weights_half, value).astype(BF16)
        weight_grad = dot_nt(grad, value)
        score_grad = weights * (weight_grad - jnp.sum(weights * weight_grad, -1, keepdims=True))
        score_grad = score_grad.astype(BF16)
        query_grad = dot(score_grad, key) * scale
        key_grad = dot(score_grad.T, query) * scale
        value_grad = dot(weights_half.T, grad)
        gain_mine[0:1, :] = jnp.sum(query_grad * query_hat, 0, keepdims=True)
        gain_mine[1:2, :] = jnp.sum(key_grad * key_hat, 0, keepdims=True)
        g_ref[xi, p, 1] = norm_back(query_grad, query_hat, query_factor, query_gain).astype(BF16)
        g_ref[xi, p, 2] = norm_back(key_grad, key_hat, key_factor, key_gain).astype(BF16)
        g_ref[xi, p, 3] = value_grad.astype(BF16)
        launch(p)

    gain_mine[...] = jnp.zeros_like(gain_mine)

    for turn in range(PIECES + BEHIND + 2):
        if turn < PIECES:
            pass_on(turn)
        i = turn - BEHIND
        if 0 <= i < PIECES:
            p = SUM_ORDER[i]
            for half in range(2):
                side_right(p, half).wait_recv()
                side_left(p, half).wait_recv()
            here = span(p, 0, 4)
            own[here] = own[here] + full_left[here].astype(F32) + full_right[here].astype(F32)
            if owner_z(p) > 0:
                pl.when(zi == 0)(functools.partial(chain_end, p, True))
            if owner_z(p) < 3:
                pl.when(zi == 3)(functools.partial(chain_end, p, False))
        for lag in range(1, 3):
            if 0 <= i - lag < PIECES:
                p = SUM_ORDER[i - lag]
                if owner_z(p) > lag:
                    pl.when(zi == lag)(functools.partial(chain_pass, p, True))
                if owner_z(p) < 3 - lag:
                    pl.when(zi == 3 - lag)(functools.partial(chain_pass, p, False))
        if turn == PIECES:
            pl.when(zi < 3)(lambda: attention(zi))
        if turn in (PIECES, PIECES + 1):
            pl.when(zi == 3)(functools.partial(hidden_units, turn - 3, turn - PIECES))

    pl.when(zi < 3)(lambda: hidden_units(zi + 3, 1))
    pl.when(zi == 3)(lambda: hidden_units(8, 2))

    def gain_copy(k):
        return remote(
            gain_mine, gain_in.at[k - 1], s_gain.at[k - 1], r_gain.at[k - 1], col_peer(k)
        )

    for k in range(1, cols):
        gain_copy(k).start()

    def settle(p, carry):
        opp_right(p).wait_send()
        opp_left(p).wait_send()
        for half in range(2):
            side_right(p, half).wait_send()
            side_left(p, half).wait_send()
        return carry

    lax.fori_loop(0, PIECES, settle, 0)
    out_acc[...] = jnp.zeros_like(out_acc)
    norm_acc[...] = jnp.zeros_like(norm_acc)

    low, high = pl.ds(0, 2), pl.ds(2, 2)

    def fwd_copy(p, way):
        block = xl if way == 0 else xr
        part = low if way == 0 else high
        there = right if way == 0 else left
        return remote(
            g_ref.at[block, p, part],
            g_ref.at[block, p, part],
            s_fwd.at[way, p],
            r_fwd.at[way, p],
            there,
        )

    own_count = jnp.where(zi == 3, 3, 2)

    def piece_at(i):
        piece = i * 0
        for place in range(PIECES):
            named = GATHER_ORDER[0][place]
            for z in range(1, SIDE):
                named = jnp.where(zi == z, GATHER_ORDER[z][place], named)
            piece = jnp.where(i == place, named, piece)
        return piece

    def owner_of(p):
        return jnp.where(p < 3, p, jnp.where(p < 6, p - 3, 3))

    dp_right = (lax.rem(dp + 1, dps), row, col)
    dp_left = (lax.rem(dp + dps - 1, dps), row, col)
    half_width = width // 2

    def unit_span(u, half=None):
        if half is None:
            return pl.ds(pl.multiple_of(u * width, width), width)
        return pl.ds(pl.multiple_of(u * width + half * half_width, half_width), half_width)

    def small_span(u):
        return pl.ds(pl.multiple_of(u * half_width, half_width), half_width)

    def dopp_right(u):
        return remote(
            opp.at[unit_span(u, 0)], dhalf_left.at[small_span(u)],
            s_dopp.at[0, u], r_dhalf.at[0, u], dp_right,
        )

    def dopp_left(u):
        return remote(
            opp.at[unit_span(u, 1)], dhalf_right.at[small_span(u)],
            s_dopp.at[1, u], r_dhalf.at[1, u], dp_left,
        )

    def dside_right(u, half):
        return remote(
            right_send.at[unit_span(u, half)], dfull_left.at[unit_span(u, half)],
            s_dside.at[0, half, u], r_dfull.at[0, half, u], dp_right,
        )

    def dside_left(u, half):
        return remote(
            left_send.at[unit_span(u, half)], dfull_right.at[unit_span(u, half)],
            s_dside.at[1, half, u], r_dfull.at[1, half, u], dp_left,
        )

    def emit_unit(dest, u, values):
        away = lax.rem(dest - dp + 4, 4)

        @pl.when(away == 0)
        def _():
            own[unit_span(u)] = values

        if dps == 1:
            return

        @pl.when(away == 2)
        def _():
            opp[unit_span(u)] = values.astype(BF16)
            dopp_right(u).start()
            dopp_left(u).start()

        @pl.when(away == 1)
        def _():
            right_acc[small_span(u)] = values[:half_width]
            right_send[unit_span(u, 1)] = values[half_width:].astype(BF16)
            dside_right(u, 1).start()

        @pl.when(away == 3)
        def _():
            left_acc[small_span(u)] = values[half_width:]
            left_send[unit_span(u, 0)] = values[:half_width].astype(BF16)
            dside_left(u, 0).start()

    def pass_unit(dest, u):
        if dps == 1:
            return
        away = lax.rem(dest - dp + 4, 4)

        @pl.when(away == 1)
        def _():
            dopp_right(u).wait_recv()
            right_send[unit_span(u, 0)] = (
                right_acc[small_span(u)] + dhalf_left[small_span(u)].astype(F32)
            ).astype(BF16)
            dside_right(u, 0).start()

        @pl.when(away == 3)
        def _():
            dopp_left(u).wait_recv()
            left_send[unit_span(u, 1)] = (
                left_acc[small_span(u)] + dhalf_right[small_span(u)].astype(F32)
            ).astype(BF16)
            dside_left(u, 1).start()

    def hidden_place(block, p):
        pair, second = (p - 3) // 2, lax.rem(p - 3, 2)
        start, dest = run_start(block, pair)
        return pl.multiple_of(start + second * HEAD, HEAD), dest, pair * 2 + second

    def hidden_back(block, p):
        start, dest, u = hidden_place(block, p)
        run = pl.ds(start, HEAD)
        hidden = g_ref[block, p, low].reshape(half_rows, HEAD)
        pre = g_ref[block, p, high].reshape(half_rows, HEAD)
        emit_unit(dest, u, dot(x_turned[...], pre))
        emit_unit(dest, 6 + u, dot(c_turned[...], hidden))
        out_acc[...] += dot(hidden, wdown_ref[run, :])
        norm_acc[...] += dot_nt(pre, wup_ref[:, run])

    def attention_dests(run, z):
        return 2 * run + jnp.where(z == 2, 1, 0), 2 * run + 1, jnp.where(z == 1, 1, 0)

    def attention_back(block, z):
        image, run = block // 2, lax.rem(block, 2)
        head = run * 3 + z
        here = pl.ds(pl.multiple_of(image * patches, patches), patches)
        out_acc[here] += dot(
            g_ref[block, z, 0], wout_ref[pl.ds(pl.multiple_of(head * HEAD, HEAD), HEAD), :]
        )
        columns = pl.ds(pl.multiple_of(head * HEAD, HEAD), HEAD)
        total = norm_acc[here]
        for part in range(3):
            total = total + dot_nt(g_ref[block, z, 1 + part], wq_ref[part, :, columns])
        norm_acc[here] = total

    def attention_weights(run, z):
        dest, second, which = attention_dests(run, z)
        for t in range(4):
            turned = c_turned if t == 3 else x_turned
            part = 0 if t == 3 else t + 1
            values = dot(turned[:, 0:patches], g_ref[run, z, part]) + dot(
                turned[:, patches : 2 * patches], g_ref[run + 2, z, part]
            )
            u = 12 + 2 * t + which
            emit_unit(dest, u, values)

            @pl.when(z == 1)
            def _():
                emit_unit(second, u, values)

    def pass_hidden(block, p):
        _, dest, u = hidden_place(block, p)
        pass_unit(dest, u)
        pass_unit(dest, 6 + u)

    def pass_attention(run, z):
        dest, second, which = attention_dests(run, z)
        for t in range(4):
            u = 12 + 2 * t + which
            pass_unit(dest, u)

            @pl.when(z == 1)
            def _():
                pass_unit(second, u)

    def passes(i):
        def each_pass(k, carry):
            block = lax.rem(xi + k, 4)
            turn = i - 1 - jnp.where(k == 2, 2, 0)
            p = piece_at(turn)
            live = (turn >= 0) & (turn < PIECES)

            @pl.when(live & (p >= 3))
            def _():
                pass_hidden(block, p)

            @pl.when(live & (p < 3) & (k >= 2))
            def _():
                pass_attention(lax.rem(block, 2), p)

            return carry

        lax.fori_loop(0, SIDE, each_pass, 0)

    def step(i, carry):
        ahead = i + 2

        @pl.when((ahead >= own_count) & (ahead < PIECES))
        def _():
            p = piece_at(ahead)
            z_ag(p, True).wait_recv()
            for way in range(2):
                own_ag(p, way).start()
            owner = owner_of(p)
            pl.when((owner < zi) & (zi < 3))(lambda: z_ag(p, True).start())
            pl.when((owner > zi) & (zi > 0))(lambda: z_ag(p, False).start())

        @pl.when(i < PIECES)
        def _():
            p = piece_at(i)
            for way in range(2):
                own_ag(p, way).wait_recv()
                fwd_copy(p, way).start()

        @pl.when((i >= 2) & (i < PIECES + 2))
        def _():
            p = piece_at(i - 2)
            for way in range(2):
                fwd_copy(p, way).wait_recv()

        def each_block(k, carry):
            block = lax.rem(xi + k, 4)
            turn = i - jnp.where(k == 2, 2, 0)
            p = piece_at(turn)
            live = (turn >= 0) & (turn < PIECES)

            @pl.when(live & (p >= 3))
            def _():
                hidden_back(block, p)

            @pl.when(live & (p < 3))
            def _():
                attention_back(block, p)

            @pl.when(live & (p < 3) & (k >= 2))
            def _():
                attention_weights(lax.rem(block, 2), p)

            return carry

        lax.fori_loop(0, SIDE, each_block, 0)

        passes(i)
        return carry

    lax.fori_loop(0, STEPS, step, 0)

    accs = (out_acc, norm_acc)
    parity = lax.rem(row, 2)

    def row_part(acc, r, im):
        start = im * patches + r * own_patches
        return acc[pl.ds(pl.multiple_of(start, own_patches), own_patches)]

    core_copy = remote(core_out, core_in, s_core.at[0], r_core.at[0], mate)
    row_copies = [
        remote(row_out.at[w], row_in.at[w], s_row.at[w], r_row.at[w], cross) for w in range(2)
    ]
    other_high = lax.rem(row // 2 + 1, 2)
    if rows > 1:
        for w, acc in enumerate(accs):
            for im in range(images):
                for j, high_z in enumerate((other_high, row // 2)):
                    core_out[j, w, im] = row_part(acc, high_z * 2 + 1 - parity, im).astype(BF16)
        core_copy.start()

    gain = ln_ref[...]
    stats = jnp.zeros((8, tokens), F32)
    ln_sum = jnp.zeros((1, width), F32)
    for r in range(rows):
        grads = jnp.concatenate([row_part(norm_acc, r, im) for im in range(images)], 0)
        inputs = x_ref[:, pl.ds(r * own_patches, own_patches), :].astype(F32).reshape(tokens, width)
        along = grads * inputs
        stats = jnp.where(which == 2 * r, lane_sums(grads * gain), stats)
        stats = jnp.where(which == 2 * r + 1, lane_sums(along), stats)
        ln_sum = ln_sum + jnp.sum(along, 0, keepdims=True)
    ln_sum = ln_sum / gain
    stat_mine[...] = stats

    def stat_copy(k):
        return remote(
            stat_mine, stat_in.at[k - 1], s_stat.at[k - 1], r_stat.at[k - 1], col_peer(k)
        )

    for k in range(1, cols):
        stat_copy(k).start()
    gains = gain_mine[...]
    for k in range(1, cols):
        gain_copy(k).wait_recv()
        gains = gains + gain_in[k - 1]
    last_mine[...] = gains
    runs = width // HEAD
    for j in range(runs):
        last_mine[2 + j : 3 + j, :] = ln_sum[:, j * HEAD : (j + 1) * HEAD]

    def last_copy(k):
        return remote(
            last_mine, last_in.at[k - 1], s_last.at[k - 1], r_last.at[k - 1], team_peer(k)
        )

    for k in range(1, teams):
        last_copy(k).start()
    if rows > 1:
        core_copy.wait_recv()
        for w in (1, 0):
            for im in range(images):
                row_out[w, im] = (
                    row_part(accs[w], lax.rem(row + 2, rows), im) + core_in[0, w, im].astype(F32)
                ).astype(BF16)
            row_copies[w].start()
    passes(STEPS)
    for k in range(1, cols):
        stat_copy(k).wait_recv()
        stats = stats + stat_in[k - 1]
    both_mine[...] = stats

    def both_copy(k):
        there = (dp, lax.rem(row + k, rows), col)
        return remote(both_mine, both_in.at[k - 1], s_both.at[k - 1], r_both.at[k - 1], there)

    for k in range(1, rows):
        both_copy(k).start()

    def row_total(w, acc):
        parts = []
        for im in range(images):
            total = row_part(acc, row, im)
            if rows > 1:
                total = total + core_in[1, w, im].astype(F32) + row_in[w, im].astype(F32)
            parts.append(total)
        return jnp.concatenate(parts, 0)

    def unit_total(u):
        here = unit_span(u)
        total = own[here]
        if dps > 1:
            for half in range(2):
                dside_right(u, half).wait_recv()
                dside_left(u, half).wait_recv()
            total = total + dfull_left[here].astype(F32) + dfull_right[here].astype(F32)
        return total

    for u in range(6):
        columns = slice(u * HEAD, (u + 1) * HEAD)
        up_ref[:, columns] = unit_total(u)
        down_ref[columns, :] = unit_total(6 + u).T
        qkv_ref[u] = unit_total(12 + u)
    whole, split = unit_total(18).T, unit_total(19).T
    mid = HEAD // 2

    @pl.when(lax.rem(dp, 2) == 0)
    def _():
        out_ref[0:HEAD, :] = whole
        out_ref[HEAD : HEAD + mid, :] = split[0:mid]

    @pl.when(lax.rem(dp, 2) == 1)
    def _():
        out_ref[0:mid, :] = split[mid:]
        out_ref[mid : HEAD + mid, :] = whole

    average, factor = avg_ref[:, 0:1], factor_ref[:, 0:1]
    normed = (inputs_wide - average) * factor
    for k in range(1, rows):
        both_copy(k).wait_recv()
        stats = stats + both_in[k - 1]
    stats = stats * (1.0 / (width * cols))
    centre_row = jnp.sum(jnp.where(which == 2 * row, stats, 0.0), 0, keepdims=True)
    along_row = jnp.sum(jnp.where(which == 2 * row + 1, stats, 0.0), 0, keepdims=True)
    turned = exact_nt(eye, jnp.where(which == 0, centre_row, along_row))
    centre, along = turned[:, 0:1], turned[:, 1:2]
    if rows > 1:
        row_copies[1].wait_recv()
    input_grad = cot_ref[...].astype(F32).reshape(tokens, width) + factor * (
        row_total(1, norm_acc) * gain - centre - normed * along
    )
    input_grad_ref[...] = input_grad.astype(BF16).reshape(images, own_patches, width)
    if rows > 1:
        row_copies[0].wait_recv()
    output_ref[...] = (
        (inputs_wide + row_total(0, out_acc)).astype(BF16).reshape(images, own_patches, width)
    )

    last = last_mine[...]
    for k in range(1, teams):
        last_copy(k).wait_recv()
        last = last + last_in[k - 1]
    gains_ref[...] = last[0:2]
    for j in range(runs):
        ln_grad_ref[j * HEAD : (j + 1) * HEAD] = last[2 + j]

    def finish(p, carry):
        for way in range(2):
            own_ag(p, way).wait_send()
            fwd_copy(p, way).wait_send()
        return carry

    lax.fori_loop(0, PIECES, finish, 0)

    def finish_unit(u, carry):
        dopp_right(u).wait_send()
        dopp_left(u).wait_send()
        for half in range(2):
            dside_right(u, half).wait_send()
            dside_left(u, half).wait_send()
        return carry

    if dps > 1:
        lax.fori_loop(0, UNITS, finish_unit, 0)
    for p in range(PIECES):
        pl.when(zi != owner_z(p))(lambda: chain_copy(p, True).wait_send())
        if owner_z(p) < 3:
            pl.when((zi >= owner_z(p)) & (zi < 3))(lambda: z_ag(p, True).wait_send())
        if owner_z(p) > 0:
            pl.when((zi <= owner_z(p)) & (zi > 0))(lambda: z_ag(p, False).wait_send())

    for k in range(1, cols):
        gain_copy(k).wait_send()
        stat_copy(k).wait_send()
    for k in range(1, cols):
        norm_copy(k).wait_send()
    if rows > 1:
        core_copy.wait_send()
        for w in range(2):
            row_copies[w].wait_send()
        for k in range(1, rows):
            both_copy(k).wait_send()
        for w, ref in enumerate((c_ref, x_ref)):
            for turn in range(3):
                row_gather(w, ref, turn).wait_send()
    for k in range(1, teams):
        last_copy(k).wait_send()


def exchange(w_qkv, w_up, w_out, w_down, qk_gain, features, cotangent, ln_gain):
    dps, rows, cols = lax.axis_size("dp"), lax.axis_size("row"), lax.axis_size("col")
    images, own_patches, width = features.shape
    patches = own_patches * rows
    tokens = images * own_patches
    teams = dps * rows
    dma = pltpu.SemaphoreType.DMA
    whole = max(PIECES * 4 * patches, UNITS * width)
    half = max(PIECES * 2 * patches, UNITS * width // 2)
    units = UNITS * width
    struct = jax.ShapeDtypeStruct
    others, mates, peers = max(teams - 1, 1), max(rows - 1, 1), cols - 1
    return pl.pallas_call(
        functools.partial(core_kernel, dps, rows, cols),
        out_shape=(
            struct(features.shape, BF16),
            struct(features.shape, BF16),
            struct((width,), F32),
            struct((2, HEAD), F32),
            struct((6, width, HEAD), F32),
            struct((width, 6 * HEAD), F32),
            struct((3 * HEAD // 2, width), F32),
            struct((6 * HEAD, width), F32),
        ),
        in_specs=[pl.BlockSpec(memory_space=pl.ANY)] * 4 + vmem(4),
        out_specs=tuple(vmem(8)),
        scratch_shapes=[
            pltpu.VMEM((images, patches, width), BF16),
            pltpu.VMEM((images, patches, width), BF16),
            pltpu.VMEM(w_qkv.shape, BF16),
            pltpu.VMEM(w_up.shape, BF16),
            pltpu.VMEM(w_out.shape, BF16),
            pltpu.VMEM(w_down.shape, BF16),
            pltpu.VMEM((tokens, HEAD), F32),
            pltpu.VMEM((tokens, HEAD), F32),
            pltpu.VMEM((SIDE, PIECES, 4, patches, HEAD), BF16),
            pltpu.VMEM((whole, HEAD), BF16),
            pltpu.VMEM((whole, HEAD), BF16),
            pltpu.VMEM((whole, HEAD), BF16),
            pltpu.VMEM((half, HEAD), F32),
            pltpu.VMEM((half, HEAD), F32),
            pltpu.VMEM((whole, HEAD), F32),
            pltpu.VMEM((PIECES * 2 * patches, HEAD), BF16),
            pltpu.VMEM((PIECES * 2 * patches, HEAD), BF16),
            pltpu.VMEM((PIECES * 4 * patches, HEAD), BF16),
            pltpu.VMEM((PIECES * 4 * patches, HEAD), BF16),
            pltpu.VMEM((PIECES * 4 * patches, HEAD), BF16),
            pltpu.VMEM(((PIECES + 3) * 4 * patches, HEAD), BF16),
            pltpu.VMEM((units // 2, HEAD), BF16),
            pltpu.VMEM((units // 2, HEAD), BF16),
            pltpu.VMEM((units, HEAD), BF16),
            pltpu.VMEM((units, HEAD), BF16),
            pltpu.VMEM((width, images * patches), BF16),
            pltpu.VMEM((width, images * patches), BF16),
            pltpu.VMEM((images * patches, width), F32),
            pltpu.VMEM((images * patches, width), F32),
            pltpu.VMEM((2, 2, images, own_patches, width), BF16),
            pltpu.VMEM((2, 2, images, own_patches, width), BF16),
            pltpu.VMEM((2, images, own_patches, width), BF16),
            pltpu.VMEM((2, images, own_patches, width), BF16),
            pltpu.VMEM((8, tokens), F32),
            pltpu.VMEM((peers, 8, tokens), F32),
            pltpu.VMEM((8, HEAD), F32),
            pltpu.VMEM((peers, 8, HEAD), F32),
            pltpu.VMEM((8, tokens), F32),
            pltpu.VMEM((peers, 8, tokens), F32),
            pltpu.VMEM((8, HEAD), F32),
            pltpu.VMEM((others, 8, HEAD), F32),
            pltpu.VMEM((8, tokens), F32),
            pltpu.VMEM((mates, 8, tokens), F32),
            dma((2, PIECES)),
            dma((2, PIECES)),
            dma((2, 2, PIECES)),
            dma((2, 2, PIECES)),
            dma((PIECES,)),
            dma((PIECES + 3,)),
            dma((2, PIECES)),
            dma((2, PIECES)),
            dma((2, PIECES)),
            dma((2, PIECES)),
            dma((2, PIECES)),
            dma((PIECES,)),
            dma((4,)),
            dma((peers,)),
            dma((peers,)),
            dma((2, 3)),
            dma((2, 3)),
            dma((1,)),
            dma((1,)),
            dma((2, UNITS)),
            dma((2, UNITS)),
            dma((2, 2, UNITS)),
            dma((2, 2, UNITS)),
            dma((2,)),
            dma((2,)),
            dma((peers,)),
            dma((peers,)),
            dma((peers,)),
            dma((peers,)),
            dma((others,)),
            dma((others,)),
            dma((mates,)),
            dma((mates,)),
        ],
        compiler_params=pltpu.CompilerParams(
            collective_id=0, has_side_effects=True, vmem_limit_bytes=VMEM_BYTES
        ),
        name="exchange",
    )(w_qkv, w_up, w_out, w_down, qk_gain, features, cotangent, ln_gain)


def on_device(features, ln_gain, w_qkv, qk_gain, w_up, w_out, w_down, cotangent):
    images, patches, width = features.shape
    output, input_grad, ln_grad, gains, qkv_units, up_grad, out_grad, down_grad = exchange(
        jnp.transpose(w_qkv, (1, 0, 2)), w_up, w_out, w_down, qk_gain, features, cotangent, ln_gain.reshape(1, width)
    )
    units = qkv_units.reshape(3, 2, width, HEAD)
    whole, split = units[:, 0], units[:, 1]
    mid = HEAD // 2
    qkv_grad = jnp.where(
        lax.rem(lax.axis_index("dp"), 2) == 0,
        jnp.concatenate([whole, split[..., :mid]], -1),
        jnp.concatenate([split[..., mid:], whole], -1),
    )
    qkv_grad = jnp.transpose(qkv_grad, (1, 0, 2))
    return (
        output, input_grad, ln_grad, gains, qkv_grad, up_grad, out_grad, down_grad
    )


def solution(mesh):
    in_specs = (
        P("dp", "row", "col"),
        P("col"),
        P("col", None, "row"),
        P(),
        P("col", "row"),
        P("row", "col"),
        P("row", "col"),
        P("dp", "row", "col"),
    )
    out_specs = (
        P("dp", "row", "col"),
        P("dp", "row", "col"),
        P("col"),
        P(),
        P("col", None, ("row", "dp")),
        P("col", ("row", "dp")),
        P(("row", "dp"), "col"),
        P(("row", "dp"), "col"),
    )
    return jax.shard_map(
        on_device, mesh=mesh, in_specs=in_specs, out_specs=out_specs, check_vma=False
    )
```

```python
import functools

import jax
import jax.numpy as jnp
from jax import lax
from jax.experimental import pallas as pl
from jax.experimental.pallas import tpu as pltpu
from jax.sharding import PartitionSpec as P

EPS = 1e-06
SQRT_HALF = 0.7071067811865476
INV_ROOT = 0.3989422804014327
HEAD = 128
SIDE = 4
PIECES = 9
MESH = pl.DeviceIdType.MESH
VMEM_BYTES = 62 * 1024 * 1024
F32 = jnp.float32
BF16 = jnp.bfloat16


def gelu_both(values):
    cdf = 0.5 * (1.0 + lax.erf(values * SQRT_HALF))
    slope = cdf + values * jnp.exp(-0.5 * values * values) * INV_ROOT
    return values * cdf, slope


def normalize(values):
    average = jnp.mean(values, -1, keepdims=True)
    spread = jnp.mean(values * values, -1, keepdims=True) - average * average
    factor = lax.rsqrt(spread + EPS)
    return ((values - average) * factor, factor)


def norm_back(grad_normed, normed, factor, gain):
    scaled = grad_normed * gain
    centre = jnp.mean(scaled, -1, keepdims=True)
    along = jnp.mean(scaled * normed, -1, keepdims=True)
    return factor * (scaled - centre - normed * along)


def dot(a, b):
    return lax.dot_general(a, b, (((1,), (0,)), ((), ())), preferred_element_type=F32)


def dot_nt(a, b):
    return lax.dot_general(a, b, (((1,), (1,)), ((), ())), preferred_element_type=F32)


def exact_nt(a, b):
    return lax.dot_general(
        a,
        b,
        (((1,), (1,)), ((), ())),
        precision=lax.Precision.HIGHEST,
        preferred_element_type=F32,
    )


def lane_sums(values):
    ones = jnp.ones((8, values.shape[1]), BF16)
    high = values.astype(BF16)
    low = (values - high.astype(F32)).astype(BF16)
    return dot_nt(ones, high) + dot_nt(ones, low)


def greet(peers, meanwhile):
    barrier = pltpu.get_barrier_semaphore()
    for peer in peers:
        pl.semaphore_signal(barrier, inc=1, device_id=peer, device_id_type=MESH)
    result = meanwhile()
    pl.semaphore_wait(barrier, len(peers))
    return result


def remote(src, dst, send, recv, peer):
    return pltpu.make_async_remote_copy(
        src_ref=src,
        dst_ref=dst,
        send_sem=send,
        recv_sem=recv,
        device_id=peer,
        device_id_type=MESH,
    )


def vmem(count):
    return [pl.BlockSpec(memory_space=pltpu.VMEM)] * count


def owner_z(piece):
    return piece if piece < 3 else piece - 3 if piece < 6 else 3


def owner_slot(piece):
    return 0 if piece < 3 else 1 if piece < 6 else piece - 6


UNITS = 20
BEHIND = 2
STEPS = PIECES + 2
SUM_ORDER = (6, 0, 7, 3, 1, 2, 8, 4, 5)
GATHER_ORDER = (
    (0, 3, 1, 4, 2, 5, 6, 7, 8),
    (1, 4, 0, 2, 3, 5, 6, 7, 8),
    (2, 5, 1, 6, 0, 7, 4, 8, 3),
    (6, 7, 8, 2, 5, 1, 0, 4, 3),
)


def core_kernel(
    dps, rows, cols,
    wq_hbm, wup_hbm, wout_hbm, wdown_hbm, gain_ref, feat_ref, cot_ref, ln_ref,
    output_ref, input_grad_ref, ln_grad_ref, gains_ref, qkv_ref, up_ref, out_ref, down_ref,
    x_ref, c_ref, wq_ref, wup_ref, wout_ref, wdown_ref, avg_ref, factor_ref,
    g_ref, opp, right_send, left_send, right_acc, left_acc, own,
    half_left, half_right, full_left, full_right, z_send, z_recv,
    dhalf_left, dhalf_right, dfull_left, dfull_right,
    x_turned, c_turned, out_acc, norm_acc, core_out, core_in, row_out, row_in,
    norm_mine, norm_in,
    gain_mine, gain_in, stat_mine, stat_in, last_mine, last_in, both_mine, both_in,
    s_opp, r_half, s_side, r_full, s_z, r_z, s_own, r_own, s_fwd, r_fwd, s_zag, r_zag,
    s_load, s_norm, r_norm, s_rowg, r_rowg, s_core, r_core,
    s_dopp, r_dhalf, s_dside, r_dfull, s_row, r_row, s_gain, r_gain, s_stat, r_stat, s_last, r_last, s_both, r_both,
):
    dp, row, col = lax.axis_index("dp"), lax.axis_index("row"), lax.axis_index("col")
    xi, zi = col // SIDE, lax.rem(col, SIDE)
    xr, xl, xo = lax.rem(xi + 1, SIDE), lax.rem(xi + 3, SIDE), lax.rem(xi + 2, SIDE)
    right, left = (dp, row, xr * SIDE + zi), (dp, row, xl * SIDE + zi)
    images, patches, width = x_ref.shape
    own_patches = patches // rows
    tokens = images * own_patches
    teams = dps * rows
    full_rows, half_rows = 4 * patches, 2 * patches

    def col_peer(k):
        return (dp, row, lax.rem(col + k, cols))

    mate = (dp, row + 1 - 2 * lax.rem(row, 2), col)
    cross = (dp, lax.rem(row + 2, rows), col)

    def team_peer(k):
        other = lax.rem(dp * rows + row + k, teams)
        return (other // rows, lax.rem(other, rows), col)

    loads = [
        pltpu.make_async_copy(src, dst, s_load.at[i])
        for i, (src, dst) in enumerate(
            ((wdown_hbm, wdown_ref), (wout_hbm, wout_ref), (wup_hbm, wup_ref), (wq_hbm, wq_ref))
        )
    ]
    for load in loads:
        load.start()
    def patch_rows(r):
        return pl.ds(pl.multiple_of(r * own_patches, own_patches), own_patches)

    def row_gather(which, ref, step):
        here = ref.at[:, patch_rows(row if step < 2 else lax.rem(row + 2, rows)), :]
        return remote(
            here, here, s_rowg.at[which, step], r_rowg.at[which, step], cross if step == 1 else mate
        )

    def row_send(which, ref):
        if rows > 1:
            row_gather(which, ref, 1).start()
            row_gather(which, ref, 0).start()

    def row_arrive(which, ref):
        if rows > 1:
            row_gather(which, ref, 1).wait_recv()
            row_gather(which, ref, 2).start()
            row_gather(which, ref, 0).wait_recv()
            row_gather(which, ref, 2).wait_recv()

    inputs_wide = feat_ref[...].astype(F32).reshape(tokens, width)
    which = lax.broadcasted_iota(jnp.int32, (8, tokens), 0)

    def own_sums():
        c_ref[:, patch_rows(row), :] = cot_ref[...]
        sums = jnp.where(
            which == 0, lane_sums(inputs_wide), lane_sums(inputs_wide * inputs_wide)
        )
        norm_mine[...] = sums
        return sums

    norm_sums = greet(
        [col_peer(k) for k in range(1, cols)] + [team_peer(k) for k in range(1, teams)], own_sums
    )
    row_send(0, c_ref)

    def norm_copy(k):
        return remote(
            norm_mine, norm_in.at[k - 1], s_norm.at[k - 1], r_norm.at[k - 1], col_peer(k)
        )

    for k in range(1, cols):
        norm_copy(k).start()
    eye = (
        lax.broadcasted_iota(jnp.int32, (tokens, tokens), 0)
        == lax.broadcasted_iota(jnp.int32, (tokens, tokens), 1)
    ).astype(F32)

    def run_start(block, pair):
        dest = lax.rem(block + pair, 4)
        return (dest * 6 + pair * 2) * HEAD, dest

    def cot_block(block, emit, send=None):
        image, run = block // 2, lax.rem(block, 2)
        triple = pl.ds(pl.multiple_of(run * 3 * HEAD, 3 * HEAD), 3 * HEAD)
        for pair in range(3):
            start, _ = run_start(block, pair)
            hidden = pl.ds(pl.multiple_of(start, 2 * HEAD), 2 * HEAD)
            for im in range(2):
                values = dot_nt(c_ref[im], wdown_ref[hidden, :])
                for j in range(2):
                    emit(3 + 2 * pair + j, 2 + im, values[:, j * HEAD : (j + 1) * HEAD])
            if send is not None:
                for j in range(2):
                    send(3 + 2 * pair + j)
        values = dot_nt(c_ref[image], wout_ref[triple, :])
        for z in range(3):
            emit(z, 3, values[:, z * HEAD : (z + 1) * HEAD])

    def x_block(block, emit):
        image, run = block // 2, lax.rem(block, 2)
        triple = pl.ds(pl.multiple_of(run * 3 * HEAD, 3 * HEAD), 3 * HEAD)
        for part in range(3):
            values = dot(x_ref[image], wq_ref[part, :, triple])
            for z in range(3):
                emit(z, part, values[:, z * HEAD : (z + 1) * HEAD])
        for pair in range(3):
            start, _ = run_start(block, pair)
            hidden = pl.ds(pl.multiple_of(start, 2 * HEAD), 2 * HEAD)
            for im in range(2):
                values = dot(x_ref[im], wup_ref[:, hidden])
                for j in range(2):
                    emit(3 + 2 * pair + j, im, values[:, j * HEAD : (j + 1) * HEAD])

    def at(ref, p, part, parts=1):
        return ref.at[span(p, part, parts)]

    def span(p, part, parts=1):
        return pl.ds(pl.multiple_of(p * full_rows + part * patches, patches), parts * patches)

    def half_span(p):
        return pl.ds(pl.multiple_of(p * half_rows, half_rows), half_rows)

    def opp_right(p):
        return remote(
            at(opp, p, 0, 2), half_left.at[half_span(p)], s_opp.at[0, p], r_half.at[0, p], right
        )

    def opp_left(p):
        return remote(
            at(opp, p, 2, 2), half_right.at[half_span(p)], s_opp.at[1, p], r_half.at[1, p], left
        )

    def side_right(p, half):
        return remote(
            at(right_send, p, 2 * half, 2),
            at(full_left, p, 2 * half, 2),
            s_side.at[0, half, p],
            r_full.at[0, half, p],
            right,
        )

    def side_left(p, half):
        return remote(
            at(left_send, p, 2 * half, 2),
            at(full_right, p, 2 * half, 2),
            s_side.at[1, half, p],
            r_full.at[1, half, p],
            left,
        )

    def emit_opp(p, part, values):
        opp[span(p, part)] = values.astype(BF16)

    def emit_right(p, part, values):
        if part >= 2:
            right_send[span(p, part)] = values.astype(BF16)
        else:
            right_acc[pl.ds(p * half_rows + part * patches, patches)] = values

    def emit_left(p, part, values):
        if part < 2:
            left_send[span(p, part)] = values.astype(BF16)
        else:
            left_acc[pl.ds(p * half_rows + (part - 2) * patches, patches)] = values

    def emit_own(p, part, values):
        own[span(p, part)] = values

    row_arrive(0, c_ref)
    loads[0].wait()
    loads[1].wait()
    cot_block(xo, emit_opp, lambda p: opp_left(p).start())
    cot_block(xr, emit_right, lambda p: side_right(p, 1).start())
    normed_sums = norm_sums
    for k in range(1, cols):
        norm_copy(k).wait_recv()
        normed_sums = normed_sums + norm_in[k - 1]
    normed_sums = normed_sums * (1.0 / (width * cols))
    average = normed_sums[0:1]
    factor = lax.rsqrt(normed_sums[1:2] - average * average + EPS)
    turned = exact_nt(eye, jnp.where(which == 0, average, factor))
    avg_ref[...] = jnp.broadcast_to(turned[:, 0:1], avg_ref.shape)
    factor_ref[...] = jnp.broadcast_to(turned[:, 1:2], factor_ref.shape)
    normed = (inputs_wide - turned[:, 0:1]) * turned[:, 1:2]
    x_ref[:, patch_rows(row), :] = (
        (normed * ln_ref[...]).astype(BF16).reshape(images, own_patches, width)
    )
    row_send(1, x_ref)

    cot_block(xl, emit_left)
    cot_block(xi, emit_own)
    loads[2].wait()
    loads[3].wait()
    row_arrive(1, x_ref)
    x_block(xo, emit_opp)
    for p in range(3):
        opp_left(p).start()
    for i in range(2):
        opp_right(SUM_ORDER[i]).start()
    x_block(xl, emit_left)
    for i in range(2):
        side_left(SUM_ORDER[i], 0).start()
    x_block(xr, emit_right)
    x_block(xi, emit_own)

    for im in range(images):
        here = slice(im * patches, (im + 1) * patches)
        x_turned[:, here] = x_ref[im].T
        c_turned[:, here] = c_ref[im].T

    def pass_on(i):
        p = SUM_ORDER[i]
        if i + 2 < PIECES:
            opp_right(SUM_ORDER[i + 2]).start()
            side_left(SUM_ORDER[i + 2], 0).start()
        if p < 3:
            side_right(p, 1).start()
        opp_left(p).wait_recv()
        left_send[span(p, 2, 2)] = (
            left_acc[half_span(p)] + half_right[half_span(p)].astype(F32)
        ).astype(BF16)
        side_left(p, 1).start()
        opp_right(p).wait_recv()
        right_send[span(p, 0, 2)] = (
            right_acc[half_span(p)] + half_left[half_span(p)].astype(F32)
        ).astype(BF16)
        side_right(p, 0).start()

    z_up, z_down = (dp, row, xi * SIDE + lax.rem(zi + 1, SIDE)), (
        dp, row, xi * SIDE + lax.rem(zi + 3, SIDE)
    )

    def chain_copy(p, up):
        slot = p if up else jnp.where(zi - 1 == owner_z(p), PIECES + owner_slot(p), p)
        return remote(
            at(z_send, p, 0, 4),
            at(z_recv, slot, 0, 4),
            s_z.at[p],
            r_z.at[slot],
            z_up if up else z_down,
        )

    def chain_pass(p, up):
        here = span(p, 0, 4)
        chain_copy(p, True).wait_recv()
        z_send[here] = (own[here] + z_recv[here].astype(F32)).astype(BF16)
        chain_copy(p, up).start()

    def chain_end(p, up):
        here = span(p, 0, 4)
        z_send[here] = own[here].astype(BF16)
        chain_copy(p, up).start()

    def arrived(p, slot):
        for come, place in ((zi > 0, p), (zi < 3, PIECES + slot)):

            @pl.when(come)
            def _():
                there, here = span(place, 0, 4), span(p, 0, 4)
                remote(
                    at(z_send, 0, 0, 4), z_recv.at[there], s_z.at[0], r_z.at[place], z_up
                ).wait_recv()
                own[here] = own[here] + z_recv[there].astype(F32)

    def summed(p, part):
        return own[span(p, part)]

    def own_ag(p, way):
        peer = right if way == 0 else left
        return remote(g_ref.at[xi, p], g_ref.at[xi, p], s_own.at[way, p], r_own.at[way, p], peer)

    def z_ag(p, up):
        way = 0 if up else 1
        peer = z_up if up else z_down
        return remote(g_ref.at[xi, p], g_ref.at[xi, p], s_zag.at[way, p], r_zag.at[p], peer)

    def launch(p):
        for way in range(2):
            own_ag(p, way).start()
        pl.when(zi < 3)(lambda: z_ag(p, True).start())
        pl.when(zi > 0)(lambda: z_ag(p, False).start())

    def hidden_units(p, slot):
        arrived(p, slot)
        for im in range(2):
            value, slope = gelu_both(summed(p, im))
            g_ref[xi, p, im] = value.astype(BF16)
            g_ref[xi, p, 2 + im] = (summed(p, 2 + im) * slope).astype(BF16)
        launch(p)

    scale = HEAD ** (-0.5)

    def attention(p):
        arrived(p, 0)
        query_hat, query_factor = normalize(summed(p, 0))
        key_hat, key_factor = normalize(summed(p, 1))
        query_gain, key_gain = gain_ref[0:1, :], gain_ref[1:2, :]
        query = (query_hat * query_gain).astype(BF16)
        key = (key_hat * key_gain).astype(BF16)
        value = summed(p, 2).astype(BF16)
        grad = summed(p, 3).astype(BF16)
        expo = jnp.exp(dot_nt(query, key) * scale)
        weights = expo / jnp.sum(expo, -1, keepdims=True)
        weights_half = weights.astype(BF16)
        g_ref[xi, p, 0] = dot(weights_half, value).astype(BF16)
        weight_grad = dot_nt(grad, value)
        score_grad = weights * (weight_grad - jnp.sum(weights * weight_grad, -1, keepdims=True))
        score_grad = score_grad.astype(BF16)
        query_grad = dot(score_grad, key) * scale
        key_grad = dot(score_grad.T, query) * scale
        value_grad = dot(weights_half.T, grad)
        gain_mine[0:1, :] = jnp.sum(query_grad * query_hat, 0, keepdims=True)
        gain_mine[1:2, :] = jnp.sum(key_grad * key_hat, 0, keepdims=True)
        g_ref[xi, p, 1] = norm_back(query_grad, query_hat, query_factor, query_gain).astype(BF16)
        g_ref[xi, p, 2] = norm_back(key_grad, key_hat, key_factor, key_gain).astype(BF16)
        g_ref[xi, p, 3] = value_grad.astype(BF16)
        launch(p)

    gain_mine[...] = jnp.zeros_like(gain_mine)

    for turn in range(PIECES + BEHIND + 2):
        if turn < PIECES:
            pass_on(turn)
        i = turn - BEHIND
        if 0 <= i < PIECES:
            p = SUM_ORDER[i]
            for half in range(2):
                side_right(p, half).wait_recv()
                side_left(p, half).wait_recv()
            here = span(p, 0, 4)
            own[here] = own[here] + full_left[here].astype(F32) + full_right[here].astype(F32)
            if owner_z(p) > 0:
                pl.when(zi == 0)(functools.partial(chain_end, p, True))
            if owner_z(p) < 3:
                pl.when(zi == 3)(functools.partial(chain_end, p, False))
        for lag in range(1, 3):
            if 0 <= i - lag < PIECES:
                p = SUM_ORDER[i - lag]
                if owner_z(p) > lag:
                    pl.when(zi == lag)(functools.partial(chain_pass, p, True))
                if owner_z(p) < 3 - lag:
                    pl.when(zi == 3 - lag)(functools.partial(chain_pass, p, False))
        if turn == PIECES:
            pl.when(zi < 3)(lambda: attention(zi))
        if turn in (PIECES, PIECES + 1):
            pl.when(zi == 3)(functools.partial(hidden_units, turn - 3, turn - PIECES))

    pl.when(zi < 3)(lambda: hidden_units(zi + 3, 1))
    pl.when(zi == 3)(lambda: hidden_units(8, 2))

    def gain_copy(k):
        return remote(
            gain_mine, gain_in.at[k - 1], s_gain.at[k - 1], r_gain.at[k - 1], col_peer(k)
        )

    for k in range(1, cols):
        gain_copy(k).start()

    def settle(p, carry):
        opp_right(p).wait_send()
        opp_left(p).wait_send()
        for half in range(2):
            side_right(p, half).wait_send()
            side_left(p, half).wait_send()
        return carry

    lax.fori_loop(0, PIECES, settle, 0)
    for k in range(1, cols):
        norm_copy(k).wait_send()
    if rows > 1:
        for w, ref in enumerate((c_ref, x_ref)):
            for turn in range(3):
                row_gather(w, ref, turn).wait_send()
    out_acc[...] = jnp.zeros_like(out_acc)
    norm_acc[...] = jnp.zeros_like(norm_acc)

    low, high = pl.ds(0, 2), pl.ds(2, 2)

    def fwd_copy(p, way):
        block = xl if way == 0 else xr
        part = low if way == 0 else high
        there = right if way == 0 else left
        return remote(
            g_ref.at[block, p, part],
            g_ref.at[block, p, part],
            s_fwd.at[way, p],
            r_fwd.at[way, p],
            there,
        )

    own_count = jnp.where(zi == 3, 3, 2)

    def piece_at(i):
        piece = i * 0
        for place in range(PIECES):
            named = GATHER_ORDER[0][place]
            for z in range(1, SIDE):
                named = jnp.where(zi == z, GATHER_ORDER[z][place], named)
            piece = jnp.where(i == place, named, piece)
        return piece

    def owner_of(p):
        return jnp.where(p < 3, p, jnp.where(p < 6, p - 3, 3))

    dp_right = (lax.rem(dp + 1, dps), row, col)
    dp_left = (lax.rem(dp + dps - 1, dps), row, col)
    half_width = width // 2

    def unit_span(u, half=None):
        if half is None:
            return pl.ds(pl.multiple_of(u * width, width), width)
        return pl.ds(pl.multiple_of(u * width + half * half_width, half_width), half_width)

    def small_span(u):
        return pl.ds(pl.multiple_of(u * half_width, half_width), half_width)

    all_halves = pl.ds(0, UNITS * half_width)

    def dopp_right(u):
        return remote(
            opp.at[unit_span(u, 0)], dhalf_left.at[small_span(u)],
            s_dopp.at[0], r_dhalf.at[0, u], dp_right,
        )

    def dopp_left(u):
        return remote(
            opp.at[unit_span(u, 1)], dhalf_right.at[small_span(u)],
            s_dopp.at[1], r_dhalf.at[1, u], dp_left,
        )

    def dside_right(u, half):
        return remote(
            right_send.at[unit_span(u, half)], dfull_left.at[unit_span(u, half)],
            s_dside.at[0, half], r_dfull.at[0, half, u], dp_right,
        )

    def dside_left(u, half):
        return remote(
            left_send.at[unit_span(u, half)], dfull_right.at[unit_span(u, half)],
            s_dside.at[1, half], r_dfull.at[1, half, u], dp_left,
        )

    def emit_unit(dest, u, values):
        away = lax.rem(dest - dp + 4, 4)

        @pl.when(away == 0)
        def _():
            own[unit_span(u)] = values

        if dps == 1:
            return

        @pl.when(away == 2)
        def _():
            opp[unit_span(u)] = values.astype(BF16)
            dopp_right(u).start()
            dopp_left(u).start()

        @pl.when(away == 1)
        def _():
            right_acc[small_span(u)] = values[:half_width]
            right_send[unit_span(u, 1)] = values[half_width:].astype(BF16)
            dside_right(u, 1).start()

        @pl.when(away == 3)
        def _():
            left_acc[small_span(u)] = values[half_width:]
            left_send[unit_span(u, 0)] = values[:half_width].astype(BF16)
            dside_left(u, 0).start()

    def pass_unit(dest, u):
        if dps == 1:
            return
        away = lax.rem(dest - dp + 4, 4)

        @pl.when(away == 1)
        def _():
            dopp_right(u).wait_recv()
            right_send[unit_span(u, 0)] = (
                right_acc[small_span(u)] + dhalf_left[small_span(u)].astype(F32)
            ).astype(BF16)
            dside_right(u, 0).start()

        @pl.when(away == 3)
        def _():
            dopp_left(u).wait_recv()
            left_send[unit_span(u, 1)] = (
                left_acc[small_span(u)] + dhalf_right[small_span(u)].astype(F32)
            ).astype(BF16)
            dside_left(u, 1).start()

    def hidden_place(block, p):
        pair, second = (p - 3) // 2, lax.rem(p - 3, 2)
        start, dest = run_start(block, pair)
        return pl.multiple_of(start + second * HEAD, HEAD), dest, pair * 2 + second

    def hidden_back(block, p):
        start, dest, u = hidden_place(block, p)
        run = pl.ds(start, HEAD)
        hidden = g_ref[block, p, low].reshape(half_rows, HEAD)
        pre = g_ref[block, p, high].reshape(half_rows, HEAD)
        emit_unit(dest, u, dot(x_turned[...], pre))
        emit_unit(dest, 6 + u, dot(c_turned[...], hidden))
        out_acc[...] += dot(hidden, wdown_ref[run, :])
        norm_acc[...] += dot_nt(pre, wup_ref[:, run])

    def attention_dests(run, z):
        return 2 * run + jnp.where(z == 2, 1, 0), 2 * run + 1, jnp.where(z == 1, 1, 0)

    def attention_back(block, z):
        image, run = block // 2, lax.rem(block, 2)
        head = run * 3 + z
        here = pl.ds(pl.multiple_of(image * patches, patches), patches)
        out_acc[here] += dot(
            g_ref[block, z, 0], wout_ref[pl.ds(pl.multiple_of(head * HEAD, HEAD), HEAD), :]
        )
        columns = pl.ds(pl.multiple_of(head * HEAD, HEAD), HEAD)
        total = norm_acc[here]
        for part in range(3):
            total = total + dot_nt(g_ref[block, z, 1 + part], wq_ref[part, :, columns])
        norm_acc[here] = total

    def attention_weights(run, z):
        dest, second, which = attention_dests(run, z)
        for t in range(4):
            turned = c_turned if t == 3 else x_turned
            part = 0 if t == 3 else t + 1
            values = dot(turned[:, 0:patches], g_ref[run, z, part]) + dot(
                turned[:, patches : 2 * patches], g_ref[run + 2, z, part]
            )
            u = 12 + 2 * t + which
            emit_unit(dest, u, values)

            @pl.when(z == 1)
            def _():
                emit_unit(second, u, values)

    def pass_hidden(block, p):
        _, dest, u = hidden_place(block, p)
        pass_unit(dest, u)
        pass_unit(dest, 6 + u)

    def pass_attention(run, z):
        dest, second, which = attention_dests(run, z)
        for t in range(4):
            u = 12 + 2 * t + which
            pass_unit(dest, u)

            @pl.when(z == 1)
            def _():
                pass_unit(second, u)

    def passes(i):
        def each_pass(k, carry):
            block = lax.rem(xi + k, 4)
            turn = i - 2 - jnp.where(k == 2, 2, 0)
            p = piece_at(turn)
            live = (turn >= 0) & (turn < PIECES)

            @pl.when(live & (p >= 3))
            def _():
                pass_hidden(block, p)

            @pl.when(live & (p < 3) & (k >= 2))
            def _():
                pass_attention(lax.rem(block, 2), p)

            return carry

        lax.fori_loop(0, SIDE, each_pass, 0)

    def gathered(p):
        for way in range(2):
            own_ag(p, way).wait_send()
            fwd_copy(p, way).wait_send()

    def step(i, carry):
        ahead = i + 2

        @pl.when((ahead >= own_count) & (ahead < PIECES))
        def _():
            p = piece_at(ahead)
            z_ag(p, True).wait_recv()
            for way in range(2):
                own_ag(p, way).start()
            owner = owner_of(p)
            pl.when((owner < zi) & (zi < 3))(lambda: z_ag(p, True).start())
            pl.when((owner > zi) & (zi > 0))(lambda: z_ag(p, False).start())

        @pl.when(i < PIECES)
        def _():
            p = piece_at(i)
            for way in range(2):
                own_ag(p, way).wait_recv()
                fwd_copy(p, way).start()

        @pl.when((i >= 2) & (i < PIECES + 2))
        def _():
            p = piece_at(i - 2)
            for way in range(2):
                fwd_copy(p, way).wait_recv()

        def each_block(k, carry):
            block = lax.rem(xi + k, 4)
            turn = i - jnp.where(k == 2, 2, 0)
            p = piece_at(turn)
            live = (turn >= 0) & (turn < PIECES)

            @pl.when(live & (p >= 3))
            def _():
                hidden_back(block, p)

            @pl.when(live & (p < 3))
            def _():
                attention_back(block, p)

            @pl.when(live & (p < 3) & (k >= 2))
            def _():
                attention_weights(lax.rem(block, 2), p)

            return carry

        lax.fori_loop(0, SIDE, each_block, 0)
        passes(i)

        @pl.when((i >= 3) & (i < PIECES + 2))
        def _():
            gathered(piece_at(i - 3))

        @pl.when(i == PIECES - 3)
        def _():
            gains = gain_mine[...]
            for k in range(1, cols):
                gain_copy(k).wait()
                gains = gains + gain_in[k - 1]
            last_mine[...] = gains

        return carry

    lax.fori_loop(0, STEPS, step, 0)

    accs = (out_acc, norm_acc)
    parity = lax.rem(row, 2)

    def row_part(acc, r, im):
        start = im * patches + r * own_patches
        return acc[pl.ds(pl.multiple_of(start, own_patches), own_patches)]

    core_copy = remote(core_out, core_in, s_core.at[0], r_core.at[0], mate)
    row_copies = [
        remote(row_out.at[w], row_in.at[w], s_row.at[w], r_row.at[w], cross) for w in range(2)
    ]
    other_high = lax.rem(row // 2 + 1, 2)
    if rows > 1:
        for w, acc in enumerate(accs):
            for im in range(images):
                for j, high_z in enumerate((other_high, row // 2)):
                    core_out[j, w, im] = row_part(acc, high_z * 2 + 1 - parity, im).astype(BF16)
        core_copy.start()

    gain = ln_ref[...]
    stats = jnp.zeros((8, tokens), F32)
    ln_sum = jnp.zeros((1, width), F32)
    for r in range(rows):
        grads = jnp.concatenate([row_part(norm_acc, r, im) for im in range(images)], 0)
        inputs = x_ref[:, pl.ds(r * own_patches, own_patches), :].astype(F32).reshape(tokens, width)
        along = grads * inputs
        stats = jnp.where(which == 2 * r, lane_sums(grads * gain), stats)
        stats = jnp.where(which == 2 * r + 1, lane_sums(along), stats)
        ln_sum = ln_sum + jnp.sum(along, 0, keepdims=True)
    ln_sum = ln_sum / gain
    stat_mine[...] = stats

    def stat_copy(k):
        return remote(
            stat_mine, stat_in.at[k - 1], s_stat.at[k - 1], r_stat.at[k - 1], col_peer(k)
        )

    for k in range(1, cols):
        stat_copy(k).start()
    runs = width // HEAD
    for j in range(runs):
        last_mine[2 + j : 3 + j, :] = ln_sum[:, j * HEAD : (j + 1) * HEAD]

    def last_copy(k):
        return remote(
            last_mine, last_in.at[k - 1], s_last.at[k - 1], r_last.at[k - 1], team_peer(k)
        )

    if rows > 1:
        core_copy.wait_recv()
        for w in (1, 0):
            for im in range(images):
                row_out[w, im] = (
                    row_part(accs[w], lax.rem(row + 2, rows), im) + core_in[0, w, im].astype(F32)
                ).astype(BF16)
            row_copies[w].start()
    for k in range(1, teams):
        last_copy(k).start()

    def last_passes(i, carry):
        passes(i)
        return carry

    lax.fori_loop(STEPS, STEPS + 2, last_passes, 0)
    for k in range(1, cols):
        stat_copy(k).wait_recv()
        stats = stats + stat_in[k - 1]
    both_mine[...] = stats

    def both_copy(k):
        there = (dp, lax.rem(row + k, rows), col)
        return remote(both_mine, both_in.at[k - 1], s_both.at[k - 1], r_both.at[k - 1], there)

    for k in range(1, rows):
        both_copy(k).start()

    def row_total(w, acc):
        parts = []
        for im in range(images):
            total = row_part(acc, row, im)
            if rows > 1:
                total = total + core_in[1, w, im].astype(F32) + row_in[w, im].astype(F32)
            parts.append(total)
        return jnp.concatenate(parts, 0)

    def unit_total(u):
        here = unit_span(u)
        total = own[here]
        if dps > 1:
            for half in range(2):
                dside_right(u, half).wait_recv()
                dside_left(u, half).wait_recv()
            total = total + dfull_left[here].astype(F32) + dfull_right[here].astype(F32)
        return total

    for u in range(6):
        columns = slice(u * HEAD, (u + 1) * HEAD)
        up_ref[:, columns] = unit_total(u)
        down_ref[columns, :] = unit_total(6 + u).T
        qkv_ref[u] = unit_total(12 + u)
    whole, split = unit_total(18).T, unit_total(19).T
    mid = HEAD // 2

    @pl.when(lax.rem(dp, 2) == 0)
    def _():
        out_ref[0:HEAD, :] = whole
        out_ref[HEAD : HEAD + mid, :] = split[0:mid]

    @pl.when(lax.rem(dp, 2) == 1)
    def _():
        out_ref[0:mid, :] = split[mid:]
        out_ref[mid : HEAD + mid, :] = whole

    average, factor = avg_ref[:, 0:1], factor_ref[:, 0:1]
    normed = (inputs_wide - average) * factor
    for k in range(1, rows):
        both_copy(k).wait_recv()
        stats = stats + both_in[k - 1]
    stats = stats * (1.0 / (width * cols))
    centre_row = jnp.sum(jnp.where(which == 2 * row, stats, 0.0), 0, keepdims=True)
    along_row = jnp.sum(jnp.where(which == 2 * row + 1, stats, 0.0), 0, keepdims=True)
    turned = exact_nt(eye, jnp.where(which == 0, centre_row, along_row))
    centre, along = turned[:, 0:1], turned[:, 1:2]
    if rows > 1:
        row_copies[1].wait_recv()
    input_grad = cot_ref[...].astype(F32).reshape(tokens, width) + factor * (
        row_total(1, norm_acc) * gain - centre - normed * along
    )
    input_grad_ref[...] = input_grad.astype(BF16).reshape(images, own_patches, width)
    if rows > 1:
        row_copies[0].wait_recv()
    output_ref[...] = (
        (inputs_wide + row_total(0, out_acc)).astype(BF16).reshape(images, own_patches, width)
    )

    last = last_mine[...]
    for k in range(1, teams):
        last_copy(k).wait_recv()
        last = last + last_in[k - 1]
    gains_ref[...] = last[0:2]
    for j in range(runs):
        ln_grad_ref[j * HEAD : (j + 1) * HEAD] = last[2 + j]

    gathered(piece_at(PIECES - 1))
    if dps > 1:
        for way, (send, there) in enumerate(((right_send, dp_right), (left_send, dp_left))):
            remote(
                opp.at[all_halves], dhalf_left, s_dopp.at[way], r_dhalf.at[way, 0], there
            ).wait_send()
            for half in range(2):
                remote(
                    send.at[all_halves], dhalf_left, s_dside.at[way, half], r_dhalf.at[way, 0], there
                ).wait_send()
    for p in range(PIECES):
        pl.when(zi != owner_z(p))(lambda: chain_copy(p, True).wait_send())
        if owner_z(p) < 3:
            pl.when((zi >= owner_z(p)) & (zi < 3))(lambda: z_ag(p, True).wait_send())
        if owner_z(p) > 0:
            pl.when((zi <= owner_z(p)) & (zi > 0))(lambda: z_ag(p, False).wait_send())

    for k in range(1, cols):
        stat_copy(k).wait_send()
    if rows > 1:
        core_copy.wait_send()
        for w in range(2):
            row_copies[w].wait_send()
        for k in range(1, rows):
            both_copy(k).wait_send()
    for k in range(1, teams):
        last_copy(k).wait_send()


def exchange(w_qkv, w_up, w_out, w_down, qk_gain, features, cotangent, ln_gain):
    dps, rows, cols = lax.axis_size("dp"), lax.axis_size("row"), lax.axis_size("col")
    images, own_patches, width = features.shape
    patches = own_patches * rows
    tokens = images * own_patches
    teams = dps * rows
    dma = pltpu.SemaphoreType.DMA
    whole = max(PIECES * 4 * patches, UNITS * width)
    half = max(PIECES * 2 * patches, UNITS * width // 2)
    units = UNITS * width
    struct = jax.ShapeDtypeStruct
    others, mates, peers = max(teams - 1, 1), max(rows - 1, 1), cols - 1
    return pl.pallas_call(
        functools.partial(core_kernel, dps, rows, cols),
        out_shape=(
            struct(features.shape, BF16),
            struct(features.shape, BF16),
            struct((width,), F32),
            struct((2, HEAD), F32),
            struct((6, width, HEAD), F32),
            struct((width, 6 * HEAD), F32),
            struct((3 * HEAD // 2, width), F32),
            struct((6 * HEAD, width), F32),
        ),
        in_specs=[pl.BlockSpec(memory_space=pl.ANY)] * 4 + vmem(4),
        out_specs=tuple(vmem(8)),
        scratch_shapes=[
            pltpu.VMEM((images, patches, width), BF16),
            pltpu.VMEM((images, patches, width), BF16),
            pltpu.VMEM(w_qkv.shape, BF16),
            pltpu.VMEM(w_up.shape, BF16),
            pltpu.VMEM(w_out.shape, BF16),
            pltpu.VMEM(w_down.shape, BF16),
            pltpu.VMEM((tokens, HEAD), F32),
            pltpu.VMEM((tokens, HEAD), F32),
            pltpu.VMEM((SIDE, PIECES, 4, patches, HEAD), BF16),
            pltpu.VMEM((whole, HEAD), BF16),
            pltpu.VMEM((whole, HEAD), BF16),
            pltpu.VMEM((whole, HEAD), BF16),
            pltpu.VMEM((half, HEAD), F32),
            pltpu.VMEM((half, HEAD), F32),
            pltpu.VMEM((whole, HEAD), F32),
            pltpu.VMEM((PIECES * 2 * patches, HEAD), BF16),
            pltpu.VMEM((PIECES * 2 * patches, HEAD), BF16),
            pltpu.VMEM((PIECES * 4 * patches, HEAD), BF16),
            pltpu.VMEM((PIECES * 4 * patches, HEAD), BF16),
            pltpu.VMEM((PIECES * 4 * patches, HEAD), BF16),
            pltpu.VMEM(((PIECES + 3) * 4 * patches, HEAD), BF16),
            pltpu.VMEM((units // 2, HEAD), BF16),
            pltpu.VMEM((units // 2, HEAD), BF16),
            pltpu.VMEM((units, HEAD), BF16),
            pltpu.VMEM((units, HEAD), BF16),
            pltpu.VMEM((width, images * patches), BF16),
            pltpu.VMEM((width, images * patches), BF16),
            pltpu.VMEM((images * patches, width), F32),
            pltpu.VMEM((images * patches, width), F32),
            pltpu.VMEM((2, 2, images, own_patches, width), BF16),
            pltpu.VMEM((2, 2, images, own_patches, width), BF16),
            pltpu.VMEM((2, images, own_patches, width), BF16),
            pltpu.VMEM((2, images, own_patches, width), BF16),
            pltpu.VMEM((8, tokens), F32),
            pltpu.VMEM((peers, 8, tokens), F32),
            pltpu.VMEM((8, HEAD), F32),
            pltpu.VMEM((peers, 8, HEAD), F32),
            pltpu.VMEM((8, tokens), F32),
            pltpu.VMEM((peers, 8, tokens), F32),
            pltpu.VMEM((8, HEAD), F32),
            pltpu.VMEM((others, 8, HEAD), F32),
            pltpu.VMEM((8, tokens), F32),
            pltpu.VMEM((mates, 8, tokens), F32),
            dma((2, PIECES)),
            dma((2, PIECES)),
            dma((2, 2, PIECES)),
            dma((2, 2, PIECES)),
            dma((PIECES,)),
            dma((PIECES + 3,)),
            dma((2, PIECES)),
            dma((2, PIECES)),
            dma((2, PIECES)),
            dma((2, PIECES)),
            dma((2, PIECES)),
            dma((PIECES,)),
            dma((4,)),
            dma((peers,)),
            dma((peers,)),
            dma((2, 3)),
            dma((2, 3)),
            dma((1,)),
            dma((1,)),
            dma((2,)),
            dma((2, UNITS)),
            dma((2, 2)),
            dma((2, 2, UNITS)),
            dma((2,)),
            dma((2,)),
            dma((peers,)),
            dma((peers,)),
            dma((peers,)),
            dma((peers,)),
            dma((others,)),
            dma((others,)),
            dma((mates,)),
            dma((mates,)),
        ],
        compiler_params=pltpu.CompilerParams(
            collective_id=0, has_side_effects=True, vmem_limit_bytes=VMEM_BYTES
        ),
        name="exchange",
    )(w_qkv, w_up, w_out, w_down, qk_gain, features, cotangent, ln_gain)


def on_device(features, ln_gain, w_qkv, qk_gain, w_up, w_out, w_down, cotangent):
    images, patches, width = features.shape
    output, input_grad, ln_grad, gains, qkv_units, up_grad, out_grad, down_grad = exchange(
        jnp.transpose(w_qkv, (1, 0, 2)), w_up, w_out, w_down, qk_gain, features, cotangent, ln_gain.reshape(1, width)
    )
    units = qkv_units.reshape(3, 2, width, HEAD)
    whole, split = units[:, 0], units[:, 1]
    mid = HEAD // 2
    qkv_grad = jnp.where(
        lax.rem(lax.axis_index("dp"), 2) == 0,
        jnp.concatenate([whole, split[..., :mid]], -1),
        jnp.concatenate([split[..., mid:], whole], -1),
    )
    qkv_grad = jnp.transpose(qkv_grad, (1, 0, 2))
    return (
        output, input_grad, ln_grad, gains, qkv_grad, up_grad, out_grad, down_grad
    )


def solution(mesh):
    in_specs = (
        P("dp", "row", "col"),
        P("col"),
        P("col", None, "row"),
        P(),
        P("col", "row"),
        P("row", "col"),
        P("row", "col"),
        P("dp", "row", "col"),
    )
    out_specs = (
        P("dp", "row", "col"),
        P("dp", "row", "col"),
        P("col"),
        P(),
        P("col", None, ("row", "dp")),
        P("col", ("row", "dp")),
        P(("row", "dp"), "col"),
        P(("row", "dp"), "col"),
    )
    return jax.shard_map(
        on_device, mesh=mesh, in_specs=in_specs, out_specs=out_specs, check_vma=False
    )
```

```python
import functools

import jax
import jax.numpy as jnp
from jax import lax
from jax.experimental import pallas as pl
from jax.experimental.pallas import tpu as pltpu
from jax.sharding import PartitionSpec as P

EPS = 1e-06
SQRT_HALF = 0.7071067811865476
INV_ROOT = 0.3989422804014327
HEAD = 128
SIDE = 4
PIECES = 9
MESH = pl.DeviceIdType.MESH
VMEM_BYTES = 62 * 1024 * 1024
F32 = jnp.float32
BF16 = jnp.bfloat16


def gelu_both(values):
    cdf = 0.5 * (1.0 + lax.erf(values * SQRT_HALF))
    slope = cdf + values * jnp.exp(-0.5 * values * values) * INV_ROOT
    return values * cdf, slope


def normalize(values):
    average = jnp.mean(values, -1, keepdims=True)
    spread = jnp.mean(values * values, -1, keepdims=True) - average * average
    factor = lax.rsqrt(spread + EPS)
    return ((values - average) * factor, factor)


def norm_back(grad_normed, normed, factor, gain):
    scaled = grad_normed * gain
    centre = jnp.mean(scaled, -1, keepdims=True)
    along = jnp.mean(scaled * normed, -1, keepdims=True)
    return factor * (scaled - centre - normed * along)


def dot(a, b):
    return lax.dot_general(a, b, (((1,), (0,)), ((), ())), preferred_element_type=F32)


def dot_nt(a, b):
    return lax.dot_general(a, b, (((1,), (1,)), ((), ())), preferred_element_type=F32)


def exact_nt(a, b):
    return lax.dot_general(
        a,
        b,
        (((1,), (1,)), ((), ())),
        precision=lax.Precision.HIGHEST,
        preferred_element_type=F32,
    )


def lane_sums(values):
    ones = jnp.ones((8, values.shape[1]), BF16)
    high = values.astype(BF16)
    low = (values - high.astype(F32)).astype(BF16)
    return dot_nt(ones, high) + dot_nt(ones, low)


def greet(peers, meanwhile):
    barrier = pltpu.get_barrier_semaphore()
    for peer in peers:
        pl.semaphore_signal(barrier, inc=1, device_id=peer, device_id_type=MESH)
    result = meanwhile()
    pl.semaphore_wait(barrier, len(peers))
    return result


def remote(src, dst, send, recv, peer):
    return pltpu.make_async_remote_copy(
        src_ref=src,
        dst_ref=dst,
        send_sem=send,
        recv_sem=recv,
        device_id=peer,
        device_id_type=MESH,
    )


def vmem(count):
    return [pl.BlockSpec(memory_space=pltpu.VMEM)] * count


def owner_z(piece):
    return piece if piece < 3 else piece - 3 if piece < 6 else 3


def owner_slot(piece):
    return 0 if piece < 3 else 1 if piece < 6 else piece - 6


UNITS = 20
BEHIND = 2
STEPS = PIECES + 2
SUM_ORDER = (6, 0, 7, 3, 1, 2, 8, 4, 5)
GATHER_ORDER = (
    (0, 3, 1, 4, 2, 5, 6, 7, 8),
    (1, 4, 0, 2, 3, 5, 6, 7, 8),
    (2, 5, 1, 6, 0, 7, 4, 8, 3),
    (6, 7, 8, 2, 5, 1, 0, 4, 3),
)


def core_kernel(
    dps, rows, cols,
    wq_hbm, wup_hbm, wout_hbm, wdown_hbm, gain_ref, feat_ref, cot_ref, ln_ref,
    output_ref, input_grad_ref, ln_grad_ref, gains_ref, qkv_ref, up_ref, out_ref, down_ref,
    x_ref, c_ref, wq_ref, wup_ref, wout_ref, wdown_ref, avg_ref, factor_ref,
    g_ref, opp, right_send, left_send, right_acc, left_acc, own,
    half_left, half_right, full_left, full_right, z_send, z_recv,
    dhalf_left, dhalf_right, dfull_left, dfull_right,
    x_turned, c_turned, out_acc, norm_acc, core_out, core_in, row_out, row_in,
    norm_mine, norm_in,
    gain_mine, gain_in, stat_mine, stat_in, last_mine, last_in, both_mine, both_in,
    s_opp, r_half, s_side, r_full, s_z, r_z, s_own, r_own, s_fwd, r_fwd, s_zag, r_zag,
    s_load, s_norm, r_norm, s_rowg, r_rowg, s_core, r_core,
    s_dopp, r_dhalf, s_dside, r_dfull, s_row, r_row, s_gain, r_gain, s_stat, r_stat, s_last, r_last, s_both, r_both,
):
    dp, row, col = lax.axis_index("dp"), lax.axis_index("row"), lax.axis_index("col")
    xi, zi = col // SIDE, lax.rem(col, SIDE)
    xr, xl, xo = lax.rem(xi + 1, SIDE), lax.rem(xi + 3, SIDE), lax.rem(xi + 2, SIDE)
    right, left = (dp, row, xr * SIDE + zi), (dp, row, xl * SIDE + zi)
    images, patches, width = x_ref.shape
    own_patches = patches // rows
    tokens = images * own_patches
    teams = dps * rows
    full_rows, half_rows = 4 * patches, 2 * patches

    def col_peer(k):
        return (dp, row, lax.rem(col + k, cols))

    mate = (dp, row + 1 - 2 * lax.rem(row, 2), col)
    cross = (dp, lax.rem(row + 2, rows), col)

    def team_peer(k):
        other = lax.rem(dp * rows + row + k, teams)
        return (other // rows, lax.rem(other, rows), col)

    loads = [
        pltpu.make_async_copy(src, dst, s_load.at[i])
        for i, (src, dst) in enumerate(
            ((wdown_hbm, wdown_ref), (wout_hbm, wout_ref), (wup_hbm, wup_ref), (wq_hbm, wq_ref))
        )
    ]
    for load in loads:
        load.start()
    def patch_rows(r):
        return pl.ds(pl.multiple_of(r * own_patches, own_patches), own_patches)

    def row_gather(which, ref, step):
        here = ref.at[:, patch_rows(row if step < 2 else lax.rem(row + 2, rows)), :]
        return remote(
            here, here, s_rowg.at[which, step], r_rowg.at[which, step], cross if step == 1 else mate
        )

    def row_send(which, ref):
        if rows > 1:
            row_gather(which, ref, 1).start()
            row_gather(which, ref, 0).start()

    def row_arrive(which, ref):
        if rows > 1:
            row_gather(which, ref, 1).wait_recv()
            row_gather(which, ref, 2).start()
            row_gather(which, ref, 0).wait_recv()
            row_gather(which, ref, 2).wait_recv()

    inputs_wide = feat_ref[...].astype(F32).reshape(tokens, width)
    which = lax.broadcasted_iota(jnp.int32, (8, tokens), 0)

    def own_sums():
        c_ref[:, patch_rows(row), :] = cot_ref[...]
        sums = jnp.where(
            which == 0, lane_sums(inputs_wide), lane_sums(inputs_wide * inputs_wide)
        )
        norm_mine[...] = sums
        return sums

    norm_sums = greet(
        [col_peer(k) for k in range(1, cols)] + [team_peer(k) for k in range(1, teams)], own_sums
    )
    row_send(0, c_ref)

    def norm_copy(k):
        return remote(
            norm_mine, norm_in.at[k - 1], s_norm.at[k - 1], r_norm.at[k - 1], col_peer(k)
        )

    for k in range(1, cols):
        norm_copy(k).start()
    eye = (
        lax.broadcasted_iota(jnp.int32, (tokens, tokens), 0)
        == lax.broadcasted_iota(jnp.int32, (tokens, tokens), 1)
    ).astype(F32)

    def run_start(block, pair):
        dest = lax.rem(block + pair, 4)
        return (dest * 6 + pair * 2) * HEAD, dest

    def cot_block(block, emit, send=None):
        image, run = block // 2, lax.rem(block, 2)
        triple = pl.ds(pl.multiple_of(run * 3 * HEAD, 3 * HEAD), 3 * HEAD)
        for pair in range(3):
            start, _ = run_start(block, pair)
            hidden = pl.ds(pl.multiple_of(start, 2 * HEAD), 2 * HEAD)
            for im in range(2):
                values = dot_nt(c_ref[im], wdown_ref[hidden, :])
                for j in range(2):
                    emit(3 + 2 * pair + j, 2 + im, values[:, j * HEAD : (j + 1) * HEAD])
            if send is not None:
                for j in range(2):
                    send(3 + 2 * pair + j)
        values = dot_nt(c_ref[image], wout_ref[triple, :])
        for z in range(3):
            emit(z, 3, values[:, z * HEAD : (z + 1) * HEAD])

    def x_block(block, emit):
        image, run = block // 2, lax.rem(block, 2)
        triple = pl.ds(pl.multiple_of(run * 3 * HEAD, 3 * HEAD), 3 * HEAD)
        for part in range(3):
            values = dot(x_ref[image], wq_ref[part, :, triple])
            for z in range(3):
                emit(z, part, values[:, z * HEAD : (z + 1) * HEAD])
        for pair in range(3):
            start, _ = run_start(block, pair)
            hidden = pl.ds(pl.multiple_of(start, 2 * HEAD), 2 * HEAD)
            for im in range(2):
                values = dot(x_ref[im], wup_ref[:, hidden])
                for j in range(2):
                    emit(3 + 2 * pair + j, im, values[:, j * HEAD : (j + 1) * HEAD])

    def at(ref, p, part, parts=1):
        return ref.at[span(p, part, parts)]

    def span(p, part, parts=1):
        return pl.ds(pl.multiple_of(p * full_rows + part * patches, patches), parts * patches)

    def half_span(p):
        return pl.ds(pl.multiple_of(p * half_rows, half_rows), half_rows)

    def opp_right(p):
        return remote(
            at(opp, p, 0, 2), half_left.at[half_span(p)], s_opp.at[0, p], r_half.at[0, p], right
        )

    def opp_left(p):
        return remote(
            at(opp, p, 2, 2), half_right.at[half_span(p)], s_opp.at[1, p], r_half.at[1, p], left
        )

    def side_right(p, half):
        return remote(
            at(right_send, p, 2 * half, 2),
            at(full_left, p, 2 * half, 2),
            s_side.at[0, half, p],
            r_full.at[0, half, p],
            right,
        )

    def side_left(p, half):
        return remote(
            at(left_send, p, 2 * half, 2),
            at(full_right, p, 2 * half, 2),
            s_side.at[1, half, p],
            r_full.at[1, half, p],
            left,
        )

    def emit_opp(p, part, values):
        opp[span(p, part)] = values.astype(BF16)

    def emit_right(p, part, values):
        if part >= 2:
            right_send[span(p, part)] = values.astype(BF16)
        else:
            right_acc[pl.ds(p * half_rows + part * patches, patches)] = values

    def emit_left(p, part, values):
        if part < 2:
            left_send[span(p, part)] = values.astype(BF16)
        else:
            left_acc[pl.ds(p * half_rows + (part - 2) * patches, patches)] = values

    def emit_own(p, part, values):
        own[span(p, part)] = values

    row_arrive(0, c_ref)
    loads[0].wait()
    loads[1].wait()
    cot_block(xo, emit_opp, lambda p: opp_left(p).start())
    cot_block(xr, emit_right, lambda p: side_right(p, 1).start())
    normed_sums = norm_sums
    for k in range(1, cols):
        norm_copy(k).wait_recv()
        normed_sums = normed_sums + norm_in[k - 1]
    normed_sums = normed_sums * (1.0 / (width * cols))
    average = normed_sums[0:1]
    factor = lax.rsqrt(normed_sums[1:2] - average * average + EPS)
    turned = exact_nt(eye, jnp.where(which == 0, average, factor))
    avg_ref[...] = jnp.broadcast_to(turned[:, 0:1], avg_ref.shape)
    factor_ref[...] = jnp.broadcast_to(turned[:, 1:2], factor_ref.shape)
    normed = (inputs_wide - turned[:, 0:1]) * turned[:, 1:2]
    x_ref[:, patch_rows(row), :] = (
        (normed * ln_ref[...]).astype(BF16).reshape(images, own_patches, width)
    )
    row_send(1, x_ref)

    cot_block(xl, emit_left)
    cot_block(xi, emit_own)
    loads[2].wait()
    loads[3].wait()
    row_arrive(1, x_ref)
    x_block(xo, emit_opp)
    for p in range(3):
        opp_left(p).start()
    for i in range(2):
        opp_right(SUM_ORDER[i]).start()
    x_block(xl, emit_left)
    for i in range(2):
        side_left(SUM_ORDER[i], 0).start()
    x_block(xr, emit_right)
    x_block(xi, emit_own)

    for im in range(images):
        here = slice(im * patches, (im + 1) * patches)
        x_turned[:, here] = x_ref[im].T
        c_turned[:, here] = c_ref[im].T

    def pass_on(i):
        p = SUM_ORDER[i]
        if i + 2 < PIECES:
            opp_right(SUM_ORDER[i + 2]).start()
            side_left(SUM_ORDER[i + 2], 0).start()
        if p < 3:
            side_right(p, 1).start()
        opp_left(p).wait_recv()
        left_send[span(p, 2, 2)] = (
            left_acc[half_span(p)] + half_right[half_span(p)].astype(F32)
        ).astype(BF16)
        side_left(p, 1).start()
        opp_right(p).wait_recv()
        right_send[span(p, 0, 2)] = (
            right_acc[half_span(p)] + half_left[half_span(p)].astype(F32)
        ).astype(BF16)
        side_right(p, 0).start()

    z_up, z_down = (dp, row, xi * SIDE + lax.rem(zi + 1, SIDE)), (
        dp, row, xi * SIDE + lax.rem(zi + 3, SIDE)
    )

    def chain_copy(p, up):
        slot = p if up else jnp.where(zi - 1 == owner_z(p), PIECES + owner_slot(p), p)
        return remote(
            at(z_send, p, 0, 4),
            at(z_recv, slot, 0, 4),
            s_z.at[p],
            r_z.at[slot],
            z_up if up else z_down,
        )

    def chain_pass(p, up):
        here = span(p, 0, 4)
        chain_copy(p, True).wait_recv()
        z_send[here] = (own[here] + z_recv[here].astype(F32)).astype(BF16)
        chain_copy(p, up).start()

    def chain_end(p, up):
        here = span(p, 0, 4)
        z_send[here] = own[here].astype(BF16)
        chain_copy(p, up).start()

    def arrived(p, slot):
        for come, place in ((zi > 0, p), (zi < 3, PIECES + slot)):

            @pl.when(come)
            def _():
                there, here = span(place, 0, 4), span(p, 0, 4)
                remote(
                    at(z_send, 0, 0, 4), z_recv.at[there], s_z.at[0], r_z.at[place], z_up
                ).wait_recv()
                own[here] = own[here] + z_recv[there].astype(F32)

    def summed(p, part):
        return own[span(p, part)]

    def own_ag(p, way):
        peer = right if way == 0 else left
        return remote(g_ref.at[xi, p], g_ref.at[xi, p], s_own.at[way, p], r_own.at[way, p], peer)

    def z_ag(p, up):
        way = 0 if up else 1
        peer = z_up if up else z_down
        return remote(g_ref.at[xi, p], g_ref.at[xi, p], s_zag.at[way, p], r_zag.at[p], peer)

    def launch(p):
        for way in range(2):
            own_ag(p, way).start()
        pl.when(zi < 3)(lambda: z_ag(p, True).start())
        pl.when(zi > 0)(lambda: z_ag(p, False).start())

    def hidden_units(p, slot):
        arrived(p, slot)
        for im in range(2):
            value, slope = gelu_both(summed(p, im))
            g_ref[xi, p, im] = value.astype(BF16)
            g_ref[xi, p, 2 + im] = (summed(p, 2 + im) * slope).astype(BF16)
        launch(p)

    scale = HEAD ** (-0.5)

    def attention(p):
        arrived(p, 0)
        query_hat, query_factor = normalize(summed(p, 0))
        key_hat, key_factor = normalize(summed(p, 1))
        query_gain, key_gain = gain_ref[0:1, :], gain_ref[1:2, :]
        query = (query_hat * query_gain).astype(BF16)
        key = (key_hat * key_gain).astype(BF16)
        value = summed(p, 2).astype(BF16)
        grad = summed(p, 3).astype(BF16)
        expo = jnp.exp(dot_nt(query, key) * scale)
        weights = expo / jnp.sum(expo, -1, keepdims=True)
        weights_half = weights.astype(BF16)
        g_ref[xi, p, 0] = dot(weights_half, value).astype(BF16)
        weight_grad = dot_nt(grad, value)
        score_grad = weights * (weight_grad - jnp.sum(weights * weight_grad, -1, keepdims=True))
        score_grad = score_grad.astype(BF16)
        query_grad = dot(score_grad, key) * scale
        key_grad = dot(score_grad.T, query) * scale
        value_grad = dot(weights_half.T, grad)
        gain_mine[0:1, :] = jnp.sum(query_grad * query_hat, 0, keepdims=True)
        gain_mine[1:2, :] = jnp.sum(key_grad * key_hat, 0, keepdims=True)
        g_ref[xi, p, 1] = norm_back(query_grad, query_hat, query_factor, query_gain).astype(BF16)
        g_ref[xi, p, 2] = norm_back(key_grad, key_hat, key_factor, key_gain).astype(BF16)
        g_ref[xi, p, 3] = value_grad.astype(BF16)
        launch(p)

    gain_mine[...] = jnp.zeros_like(gain_mine)

    for turn in range(PIECES + BEHIND + 2):
        if turn < PIECES:
            pass_on(turn)
        i = turn - BEHIND
        if 0 <= i < PIECES:
            p = SUM_ORDER[i]
            for half in range(2):
                side_right(p, half).wait_recv()
                side_left(p, half).wait_recv()
            here = span(p, 0, 4)
            own[here] = own[here] + full_left[here].astype(F32) + full_right[here].astype(F32)
            if owner_z(p) > 0:
                pl.when(zi == 0)(functools.partial(chain_end, p, True))
            if owner_z(p) < 3:
                pl.when(zi == 3)(functools.partial(chain_end, p, False))
        for lag in range(1, 3):
            if 0 <= i - lag < PIECES:
                p = SUM_ORDER[i - lag]
                if owner_z(p) > lag:
                    pl.when(zi == lag)(functools.partial(chain_pass, p, True))
                if owner_z(p) < 3 - lag:
                    pl.when(zi == 3 - lag)(functools.partial(chain_pass, p, False))
        if turn == PIECES:
            pl.when(zi < 3)(lambda: attention(zi))
        if turn in (PIECES, PIECES + 1):
            pl.when(zi == 3)(functools.partial(hidden_units, turn - 3, turn - PIECES))

    pl.when(zi < 3)(lambda: hidden_units(zi + 3, 1))
    pl.when(zi == 3)(lambda: hidden_units(8, 2))

    def gain_copy(k):
        return remote(
            gain_mine, gain_in.at[k - 1], s_gain.at[k - 1], r_gain.at[k - 1], col_peer(k)
        )

    for k in range(1, cols):
        gain_copy(k).start()

    def settle(p, carry):
        opp_right(p).wait_send()
        opp_left(p).wait_send()
        for half in range(2):
            side_right(p, half).wait_send()
            side_left(p, half).wait_send()
        return carry

    lax.fori_loop(0, PIECES, settle, 0)
    for k in range(1, cols):
        norm_copy(k).wait_send()
    if rows > 1:
        for w, ref in enumerate((c_ref, x_ref)):
            for turn in range(3):
                row_gather(w, ref, turn).wait_send()
    out_acc[...] = jnp.zeros_like(out_acc)
    norm_acc[...] = jnp.zeros_like(norm_acc)

    low, high = pl.ds(0, 2), pl.ds(2, 2)

    def fwd_copy(p, way):
        block = xl if way == 0 else xr
        part = low if way == 0 else high
        there = right if way == 0 else left
        return remote(
            g_ref.at[block, p, part],
            g_ref.at[block, p, part],
            s_fwd.at[way, p],
            r_fwd.at[way, p],
            there,
        )

    own_count = jnp.where(zi == 3, 3, 2)

    def piece_at(i):
        piece = i * 0
        for place in range(PIECES):
            named = GATHER_ORDER[0][place]
            for z in range(1, SIDE):
                named = jnp.where(zi == z, GATHER_ORDER[z][place], named)
            piece = jnp.where(i == place, named, piece)
        return piece

    def owner_of(p):
        return jnp.where(p < 3, p, jnp.where(p < 6, p - 3, 3))

    dp_right = (lax.rem(dp + 1, dps), row, col)
    dp_left = (lax.rem(dp + dps - 1, dps), row, col)
    half_width = width // 2

    def unit_span(u, half=None):
        if half is None:
            return pl.ds(pl.multiple_of(u * width, width), width)
        return pl.ds(pl.multiple_of(u * width + half * half_width, half_width), half_width)

    def small_span(u):
        return pl.ds(pl.multiple_of(u * half_width, half_width), half_width)

    all_halves = pl.ds(0, UNITS * half_width)

    def dopp_right(u):
        return remote(
            opp.at[unit_span(u, 0)], dhalf_left.at[small_span(u)],
            s_dopp.at[0], r_dhalf.at[0, u], dp_right,
        )

    def dopp_left(u):
        return remote(
            opp.at[unit_span(u, 1)], dhalf_right.at[small_span(u)],
            s_dopp.at[1], r_dhalf.at[1, u], dp_left,
        )

    def dside_right(u, half):
        return remote(
            right_send.at[unit_span(u, half)], dfull_left.at[unit_span(u, half)],
            s_dside.at[0, half], r_dfull.at[0, half, u], dp_right,
        )

    def dside_left(u, half):
        return remote(
            left_send.at[unit_span(u, half)], dfull_right.at[unit_span(u, half)],
            s_dside.at[1, half], r_dfull.at[1, half, u], dp_left,
        )

    def emit_unit(dest, u, values):
        away = lax.rem(dest - dp + 4, 4)

        @pl.when(away == 0)
        def _():
            own[unit_span(u)] = values

        if dps == 1:
            return

        @pl.when(away == 2)
        def _():
            opp[unit_span(u)] = values.astype(BF16)
            dopp_right(u).start()
            dopp_left(u).start()

        @pl.when(away == 1)
        def _():
            right_acc[small_span(u)] = values[:half_width]
            right_send[unit_span(u, 1)] = values[half_width:].astype(BF16)
            dside_right(u, 1).start()

        @pl.when(away == 3)
        def _():
            left_acc[small_span(u)] = values[half_width:]
            left_send[unit_span(u, 0)] = values[:half_width].astype(BF16)
            dside_left(u, 0).start()

    def pass_unit(dest, u):
        if dps == 1:
            return
        away = lax.rem(dest - dp + 4, 4)

        @pl.when(away == 1)
        def _():
            dopp_right(u).wait_recv()
            right_send[unit_span(u, 0)] = (
                right_acc[small_span(u)] + dhalf_left[small_span(u)].astype(F32)
            ).astype(BF16)
            dside_right(u, 0).start()

        @pl.when(away == 3)
        def _():
            dopp_left(u).wait_recv()
            left_send[unit_span(u, 1)] = (
                left_acc[small_span(u)] + dhalf_right[small_span(u)].astype(F32)
            ).astype(BF16)
            dside_left(u, 1).start()

    def hidden_place(block, p):
        pair, second = (p - 3) // 2, lax.rem(p - 3, 2)
        start, dest = run_start(block, pair)
        return pl.multiple_of(start + second * HEAD, HEAD), dest, pair * 2 + second

    def hidden_back(block, p):
        start, dest, u = hidden_place(block, p)
        run = pl.ds(start, HEAD)
        hidden = g_ref[block, p, low].reshape(half_rows, HEAD)
        pre = g_ref[block, p, high].reshape(half_rows, HEAD)
        emit_unit(dest, u, dot(x_turned[...], pre))
        emit_unit(dest, 6 + u, dot(c_turned[...], hidden))
        out_acc[...] += dot(hidden, wdown_ref[run, :])
        norm_acc[...] += dot_nt(pre, wup_ref[:, run])

    def attention_dests(run, z):
        return 2 * run + jnp.where(z == 2, 1, 0), 2 * run + 1, jnp.where(z == 1, 1, 0)

    def attention_back(block, z):
        image, run = block // 2, lax.rem(block, 2)
        head = run * 3 + z
        here = pl.ds(pl.multiple_of(image * patches, patches), patches)
        out_acc[here] += dot(
            g_ref[block, z, 0], wout_ref[pl.ds(pl.multiple_of(head * HEAD, HEAD), HEAD), :]
        )
        columns = pl.ds(pl.multiple_of(head * HEAD, HEAD), HEAD)
        total = norm_acc[here]
        for part in range(3):
            total = total + dot_nt(g_ref[block, z, 1 + part], wq_ref[part, :, columns])
        norm_acc[here] = total

    def attention_weights(run, z):
        dest, second, which = attention_dests(run, z)
        for t in range(4):
            turned = c_turned if t == 3 else x_turned
            part = 0 if t == 3 else t + 1
            values = dot(turned[:, 0:patches], g_ref[run, z, part]) + dot(
                turned[:, patches : 2 * patches], g_ref[run + 2, z, part]
            )
            u = 12 + 2 * t + which
            emit_unit(dest, u, values)

            @pl.when(z == 1)
            def _():
                emit_unit(second, u, values)

    def pass_hidden(block, p):
        _, dest, u = hidden_place(block, p)
        pass_unit(dest, u)
        pass_unit(dest, 6 + u)

    def pass_attention(run, z):
        dest, second, which = attention_dests(run, z)
        for t in range(4):
            u = 12 + 2 * t + which
            pass_unit(dest, u)

            @pl.when(z == 1)
            def _():
                pass_unit(second, u)

    def passes(i):
        def each_pass(k, carry):
            block = lax.rem(xi + k, 4)
            turn = i - 2 - jnp.where(k == 2, 2, 0)
            p = piece_at(turn)
            live = (turn >= 0) & (turn < PIECES)

            @pl.when(live & (p >= 3))
            def _():
                pass_hidden(block, p)

            @pl.when(live & (p < 3) & (k >= 2))
            def _():
                pass_attention(lax.rem(block, 2), p)

            return carry

        lax.fori_loop(0, SIDE, each_pass, 0)

    def gathered(p):
        for way in range(2):
            own_ag(p, way).wait_send()
            fwd_copy(p, way).wait_send()

    def step(i, carry):
        ahead = i + 2

        @pl.when((ahead >= own_count) & (ahead < PIECES))
        def _():
            p = piece_at(ahead)
            z_ag(p, True).wait_recv()
            for way in range(2):
                own_ag(p, way).start()
            owner = owner_of(p)
            pl.when((owner < zi) & (zi < 3))(lambda: z_ag(p, True).start())
            pl.when((owner > zi) & (zi > 0))(lambda: z_ag(p, False).start())

        @pl.when(i < PIECES)
        def _():
            p = piece_at(i)
            for way in range(2):
                own_ag(p, way).wait_recv()
                fwd_copy(p, way).start()

        @pl.when((i >= 2) & (i < PIECES + 2))
        def _():
            p = piece_at(i - 2)
            for way in range(2):
                fwd_copy(p, way).wait_recv()

        def each_block(k, carry):
            block = lax.rem(xi + k, 4)
            turn = i - jnp.where(k == 2, 2, 0)
            p = piece_at(turn)
            live = (turn >= 0) & (turn < PIECES)

            @pl.when(live & (p >= 3))
            def _():
                hidden_back(block, p)

            @pl.when(live & (p < 3))
            def _():
                attention_back(block, p)

            @pl.when(live & (p < 3) & (k >= 2))
            def _():
                attention_weights(lax.rem(block, 2), p)

            return carry

        lax.fori_loop(0, SIDE, each_block, 0)
        passes(i)

        @pl.when((i >= 3) & (i < PIECES + 2))
        def _():
            gathered(piece_at(i - 3))

        @pl.when(i == PIECES - 3)
        def _():
            gains = gain_mine[...]
            for k in range(1, cols):
                gain_copy(k).wait()
                gains = gains + gain_in[k - 1]
            last_mine[...] = gains

        return carry

    lax.fori_loop(0, STEPS, step, 0)

    accs = (out_acc, norm_acc)
    parity = lax.rem(row, 2)

    def row_part(acc, r, im):
        start = im * patches + r * own_patches
        return acc[pl.ds(pl.multiple_of(start, own_patches), own_patches)]

    core_copy = remote(core_out, core_in, s_core.at[0], r_core.at[0], mate)
    row_copies = [
        remote(row_out.at[w], row_in.at[w], s_row.at[w], r_row.at[w], cross) for w in range(2)
    ]
    other_high = lax.rem(row // 2 + 1, 2)
    if rows > 1:
        for w, acc in enumerate(accs):
            for im in range(images):
                for j, high_z in enumerate((other_high, row // 2)):
                    core_out[j, w, im] = row_part(acc, high_z * 2 + 1 - parity, im).astype(BF16)
        core_copy.start()

    gain = ln_ref[...]
    stats = jnp.zeros((8, tokens), F32)
    ln_sum = jnp.zeros((1, width), F32)
    for r in range(rows):
        grads = jnp.concatenate([row_part(norm_acc, r, im) for im in range(images)], 0)
        inputs = x_ref[:, pl.ds(r * own_patches, own_patches), :].astype(F32).reshape(tokens, width)
        along = grads * inputs
        stats = jnp.where(which == 2 * r, lane_sums(grads * gain), stats)
        stats = jnp.where(which == 2 * r + 1, lane_sums(along), stats)
        ln_sum = ln_sum + jnp.sum(along, 0, keepdims=True)
    ln_sum = ln_sum / gain
    stat_mine[...] = stats

    def stat_copy(k):
        return remote(
            stat_mine, stat_in.at[k - 1], s_stat.at[k - 1], r_stat.at[k - 1], col_peer(k)
        )

    for k in range(1, cols):
        stat_copy(k).start()
    runs = width // HEAD
    for j in range(runs):
        last_mine[2 + j : 3 + j, :] = ln_sum[:, j * HEAD : (j + 1) * HEAD]

    def last_copy(k):
        return remote(
            last_mine, last_in.at[k - 1], s_last.at[k - 1], r_last.at[k - 1], team_peer(k)
        )

    if rows > 1:
        core_copy.wait_recv()
        for w in (1, 0):
            for im in range(images):
                row_out[w, im] = (
                    row_part(accs[w], lax.rem(row + 2, rows), im) + core_in[0, w, im].astype(F32)
                ).astype(BF16)
            row_copies[w].start()
    for k in range(1, teams):
        last_copy(k).start()

    def last_passes(i, carry):
        passes(i)
        return carry

    for k in range(1, cols):
        stat_copy(k).wait_recv()
        stats = stats + stat_in[k - 1]
    both_mine[...] = stats

    def both_copy(k):
        there = (dp, lax.rem(row + k, rows), col)
        return remote(both_mine, both_in.at[k - 1], s_both.at[k - 1], r_both.at[k - 1], there)

    for k in range(1, rows):
        both_copy(k).start()

    lax.fori_loop(STEPS, STEPS + 2, last_passes, 0)

    def row_total(w, acc):
        parts = []
        for im in range(images):
            total = row_part(acc, row, im)
            if rows > 1:
                total = total + core_in[1, w, im].astype(F32) + row_in[w, im].astype(F32)
            parts.append(total)
        return jnp.concatenate(parts, 0)

    def unit_total(u):
        here = unit_span(u)
        total = own[here]
        if dps > 1:
            for half in range(2):
                dside_right(u, half).wait_recv()
                dside_left(u, half).wait_recv()
            total = total + dfull_left[here].astype(F32) + dfull_right[here].astype(F32)
        return total

    for u in range(6):
        columns = slice(u * HEAD, (u + 1) * HEAD)
        up_ref[:, columns] = unit_total(u)
        down_ref[columns, :] = unit_total(6 + u).T
        qkv_ref[u] = unit_total(12 + u)
    whole, split = unit_total(18).T, unit_total(19).T
    mid = HEAD // 2

    @pl.when(lax.rem(dp, 2) == 0)
    def _():
        out_ref[0:HEAD, :] = whole
        out_ref[HEAD : HEAD + mid, :] = split[0:mid]

    @pl.when(lax.rem(dp, 2) == 1)
    def _():
        out_ref[0:mid, :] = split[mid:]
        out_ref[mid : HEAD + mid, :] = whole

    average, factor = avg_ref[:, 0:1], factor_ref[:, 0:1]
    normed = (inputs_wide - average) * factor
    for k in range(1, rows):
        both_copy(k).wait_recv()
        stats = stats + both_in[k - 1]
    stats = stats * (1.0 / (width * cols))
    centre_row = jnp.sum(jnp.where(which == 2 * row, stats, 0.0), 0, keepdims=True)
    along_row = jnp.sum(jnp.where(which == 2 * row + 1, stats, 0.0), 0, keepdims=True)
    turned = exact_nt(eye, jnp.where(which == 0, centre_row, along_row))
    centre, along = turned[:, 0:1], turned[:, 1:2]
    if rows > 1:
        row_copies[1].wait_recv()
    input_grad = cot_ref[...].astype(F32).reshape(tokens, width) + factor * (
        row_total(1, norm_acc) * gain - centre - normed * along
    )
    input_grad_ref[...] = input_grad.astype(BF16).reshape(images, own_patches, width)
    if rows > 1:
        row_copies[0].wait_recv()
    output_ref[...] = (
        (inputs_wide + row_total(0, out_acc)).astype(BF16).reshape(images, own_patches, width)
    )

    last = last_mine[...]
    for k in range(1, teams):
        last_copy(k).wait_recv()
        last = last + last_in[k - 1]
    gains_ref[...] = last[0:2]
    for j in range(runs):
        ln_grad_ref[j * HEAD : (j + 1) * HEAD] = last[2 + j]

    gathered(piece_at(PIECES - 1))
    if dps > 1:
        for way, (send, there) in enumerate(((right_send, dp_right), (left_send, dp_left))):
            remote(
                opp.at[all_halves], dhalf_left, s_dopp.at[way], r_dhalf.at[way, 0], there
            ).wait_send()
            for half in range(2):
                remote(
                    send.at[all_halves], dhalf_left, s_dside.at[way, half], r_dhalf.at[way, 0], there
                ).wait_send()
    for p in range(PIECES):
        pl.when(zi != owner_z(p))(lambda: chain_copy(p, True).wait_send())
        if owner_z(p) < 3:
            pl.when((zi >= owner_z(p)) & (zi < 3))(lambda: z_ag(p, True).wait_send())
        if owner_z(p) > 0:
            pl.when((zi <= owner_z(p)) & (zi > 0))(lambda: z_ag(p, False).wait_send())

    for k in range(1, cols):
        stat_copy(k).wait_send()
    if rows > 1:
        core_copy.wait_send()
        for w in range(2):
            row_copies[w].wait_send()
        for k in range(1, rows):
            both_copy(k).wait_send()
    for k in range(1, teams):
        last_copy(k).wait_send()


def exchange(w_qkv, w_up, w_out, w_down, qk_gain, features, cotangent, ln_gain):
    dps, rows, cols = lax.axis_size("dp"), lax.axis_size("row"), lax.axis_size("col")
    images, own_patches, width = features.shape
    patches = own_patches * rows
    tokens = images * own_patches
    teams = dps * rows
    dma = pltpu.SemaphoreType.DMA
    whole = max(PIECES * 4 * patches, UNITS * width)
    half = max(PIECES * 2 * patches, UNITS * width // 2)
    units = UNITS * width
    struct = jax.ShapeDtypeStruct
    others, mates, peers = max(teams - 1, 1), max(rows - 1, 1), cols - 1
    return pl.pallas_call(
        functools.partial(core_kernel, dps, rows, cols),
        out_shape=(
            struct(features.shape, BF16),
            struct(features.shape, BF16),
            struct((width,), F32),
            struct((2, HEAD), F32),
            struct((6, width, HEAD), F32),
            struct((width, 6 * HEAD), F32),
            struct((3 * HEAD // 2, width), F32),
            struct((6 * HEAD, width), F32),
        ),
        in_specs=[pl.BlockSpec(memory_space=pl.ANY)] * 4 + vmem(4),
        out_specs=tuple(vmem(8)),
        scratch_shapes=[
            pltpu.VMEM((images, patches, width), BF16),
            pltpu.VMEM((images, patches, width), BF16),
            pltpu.VMEM(w_qkv.shape, BF16),
            pltpu.VMEM(w_up.shape, BF16),
            pltpu.VMEM(w_out.shape, BF16),
            pltpu.VMEM(w_down.shape, BF16),
            pltpu.VMEM((tokens, HEAD), F32),
            pltpu.VMEM((tokens, HEAD), F32),
            pltpu.VMEM((SIDE, PIECES, 4, patches, HEAD), BF16),
            pltpu.VMEM((whole, HEAD), BF16),
            pltpu.VMEM((whole, HEAD), BF16),
            pltpu.VMEM((whole, HEAD), BF16),
            pltpu.VMEM((half, HEAD), F32),
            pltpu.VMEM((half, HEAD), F32),
            pltpu.VMEM((whole, HEAD), F32),
            pltpu.VMEM((PIECES * 2 * patches, HEAD), BF16),
            pltpu.VMEM((PIECES * 2 * patches, HEAD), BF16),
            pltpu.VMEM((PIECES * 4 * patches, HEAD), BF16),
            pltpu.VMEM((PIECES * 4 * patches, HEAD), BF16),
            pltpu.VMEM((PIECES * 4 * patches, HEAD), BF16),
            pltpu.VMEM(((PIECES + 3) * 4 * patches, HEAD), BF16),
            pltpu.VMEM((units // 2, HEAD), BF16),
            pltpu.VMEM((units // 2, HEAD), BF16),
            pltpu.VMEM((units, HEAD), BF16),
            pltpu.VMEM((units, HEAD), BF16),
            pltpu.VMEM((width, images * patches), BF16),
            pltpu.VMEM((width, images * patches), BF16),
            pltpu.VMEM((images * patches, width), F32),
            pltpu.VMEM((images * patches, width), F32),
            pltpu.VMEM((2, 2, images, own_patches, width), BF16),
            pltpu.VMEM((2, 2, images, own_patches, width), BF16),
            pltpu.VMEM((2, images, own_patches, width), BF16),
            pltpu.VMEM((2, images, own_patches, width), BF16),
            pltpu.VMEM((8, tokens), F32),
            pltpu.VMEM((peers, 8, tokens), F32),
            pltpu.VMEM((8, HEAD), F32),
            pltpu.VMEM((peers, 8, HEAD), F32),
            pltpu.VMEM((8, tokens), F32),
            pltpu.VMEM((peers, 8, tokens), F32),
            pltpu.VMEM((8, HEAD), F32),
            pltpu.VMEM((others, 8, HEAD), F32),
            pltpu.VMEM((8, tokens), F32),
            pltpu.VMEM((mates, 8, tokens), F32),
            dma((2, PIECES)),
            dma((2, PIECES)),
            dma((2, 2, PIECES)),
            dma((2, 2, PIECES)),
            dma((PIECES,)),
            dma((PIECES + 3,)),
            dma((2, PIECES)),
            dma((2, PIECES)),
            dma((2, PIECES)),
            dma((2, PIECES)),
            dma((2, PIECES)),
            dma((PIECES,)),
            dma((4,)),
            dma((peers,)),
            dma((peers,)),
            dma((2, 3)),
            dma((2, 3)),
            dma((1,)),
            dma((1,)),
            dma((2,)),
            dma((2, UNITS)),
            dma((2, 2)),
            dma((2, 2, UNITS)),
            dma((2,)),
            dma((2,)),
            dma((peers,)),
            dma((peers,)),
            dma((peers,)),
            dma((peers,)),
            dma((others,)),
            dma((others,)),
            dma((mates,)),
            dma((mates,)),
        ],
        compiler_params=pltpu.CompilerParams(
            collective_id=0, has_side_effects=True, vmem_limit_bytes=VMEM_BYTES
        ),
        name="exchange",
    )(w_qkv, w_up, w_out, w_down, qk_gain, features, cotangent, ln_gain)


def on_device(features, ln_gain, w_qkv, qk_gain, w_up, w_out, w_down, cotangent):
    images, patches, width = features.shape
    output, input_grad, ln_grad, gains, qkv_units, up_grad, out_grad, down_grad = exchange(
        jnp.transpose(w_qkv, (1, 0, 2)), w_up, w_out, w_down, qk_gain, features, cotangent, ln_gain.reshape(1, width)
    )
    units = qkv_units.reshape(3, 2, width, HEAD)
    whole, split = units[:, 0], units[:, 1]
    mid = HEAD // 2
    qkv_grad = jnp.where(
        lax.rem(lax.axis_index("dp"), 2) == 0,
        jnp.concatenate([whole, split[..., :mid]], -1),
        jnp.concatenate([split[..., mid:], whole], -1),
    )
    qkv_grad = jnp.transpose(qkv_grad, (1, 0, 2))
    return (
        output, input_grad, ln_grad, gains, qkv_grad, up_grad, out_grad, down_grad
    )


def solution(mesh):
    in_specs = (
        P("dp", "row", "col"),
        P("col"),
        P("col", None, "row"),
        P(),
        P("col", "row"),
        P("row", "col"),
        P("row", "col"),
        P("dp", "row", "col"),
    )
    out_specs = (
        P("dp", "row", "col"),
        P("dp", "row", "col"),
        P("col"),
        P(),
        P("col", None, ("row", "dp")),
        P("col", ("row", "dp")),
        P(("row", "dp"), "col"),
        P(("row", "dp"), "col"),
    )
    return jax.shard_map(
        on_device, mesh=mesh, in_specs=in_specs, out_specs=out_specs, check_vma=False
    )
```
